128 devices in a mesh: expert: 2 (over z_lo), group: 4 (over z_hi, core), seq: 16 (over x, y).
Axes of the slice: x: 4, y: 4, z: 4 (z_hi: 2, z_lo: 2; z = z_hi * 2 + z_lo), core: 2. Of those that a mesh axis runs over, the one named last changes fastest.
Arguments:
- latent: bfloat16 [2, 4, 2048, 64], P('expert', 'group', 'seq'), may hold values from -17 to 17
- text_cache: bfloat16 [2, 4, 512, 32, 256], P('expert', 'group', None, 'seq'), may hold values from -6 to 6
- patch_weight: bfloat16 [2, 64, 5120], P('expert'), may hold values from -0.75 to 0.75
- patch_bias: float32 [2, 5120], P('expert'), may hold values from -3 to 3
- qkv_weight: bfloat16 [2, 5120, 3, 4096], P('expert', None, None, 'seq'), may hold values from -0.10062306 to 0.10062306
- qk_gain: float32 [2, 2, 4096], P('expert', None, 'seq'), may hold values from 0.6 to 5
- modulation: float32 [2, 40, 2, 5120], P('expert'), may hold values from -2.5 to 2.5
- step_index: int32 [2, 4], replicated, may hold values from 0 to 39
- lengths: int32 [2, 4], replicated, may hold values from 512 to 2048, as said below
- crossing: int32 [2, 2], replicated, may hold values from 0 to 3, as said below
Outputs:
- attended: bfloat16 [2, 4, 2048, 4096], P('expert', 'group', 'seq')
- cache_after: bfloat16 [2, 4, 512, 32, 256], P('expert', 'group', None, 'seq')
The draws below stay inside these ranges and needn't reach their ends.
Inputs may be any that keep to these rules, and one draw needn't show every extreme that they name: `crossing`: sources are distinct and destinations are distinct. `lengths`: some slot has exactly 2048.
All inputs are finite; a program needn't handle non-finite values.
Results may differ from the reference program's by a relative error of at most 0.0056.
Values may be sent and summed in bfloat16 or wider, within the bound.
A program may use at most 128 MiB of HBM per device.

```python
import jax
import jax.numpy as jnp
from jax import lax

D = 5120
PATCH = 64
HEADS = 32
HD = 128
TEXT = 512
STEPS = 40
CROSS = 2
EXPERTS = 2
GROUPS = 4
SEQ_LEN = 2048
HW = 4096


def draw_latent(key, part):
    key = jax.random.fold_in(key, 13)
    first_key = jax.random.fold_in(key, 0)
    normal_part = jnp.clip(jax.random.normal(first_key, (EXPERTS, GROUPS, SEQ_LEN, PATCH), jnp.float32), -4.0, 4.0)
    return normal_part.astype(jnp.bfloat16)


def draw_qkv_weight(key, part):
    key = jax.random.fold_in(key, 11)
    normal_part = jnp.clip(jax.random.normal(key, (EXPERTS, D, 3, HW), jnp.float32), -4.0, 4.0) * D ** (-0.5)
    column = jnp.arange(HW, dtype=jnp.float32) / HW
    column_scale = 0.6 * jnp.power(3.0, column)
    scales = jnp.stack([column_scale, column_scale, jnp.ones_like(column_scale)])
    return (normal_part * scales[None, None, :, :]).astype(jnp.bfloat16)


def draw_qk_gain(key, part):
    key = jax.random.fold_in(key, 12)
    gains = jax.random.uniform(key, (EXPERTS, 2, HW), jnp.float32, 0.6, 1.4)
    return gains


def draw_lengths(key, part):
    key = jax.random.fold_in(key, 14)
    first_key, second_key = jax.random.split(key)
    drawn = jax.random.randint(first_key, (EXPERTS * GROUPS,), SEQ_LEN // 4, SEQ_LEN + 1)
    longest = jax.random.randint(second_key, (), 0, EXPERTS * GROUPS)
    drawn = jnp.where(jnp.arange(EXPERTS * GROUPS) == longest, SEQ_LEN, drawn)
    return drawn.reshape(EXPERTS, GROUPS).astype(jnp.int32)


def draw_crossing(key, part):
    key = jax.random.fold_in(key, 15)
    first_key, second_key, third_key = jax.random.split(key, 3)
    sources = jnp.concatenate([jnp.array([GROUPS - 1], jnp.int32), jax.random.permutation(first_key, GROUPS - 1).astype(jnp.int32)[:CROSS - 1]])
    targets = jnp.concatenate([jnp.array([0], jnp.int32), 1 + jax.random.permutation(second_key, GROUPS - 1).astype(jnp.int32)[:CROSS - 1]])
    order = jax.random.permutation(third_key, CROSS)
    return jnp.stack([sources[order], targets], axis=1).astype(jnp.int32)


def place_ends(values, own_key, smallest, high):
    spot = [jax.random.randint(jax.random.fold_in(own_key, axis), (), 0, length) for axis, length in enumerate(values.shape)]
    main_axis = values.shape.index(max(values.shape))
    next_to = spot[:main_axis] + [(spot[main_axis] + 1) % values.shape[main_axis]] + spot[main_axis + 1:]
    return values.at[tuple(spot)].set(smallest).at[tuple(next_to)].set(high)


def steps_of(stream_key, dims, cuts, smallest, top_value):
    def one(axis_at, parts):
        heights = jax.random.uniform(jax.random.fold_in(jax.random.fold_in(stream_key, 6), axis_at), (parts,), jnp.float32, smallest / len(cuts), top_value / len(cuts))
        return jnp.repeat(jnp.exp(heights), dims[axis_at] // parts).reshape((-1,) + (1,) * (len(dims) - axis_at - 1))

    level = one(*cuts[0])
    for cut in cuts[1:]:
        level = level * one(*cut)
    return level


def gaussian(key, dims, scale, limit, cuts=(), kind=jnp.bfloat16):
    values = jax.random.normal(key, dims, jnp.float32) * scale
    if len(cuts) > 0:
        values = steps_of(key, dims, cuts, -0.22, 0.18) * values
    return jnp.clip(values, min=-limit, max=limit).astype(kind)


def setup_inputs(seed: int = 0) -> dict:
    key_of = jax.random.split(jax.random.key(seed), 11)
    return {
        "latent": draw_latent(jax.random.fold_in(key_of[10], 71), 0),
        "text_cache": gaussian(key_of[1], (EXPERTS, GROUPS, TEXT, HEADS, 2 * HD), 1.0, 6.0, ((0, 2), (1, 4), (3, 16))),
        "patch_weight": gaussian(key_of[2], (EXPERTS, PATCH, D), PATCH ** -0.5, 0.75, ((0, 2),)),
        "patch_bias": gaussian(key_of[3], (EXPERTS, D), 0.5, 3.0, ((0, 2),), jnp.float32),
        "qkv_weight": draw_qkv_weight(jax.random.fold_in(key_of[10], 71), 0),
        "qk_gain": draw_qk_gain(jax.random.fold_in(key_of[10], 71), 0),
        "modulation": gaussian(key_of[6], (EXPERTS, STEPS, 2, D), 0.3, 2.5, ((0, 2),), jnp.float32),
        "step_index": place_ends(jax.random.randint(key_of[7], (EXPERTS, GROUPS), 0, STEPS), jax.random.fold_in(key_of[7], 1), 0, STEPS - 1).astype(jnp.int32),
        "lengths": draw_lengths(jax.random.fold_in(key_of[10], 71), 0),
        "crossing": draw_crossing(jax.random.fold_in(key_of[10], 71), 0),
    }


norm_eps = 1e-06
masked_score = -1e+30

def slot_output(slot_rows, embed_weight, embed_bias, mod_table, step_now, length, weight, gain):
    modulate = lax.dynamic_index_in_dim(mod_table, step_now, 0, keepdims=False)
    values = jnp.dot(slot_rows, embed_weight, preferred_element_type=jnp.float32) + embed_bias[None, :]
    centre = lax.optimization_barrier(jnp.mean(values, axis=-1, keepdims=True))
    spread = lax.optimization_barrier(jnp.mean(jnp.square(values - centre), axis=-1, keepdims=True))
    normed = ((values - centre) * lax.rsqrt(spread + norm_eps) * (1.0 + modulate[1]) + modulate[0]).astype(jnp.bfloat16)
    projected = jnp.dot(normed, weight.reshape(D, 3 * HW), preferred_element_type=jnp.float32).reshape(SEQ_LEN, 3, HW)
    queries = projected[:, 0, :]
    key_rows = projected[:, 1, :]
    queries = (queries * lax.rsqrt(lax.optimization_barrier(jnp.mean(queries * queries, axis=-1, keepdims=True)) + norm_eps) * gain[0]).astype(jnp.bfloat16)
    key_rows = (key_rows * lax.rsqrt(lax.optimization_barrier(jnp.mean(key_rows * key_rows, axis=-1, keepdims=True)) + norm_eps) * gain[1]).astype(jnp.bfloat16)
    value_rows = projected[:, 2, :].astype(jnp.bfloat16)
    live_keys = jnp.arange(SEQ_LEN, dtype=jnp.int32) < length
    score_scale = 1.0 / HD ** 0.5

    def head_attend(operands):
        head_query, head_key, head_value = operands
        scores = jnp.dot(head_query, head_key.T, preferred_element_type=jnp.float32) * score_scale
        scores = jnp.where(live_keys[None, :], scores, masked_score)
        row_max = lax.optimization_barrier(jnp.max(scores, axis=-1, keepdims=True))
        weights = jnp.exp(scores - row_max)
        probabilities = (weights / lax.optimization_barrier(jnp.sum(weights, axis=-1, keepdims=True))).astype(jnp.bfloat16)
        return jnp.dot(probabilities, head_value, preferred_element_type=jnp.float32)

    def by_heads(matrix):
        return matrix.reshape(SEQ_LEN, HEADS, HD).transpose(1, 0, 2)
    heads_out = lax.map(head_attend, (by_heads(queries), by_heads(key_rows), by_heads(value_rows)))
    result = heads_out.transpose(1, 0, 2).reshape(SEQ_LEN, HW)
    return jnp.where(live_keys[:, None], result, 0.0).astype(jnp.bfloat16)

def reference(latent, text_cache, patch_weight, patch_bias, qkv_weight, qk_gain, modulation, step_index, lengths, crossing):
    source_expert = jnp.broadcast_to(jnp.arange(EXPERTS, dtype=jnp.int32)[:, None], (EXPERTS, GROUPS))
    source_group = jnp.broadcast_to(jnp.arange(GROUPS, dtype=jnp.int32)[None, :], (EXPERTS, GROUPS))
    vacated = jnp.zeros((EXPERTS, GROUPS), dtype=bool)
    for crossing_row in range(CROSS):
        source_expert = source_expert.at[1, crossing[crossing_row, 1]].set(0)
        source_group = source_group.at[1, crossing[crossing_row, 1]].set(crossing[crossing_row, 0])
        vacated = vacated.at[0, crossing[crossing_row, 0]].set(True)
    outputs = []
    caches = []
    for expert in range(EXPERTS):
        for group_id in range(GROUPS):
            from_expert = source_expert[expert, group_id]
            from_group = source_group[expert, group_id]
            empty = vacated[expert, group_id]
            slot_rows = latent[from_expert, from_group]
            length = jnp.where(empty, 0, lengths[from_expert, from_group]).astype(jnp.int32)
            step_now = step_index[from_expert, from_group].astype(jnp.int32)
            outputs.append(slot_output(slot_rows, patch_weight[expert], patch_bias[expert], modulation[expert], step_now, length, qkv_weight[expert], qk_gain[expert]))
            moved_cache = text_cache[from_expert, from_group]
            caches.append(jnp.where(empty, jnp.zeros_like(moved_cache), moved_cache))
    attended = jnp.stack(outputs).reshape(EXPERTS, GROUPS, SEQ_LEN, HW)
    cache_after = jnp.stack(caches).reshape(EXPERTS, GROUPS, TEXT, HEADS, 2 * HD)
    return (attended, cache_after)
```

```python
import functools

import jax
import jax.numpy as jnp
from jax import lax
from jax.experimental import pallas as pl
from jax.experimental.pallas import tpu as pltpu
from jax.sharding import PartitionSpec as P

HD = 128
EPS = 1e-06
MASKED = -1e30
LOG2E = 1.4426950408889634
BF = jnp.bfloat16
F32 = jnp.float32
MESH = pl.DeviceIdType.MESH
ROWS = 80
QB = 256
KB = 256


def dot(a, b):
    return jnp.dot(a, b, preferred_element_type=F32)


def dot_nt(a, b):
    return lax.dot_general(a, b, (((1,), (1,)), ((), ())), preferred_element_type=F32)


def split(a):
    hi = a.astype(BF)
    lo = (a - hi.astype(F32)).astype(BF)
    return hi, lo


def gram(a):
    hi, lo = split(a)
    return dot_nt(hi, hi) + dot_nt(hi, lo) + dot_nt(lo, hi)


def kernel(
    n,
    crossing,
    lengths,
    steps,
    xt_ref,
    b_ref,
    gain_ref,
    p_hbm,
    mod_hbm,
    w_hbm,
    cache_hbm,
    out_hbm,
    land_hbm,
    p_v,
    mod_v,
    w_v,
    a2,
    c2,
    zin,
    xall,
    m_v,
    gbuf,
    rs_in,
    ag,
    z2,
    mt2,
    mtf,
    qaug,
    kaug,
    vaug,
    s_scr,
    p_scr,
    ostage,
    load_sem,
    zsend,
    zrecv,
    csend,
    crecv,
    fsend,
    frecv,
    xsend,
    xrecv,
    rsend,
    rrecv,
    asend,
    arecv,
    osend,
    orecv,
):
    e = lax.axis_index("expert")
    g = lax.axis_index("group")
    s = lax.axis_index("seq")
    half = lax.div(g, 2)
    core = lax.rem(g, 2)
    tokens = n * 128
    red = ROWS // 8

    ld_p = pltpu.make_async_copy(p_hbm, p_v, load_sem.at[0])
    ld_mod = pltpu.make_async_copy(mod_hbm, mod_v, load_sem.at[1])
    ld_w = [pltpu.make_async_copy(w_hbm.at[j], w_v.at[j], load_sem.at[2 + j]) for j in range(3)]
    ld_p.start()
    ld_mod.start()
    for copy in ld_w:
        copy.start()

    barrier = pltpu.get_barrier_semaphore()

    def greet(k, carry):
        pl.semaphore_signal(barrier, inc=1, device_id={"seq": lax.rem(s + k, n)}, device_id_type=MESH)
        return carry

    lax.fori_loop(1, n, greet, 0)
    for other in range(4):
        pl.semaphore_signal(
            barrier, inc=1, device_id={"expert": 1 - e, "group": other}, device_id_type=MESH
        )

    @pl.when(e == 1)
    def _():
        pl.semaphore_signal(barrier, inc=1, device_id={"group": 2 * half + 1 - core}, device_id_type=MESH)

    hit0 = crossing[0, 1] == g
    hit1 = crossing[1, 1] == g
    arrived = jnp.logical_and(e == 1, jnp.logical_or(hit0, hit1))
    source = jnp.where(hit0, crossing[0, 0], jnp.where(hit1, crossing[1, 0], 0))
    step_now = jnp.where(arrived, steps[0, source], steps[e, g])
    length = jnp.where(arrived, lengths[0, source], lengths[e, g])

    ld_p.wait()
    ld_mod.wait()
    width = p_v.shape[1]
    p_mean = jnp.mean(p_v[...].astype(F32), axis=1, keepdims=True)
    b_mean = jnp.mean(b_ref[...], axis=1, keepdims=True)
    part = 1024
    tail_row = lax.broadcasted_iota(jnp.int32, (16, part), 0)
    for i in range(width // part):
        cols = pl.ds(i * part, part)
        modulate = mod_v[step_now, :, cols]
        scale = 1.0 + modulate[1:2, :]
        shift = modulate[0:1, :]
        centred = p_v[:, cols].astype(F32) - p_mean
        bias = b_ref[:, cols] - b_mean
        bias_rows = jnp.broadcast_to(bias, (16, part))
        top = centred * scale
        bottom = jnp.where(
            tail_row == 0, bias_rows * scale, jnp.where(tail_row == 1, jnp.broadcast_to(shift, (16, part)), 0.0)
        )
        plain = jnp.where(tail_row == 0, bias_rows, 0.0)
        hi, lo = split(top)
        a2[0:64, cols] = hi
        a2[ROWS : ROWS + 64, cols] = lo
        hi, lo = split(bottom)
        a2[64:ROWS, cols] = hi
        a2[ROWS + 64 : 2 * ROWS, cols] = lo
        hi, lo = split(centred)
        c2[0:64, cols] = hi
        c2[ROWS : ROWS + 64, cols] = lo
        hi, lo = split(plain)
        c2[64:ROWS, cols] = hi
        c2[ROWS + 64 : 2 * ROWS, cols] = lo

    pl.semaphore_wait(barrier, n - 1 + 4 + e)

    def z_copy(src_group, dst_group):
        return pltpu.make_async_remote_copy(
            src_ref=xt_ref,
            dst_ref=zin.at[src_group],
            send_sem=zsend.at[dst_group],
            recv_sem=zrecv.at[src_group],
            device_id={"expert": 1, "group": dst_group},
            device_id_type=MESH,
        )

    def cache_copy(src_half, dst_half):
        return pltpu.make_async_remote_copy(
            src_ref=cache_hbm,
            dst_ref=land_hbm.at[2 * src_half + core],
            send_sem=csend.at[dst_half],
            recv_sem=crecv.at[src_half],
            device_id={"expert": 1, "group": 2 * dst_half + core},
            device_id_type=MESH,
        )

    def forward_copy(src_half, src_core):
        return pltpu.make_async_remote_copy(
            src_ref=land_hbm.at[2 * src_half + src_core],
            dst_ref=land_hbm.at[2 * src_half + src_core],
            send_sem=fsend.at[src_half],
            recv_sem=frecv.at[src_half],
            device_id={"expert": 1, "group": 2 * half + 1 - core},
            device_id_type=MESH,
        )

    @pl.when(e == 0)
    def _():
        for dst in range(4):
            z_copy(g, dst).start()
        for dst in range(2):
            cache_copy(half, dst).start()

    def project(j):
        raw = dot(a2[...], w_v[j])
        total = raw[0:ROWS, :] + raw[ROWS : 2 * ROWS, :]
        m_v[j, 0:ROWS, :] = total
        return total

    ld_w[0].wait()
    m_q = project(0)

    def x_copy(peer, slot):
        return pltpu.make_async_remote_copy(
            src_ref=xall.at[slot],
            dst_ref=xall.at[slot],
            send_sem=xsend.at[peer],
            recv_sem=xrecv.at[slot],
            device_id={"seq": peer},
            device_id_type=MESH,
        )

    @pl.when(e == 1)
    def _():
        for src in range(4):
            z_copy(src, 0).wait_recv()
        xall[s] = jnp.where(arrived, zin[source], xt_ref[...])

    @pl.when(e == 0)
    def _():
        xall[s] = xt_ref[...]

    def x_start(k, carry):
        x_copy(lax.rem(s + k, n), s).start()
        return carry

    lax.fori_loop(1, n, x_start, 0)

    ld_w[1].wait()
    m_k = project(1)
    gbuf[...] = jnp.zeros_like(gbuf)
    gbuf[:, 0:ROWS] = gram(m_q)
    gbuf[:, 128 : 128 + ROWS] = gram(m_k)

    def r_copy(peer, slot):
        return pltpu.make_async_remote_copy(
            src_ref=gbuf.at[pl.ds(pl.multiple_of(peer * 8, 8), 8)],
            dst_ref=rs_in.at[slot],
            send_sem=rsend.at[peer],
            recv_sem=rrecv.at[slot],
            device_id={"seq": peer},
            device_id_type=MESH,
        )

    def r_start(k, carry):
        peer = lax.rem(s + k, n)

        @pl.when(peer < red)
        def _():
            r_copy(peer, s).start()

        return carry

    lax.fori_loop(1, n, r_start, 0)

    var_gram = (
        dot_nt(c2[0:ROWS, :], c2[0:ROWS, :])
        + dot_nt(c2[0:ROWS, :], c2[ROWS : 2 * ROWS, :])
        + dot_nt(c2[ROWS : 2 * ROWS, :], c2[0:ROWS, :])
    ) * (1.0 / width)

    ld_w[2].wait()
    project(2)

    for j in range(3):
        m_v[j, ROWS:128, :] = jnp.zeros((128 - ROWS, 256), F32)
        full = m_v[j]
        if j < 2:
            full = full * gain_ref[j : j + 1, :]
        flipped = full.T
        hi, lo = split(flipped)
        mt2[j, :, 0:128] = hi
        mt2[j, :, 128:256] = lo
        mtf[j] = flipped

    def a_copy(peer, slot):
        return pltpu.make_async_remote_copy(
            src_ref=ag.at[slot],
            dst_ref=ag.at[slot],
            send_sem=asend.at[peer],
            recv_sem=arecv.at[slot],
            device_id={"seq": peer},
            device_id_type=MESH,
        )

    @pl.when(s < red)
    def _():
        def r_wait(k, carry):
            r_copy(0, lax.rem(s + k, n)).wait_recv()
            return carry

        lax.fori_loop(1, n, r_wait, 0)
        rs_in[s] = gbuf[pl.ds(pl.multiple_of(s * 8, 8), 8), :]
        total = rs_in[0]
        for src in range(1, n):
            total = total + rs_in[src]
        ag[s] = total

        def a_start(k, carry):
            a_copy(lax.rem(s + k, n), s).start()
            return carry

        lax.fori_loop(1, n, a_start, 0)

    def x_wait(k, carry):
        x_copy(0, lax.rem(s + k, n)).wait_recv()
        return carry

    lax.fori_loop(1, n, x_wait, 0)
    tail64 = lax.broadcasted_iota(jnp.int32, (64, 128), 0)
    ones_row = jnp.where(tail64 == 0, 1.0, 0.0).astype(BF)
    for i in range(n):
        cols = pl.ds(i * 128, 128)
        z2[0:64, cols] = xall[i]
        z2[128:192, cols] = xall[i]
        z2[64:128, cols] = ones_row
        z2[192:256, cols] = ones_row

    z0 = z2[0:128, :]
    z0f = z0.astype(F32)[0:ROWS, :]
    z80 = z0[0:ROWS, :]
    g_hi, g_lo = split(var_gram)
    t = dot(g_hi, z80) + dot(g_lo, z80)
    var = jnp.maximum(jnp.sum(t * z0f, axis=0, keepdims=True), 0.0)
    rstd = lax.rsqrt(var + EPS)

    def a_wait(k, carry):
        slot = lax.rem(s + k, n)

        @pl.when(slot < red)
        def _():
            a_copy(0, slot).wait_recv()

        return carry

    lax.fori_loop(1, n, a_wait, 0)
    both = ag[...].reshape(ROWS, 256)
    scales = []
    for j in range(2):
        g_j = both[:, j * 128 : (j + 1) * 128]
        hi, lo = split(g_j)
        t = dot(hi, z0) + dot(lo, z0)
        quad = jnp.sum(t * z0f, axis=0, keepdims=True)
        total = rstd * rstd * quad + 2.0 * rstd * t[65:66, :] + g_j[65:66, 65:66]
        scales.append(lax.rsqrt(jnp.maximum(total, 0.0) * (1.0 / (n * 256)) + EPS))
    r_q = scales[0] * (LOG2E / HD**0.5)
    r_k = scales[1]

    first16 = lax.broadcasted_iota(jnp.int32, (16, tokens), 0)
    first128 = lax.broadcasted_iota(jnp.int32, (128, tokens), 0)
    one16 = jnp.where(first16 == 0, 1.0, 0.0).astype(BF)
    one128 = jnp.where(first128 == 0, 1.0, 0.0).astype(BF)
    key_at = lax.broadcasted_iota(jnp.int32, (tokens, 128), 0)
    masks = jnp.where(key_at >= length, MASKED, 0.0).astype(BF)
    for h in range(2):
        qaug[h, 128:256, :] = one128
        vaug[h, 128:144, :] = one16
        kaug[h, :, 128:256] = masks
    piece = 512
    for i in range(tokens // piece):
        cols = slice(i * piece, (i + 1) * piece)
        rhs = z2[:, cols]
        r_i = rstd[:, cols]
        q_w = r_q[:, cols]
        k_w = r_k[:, cols]
        q_t = (dot(mt2[0], rhs) * (q_w * r_i) + mtf[0, :, 65:66] * q_w).astype(BF)
        k_t = dot(mt2[1], rhs) * (k_w * r_i) + mtf[1, :, 65:66] * k_w
        v_t = (dot(mt2[2], rhs) * r_i + mtf[2, :, 65:66]).astype(BF)
        for h in range(2):
            rows = slice(h * 128, (h + 1) * 128)
            qaug[h, 0:128, cols] = q_t[rows, :]
            vaug[h, 0:128, cols] = v_t[rows, :]
            kaug[h, cols, 0:128] = k_t[rows, :].T.astype(BF)

    blocks = tokens // QB
    mine = lax.div(s, 2)

    def o_copy(block, side, src):
        return pltpu.make_async_remote_copy(
            src_ref=ostage.at[block, pl.ds(side * 128, 128)],
            dst_ref=out_hbm.at[:, pl.ds(pl.multiple_of(src * 256, 256), 256)],
            send_sem=osend.at[2 * block + side],
            recv_sem=orecv.at[src],
            device_id={"seq": 2 * block + side},
            device_id_type=MESH,
        )

    def own_copy():
        return pltpu.make_async_copy(
            ostage.at[mine, pl.ds(pl.multiple_of((s - 2 * mine) * 128, 128), 128)],
            out_hbm.at[:, pl.ds(pl.multiple_of(s * 256, 256), 256)],
            load_sem.at[0],
        )

    def attend(t, carry):
        block = lax.rem(mine + 1 + t, blocks)
        at = pl.ds(pl.multiple_of(block * QB, QB), QB)
        for h in range(2):
            query = qaug[h, :, at]
            top = jnp.full((8, QB), -3e38, F32)
            for c in range(tokens // KB):
                rows = slice(c * KB, (c + 1) * KB)
                score = dot(kaug[h, rows, :], query)
                s_scr[h, rows, :] = score
                top = jnp.maximum(top, jnp.max(score.reshape(KB // 8, 8, QB), axis=0))
            top = jnp.max(top, axis=0, keepdims=True)
            for c in range(tokens // KB):
                rows = slice(c * KB, (c + 1) * KB)
                p_scr[h, rows, :] = jnp.exp2(s_scr[h, rows, :] - top).astype(BF)
            result = dot(vaug[h], p_scr[h])
            result = result[0:128, :] * (1.0 / result[128:129, :])
            ostage[block, :, h * 128 : (h + 1) * 128] = result.T.astype(BF)
        for side in range(2):

            @pl.when(2 * block + side != s)
            def _():
                o_copy(block, side, s).start()

            @pl.when(2 * block + side == s)
            def _():
                own_copy().start()

        return carry

    lax.fori_loop(0, blocks, attend, 0)

    @pl.when(e == 1)
    def _():
        for src in range(2):
            cache_copy(src, 0).wait_recv()
            forward_copy(src, core).start()
        for src in range(2):
            forward_copy(src, core).wait_send()
            forward_copy(src, 1 - core).wait_recv()

    @pl.when(e == 0)
    def _():
        for dst in range(4):
            z_copy(g, dst).wait_send()
        for dst in range(2):
            cache_copy(half, dst).wait_send()

    def x_done(k, carry):
        peer = lax.rem(s + k, n)
        x_copy(peer, s).wait_send()

        @pl.when(peer < red)
        def _():
            r_copy(peer, s).wait_send()

        @pl.when(s < red)
        def _():
            a_copy(peer, s).wait_send()

        o_copy(lax.div(peer, 2), lax.rem(peer, 2), s).wait_send()
        o_copy(0, 0, peer).wait_recv()
        return carry

    lax.fori_loop(1, n, x_done, 0)
    own_copy().wait()


def shards(
    n,
    latent,
    text_cache,
    patch_weight,
    patch_bias,
    qkv_weight,
    qk_gain,
    modulation,
    step_index,
    lengths,
    crossing,
):
    tokens = n * 128
    width = qkv_weight.shape[1]
    xt = latent[0, 0].T
    w3 = jnp.transpose(qkv_weight[0], (1, 0, 2))
    cache = text_cache[0, 0]
    smem = pl.BlockSpec(memory_space=pltpu.SMEM)
    vmem = pl.BlockSpec(memory_space=pltpu.VMEM)
    hbm = pl.BlockSpec(memory_space=pl.ANY)
    dma = pltpu.SemaphoreType.DMA
    red = ROWS // 8
    raw, land = pl.pallas_call(
        functools.partial(kernel, n),
        out_shape=(
            jax.ShapeDtypeStruct((128, n * 256), BF),
            jax.ShapeDtypeStruct((4,) + cache.shape, BF),
        ),
        in_specs=[smem] * 3 + [vmem] * 3 + [hbm] * 4,
        out_specs=(hbm, hbm),
        scratch_shapes=[
            pltpu.VMEM((64, width), BF),
            pltpu.VMEM(modulation.shape[1:], F32),
            pltpu.VMEM((3, width, 256), BF),
            pltpu.VMEM((2 * ROWS, width), BF),
            pltpu.VMEM((2 * ROWS, width), BF),
            pltpu.VMEM((4, 64, 128), BF),
            pltpu.VMEM((n, 64, 128), BF),
            pltpu.VMEM((3, 128, 256), F32),
            pltpu.VMEM((ROWS, 256), F32),
            pltpu.VMEM((n, 8, 256), F32),
            pltpu.VMEM((red, 8, 256), F32),
            pltpu.VMEM((256, tokens), BF),
            pltpu.VMEM((3, 256, 256), BF),
            pltpu.VMEM((3, 256, 128), F32),
            pltpu.VMEM((2, 256, tokens), BF),
            pltpu.VMEM((2, tokens, 256), BF),
            pltpu.VMEM((2, 144, tokens), BF),
            pltpu.VMEM((2, tokens, QB), F32),
            pltpu.VMEM((2, tokens, QB), BF),
            pltpu.VMEM((tokens // QB, QB, 256), BF),
            dma((5,)),
            dma((4,)),
            dma((4,)),
            dma((2,)),
            dma((2,)),
            dma((2,)),
            dma((2,)),
            dma((n,)),
            dma((n,)),
            dma((n,)),
            dma((n,)),
            dma((n,)),
            dma((n,)),
            dma((n,)),
            dma((n,)),
        ],
        compiler_params=pltpu.CompilerParams(
            collective_id=0, has_side_effects=True, vmem_limit_bytes=56 * 1024 * 1024
        ),
    )(
        crossing,
        lengths,
        step_index,
        xt,
        patch_bias,
        qk_gain[0],
        patch_weight[0],
        modulation[0],
        w3,
        cache,
    )

    expert_id = lax.axis_index("expert")
    group_id = lax.axis_index("group")
    seq_id = lax.axis_index("seq")
    dest_hit = crossing[:, 1] == group_id
    source_hit = crossing[:, 0] == group_id
    arrived = jnp.logical_and(expert_id == 1, jnp.any(dest_hit))
    vacated = jnp.logical_and(expert_id == 0, jnp.any(source_hit))
    source = jnp.sum(jnp.where(dest_hit, crossing[:, 0], 0))
    length = jnp.where(
        vacated, 0, jnp.where(arrived, lengths[0, source], lengths[expert_id, group_id])
    )
    row = seq_id * 128 + lax.broadcasted_iota(jnp.int32, raw.shape, 0)
    attended = jnp.where(row < length, raw, jnp.zeros_like(raw))
    moved = lax.dynamic_index_in_dim(land, source, 0, keepdims=False)
    cache_after = jnp.where(arrived, moved, jnp.where(vacated, jnp.zeros_like(cache), cache))
    return (attended[None, None], cache_after[None, None])


def solution(mesh):
    in_specs = (
        P("expert", "group", "seq", None),
        P("expert", "group", None, "seq", None),
        P("expert", None, None),
        P("expert", None),
        P("expert", None, None, "seq"),
        P("expert", None, "seq"),
        P("expert", None, None, None),
        P(),
        P(),
        P(),
    )
    out_specs = (P("expert", "group", "seq", None), P("expert", "group", None, "seq", None))
    return jax.shard_map(
        functools.partial(shards, mesh.shape["seq"]),
        mesh=mesh,
        in_specs=in_specs,
        out_specs=out_specs,
        check_vma=False,
    )
```

```python
import functools

import jax
import jax.numpy as jnp
from jax import lax
from jax.experimental import pallas as pl
from jax.experimental.pallas import tpu as pltpu
from jax.sharding import PartitionSpec as P

HD = 128
EPS = 1e-06
MASKED = -1e30
LOG2E = 1.4426950408889634
BF = jnp.bfloat16
F32 = jnp.float32
MESH = pl.DeviceIdType.MESH
ROWS = 80
RED = ROWS // 8
SIDE = 4
QB = 512
KB = 256
OWNERS = QB // 128
STEPS = (
    ((1, 0), (3, 0), (1, 2), (3, 2)),
    ((0, 1), (0, 3), (2, 1), (2, 3)),
    ((1, 1), (3, 3), (2, 0), (0, 2)),
    ((1, 3), (3, 1), (2, 2), (0, 0)),
)


def dot(a, b):
    return jnp.dot(a, b, preferred_element_type=F32)


def dot_nt(a, b):
    return lax.dot_general(a, b, (((1,), (1,)), ((), ())), preferred_element_type=F32)


def split(a):
    hi = a.astype(BF)
    lo = (a - hi.astype(F32)).astype(BF)
    return hi, lo


def gram(a):
    hi, lo = split(a)
    return dot_nt(hi, hi) + dot_nt(hi, lo) + dot_nt(lo, hi)


def pick(block, choices):
    value = choices[-1]
    for at in range(len(choices) - 2, -1, -1):
        value = jnp.where(block == at, choices[at], value)
    return value


def kernel(
    n,
    crossing,
    lengths,
    steps,
    xt_hbm,
    b_hbm,
    gain_hbm,
    p_hbm,
    mod_hbm,
    w_hbm,
    cache_hbm,
    out_hbm,
    land_hbm,
    x_v,
    b_v,
    gain_v,
    p_v,
    mod_v,
    w_v,
    a2,
    c2,
    zin,
    xall,
    m_v,
    gbuf,
    rs_in,
    ag,
    z2,
    mt2,
    mtf,
    qaug,
    kaug,
    vaug,
    s_a,
    s_b,
    ostage,
    load_sem,
    zsend,
    zrecv,
    csend,
    crecv,
    fsend,
    frecv,
    xsend,
    xrecv,
    rsend,
    rrecv,
    asend,
    arecv,
    osend,
    orecv,
):
    e = lax.axis_index("expert")
    g = lax.axis_index("group")
    s = lax.axis_index("seq")
    half = lax.div(g, 2)
    core = lax.rem(g, 2)
    my_x = lax.div(s, SIDE)
    my_y = lax.rem(s, SIDE)
    tokens = n * 128
    width = p_v.shape[1]

    def owner(step):
        return lax.rem(my_x + step[0], SIDE) * SIDE + lax.rem(my_y + step[1], SIDE)

    order = [owner(step) for block in STEPS for step in block]

    ld_p = pltpu.make_async_copy(p_hbm, p_v, load_sem.at[0])
    ld_b = pltpu.make_async_copy(b_hbm, b_v, load_sem.at[1])
    ld_x = pltpu.make_async_copy(xt_hbm, x_v, load_sem.at[2])
    ld_mod = pltpu.make_async_copy(mod_hbm, mod_v, load_sem.at[3])
    ld_gain = pltpu.make_async_copy(gain_hbm, gain_v, load_sem.at[4])
    ld_w = [pltpu.make_async_copy(w_hbm.at[j], w_v.at[j], load_sem.at[5 + j]) for j in range(3)]
    for copy in [ld_p, ld_b, ld_x, ld_mod, ld_gain] + ld_w:
        copy.start()

    barrier = pltpu.get_barrier_semaphore()

    def greet(k, carry):
        pl.semaphore_signal(barrier, inc=1, device_id={"seq": lax.rem(s + k, n)}, device_id_type=MESH)
        return carry

    for other in range(4):
        pl.semaphore_signal(
            barrier, inc=1, device_id={"expert": 1 - e, "group": other}, device_id_type=MESH
        )
    lax.fori_loop(1, n, greet, 0)

    @pl.when(e == 1)
    def _():
        pl.semaphore_signal(barrier, inc=1, device_id={"group": 2 * half + 1 - core}, device_id_type=MESH)

    hit0 = crossing[0, 1] == g
    hit1 = crossing[1, 1] == g
    arrived = jnp.logical_and(e == 1, jnp.logical_or(hit0, hit1))
    left = jnp.logical_and(e == 0, jnp.logical_or(crossing[0, 0] == g, crossing[1, 0] == g))
    source = jnp.where(hit0, crossing[0, 0], jnp.where(hit1, crossing[1, 0], 0))
    step_now = jnp.where(arrived, steps[0, source], steps[e, g])
    length = jnp.where(left, 0, jnp.where(arrived, lengths[0, source], lengths[e, g]))

    ld_p.wait()
    p_mean = jnp.mean(p_v[...].astype(F32), axis=1, keepdims=True)
    part = 1024
    for i in range(width // part):
        cols = pl.ds(i * part, part)
        hi, lo = split(p_v[:, cols].astype(F32) - p_mean)
        c2[0:64, cols] = hi
        c2[64:128, cols] = lo

    pl.semaphore_wait(barrier, n - 1 + 4 + e)

    def z_copy(src_group, dst_group):
        return pltpu.make_async_remote_copy(
            src_ref=xt_hbm,
            dst_ref=zin.at[src_group],
            send_sem=zsend.at[dst_group],
            recv_sem=zrecv.at[src_group],
            device_id={"expert": 1, "group": dst_group},
            device_id_type=MESH,
        )

    def cache_copy(src_half, dst_half):
        return pltpu.make_async_remote_copy(
            src_ref=cache_hbm,
            dst_ref=land_hbm.at[2 * src_half + core],
            send_sem=csend.at[dst_half],
            recv_sem=crecv.at[src_half],
            device_id={"expert": 1, "group": 2 * dst_half + core},
            device_id_type=MESH,
        )

    def forward_copy(src_half, src_core):
        return pltpu.make_async_remote_copy(
            src_ref=land_hbm.at[2 * src_half + src_core],
            dst_ref=land_hbm.at[2 * src_half + src_core],
            send_sem=fsend.at[src_half],
            recv_sem=frecv.at[src_half],
            device_id={"expert": 1, "group": 2 * half + 1 - core},
            device_id_type=MESH,
        )

    @pl.when(e == 0)
    def _():
        for dst in range(4):
            z_copy(g, dst).start()
        for dst in range(2):
            cache_copy(half, dst).start()

    ld_b.wait()
    ld_mod.wait()
    b_mean = jnp.mean(b_v[...], axis=1, keepdims=True)
    tail_row = lax.broadcasted_iota(jnp.int32, (16, part), 0)
    for i in range(width // part):
        cols = pl.ds(i * part, part)
        modulate = mod_v[step_now, :, cols]
        scale = 1.0 + modulate[1:2, :]
        shift = modulate[0:1, :]
        top = (p_v[:, cols].astype(F32) - p_mean) * scale
        bias = (b_v[:, cols] - b_mean) * scale
        bottom = jnp.where(
            tail_row == 0,
            jnp.broadcast_to(bias, (16, part)),
            jnp.where(tail_row == 1, jnp.broadcast_to(shift, (16, part)), 0.0),
        )
        hi, lo = split(top)
        a2[0:64, cols] = hi
        a2[ROWS : ROWS + 64, cols] = lo
        hi, lo = split(bottom)
        a2[64:ROWS, cols] = hi
        a2[ROWS + 64 : 2 * ROWS, cols] = lo

    def x_copy(peer, slot):
        return pltpu.make_async_remote_copy(
            src_ref=xall.at[slot],
            dst_ref=xall.at[slot],
            send_sem=xsend.at[peer],
            recv_sem=xrecv.at[slot],
            device_id={"seq": peer},
            device_id_type=MESH,
        )

    ld_x.wait()

    @pl.when(e == 1)
    def _():
        for src in range(4):
            z_copy(src, 0).wait_recv()
        xall[s] = jnp.where(arrived, zin[source], x_v[...])

    @pl.when(e == 0)
    def _():
        xall[s] = x_v[...]

    def x_start(k, carry):
        x_copy(lax.rem(s + k, n), s).start()
        return carry

    lax.fori_loop(1, n, x_start, 0)

    def project(j):
        raw = dot(a2[...], w_v[j])
        total = raw[0:ROWS, :] + raw[ROWS : 2 * ROWS, :]
        m_v[j, 0:ROWS, :] = total
        return total

    ld_w[0].wait()
    m_q = project(0)
    ld_w[1].wait()
    m_k = project(1)
    gbuf[...] = jnp.zeros_like(gbuf)
    gbuf[:, 0:ROWS] = gram(m_q)
    gbuf[:, 128 : 128 + ROWS] = gram(m_k)

    def r_copy(peer, slot):
        return pltpu.make_async_remote_copy(
            src_ref=gbuf.at[pl.ds(pl.multiple_of(peer * 8, 8), 8)],
            dst_ref=rs_in.at[slot],
            send_sem=rsend.at[peer],
            recv_sem=rrecv.at[slot],
            device_id={"seq": peer},
            device_id_type=MESH,
        )

    def r_start(k, carry):
        peer = lax.rem(s + k, n)

        @pl.when(peer < RED)
        def _():
            r_copy(peer, s).start()

        return carry

    lax.fori_loop(1, n, r_start, 0)

    own_t = xall[s].astype(F32).T.astype(BF)
    own_x = jnp.concatenate([own_t, own_t], axis=1)
    squares = jnp.zeros((128, 128), F32)
    for i in range(width // part):
        cols = pl.ds(i * part, part)
        centred = dot(own_x, c2[:, cols]) + (b_v[:, cols] - b_mean)
        centred = centred * centred
        for k in range(part // 128):
            squares = squares + centred[:, k * 128 : (k + 1) * 128]
    var = jnp.sum(squares, axis=1, keepdims=True) * (1.0 / width)
    own_rstd = jnp.broadcast_to(lax.rsqrt(var + EPS), (128, 128)).T

    ld_w[2].wait()
    project(2)

    def a_copy(peer, slot):
        return pltpu.make_async_remote_copy(
            src_ref=ag.at[slot],
            dst_ref=ag.at[slot],
            send_sem=asend.at[peer],
            recv_sem=arecv.at[slot],
            device_id={"seq": peer},
            device_id_type=MESH,
        )

    ag[s, :, 256:384] = own_rstd[0:8, :]

    @pl.when(s < RED)
    def _():
        def r_wait(k, carry):
            r_copy(0, lax.rem(s + k, n)).wait_recv()
            return carry

        lax.fori_loop(1, n, r_wait, 0)
        rs_in[s] = gbuf[pl.ds(pl.multiple_of(s * 8, 8), 8), :]
        total = rs_in[0]
        for src in range(1, n):
            total = total + rs_in[src]
        ag[s, :, 0:256] = total

    @pl.when(s >= RED)
    def _():
        ag[s, :, 0:256] = jnp.zeros((8, 256), F32)

    def a_start(k, carry):
        a_copy(lax.rem(s + k, n), s).start()
        return carry

    lax.fori_loop(1, n, a_start, 0)

    ld_gain.wait()
    for j in range(3):
        m_v[j, ROWS:128, :] = jnp.zeros((128 - ROWS, 256), F32)
        full = m_v[j]
        if j < 2:
            full = full * gain_v[j : j + 1, :]
        flipped = full.T
        hi, lo = split(flipped)
        mt2[j, :, 0:128] = hi
        mt2[j, :, 128:256] = lo
        mtf[j] = flipped

    first16 = lax.broadcasted_iota(jnp.int32, (16, tokens), 0)
    first128 = lax.broadcasted_iota(jnp.int32, (128, tokens), 0)
    one16 = jnp.where(first16 == 0, 1.0, 0.0).astype(BF)
    one128 = jnp.where(first128 == 0, 1.0, 0.0).astype(BF)
    for h in range(2):
        qaug[h, 128:256, :] = one128
        vaug[h, 128:144, :] = one16
    key_at = lax.broadcasted_iota(jnp.int32, (128, 128), 0)
    for i in range(n):
        masks = jnp.where(key_at + order[i] * 128 >= length, MASKED, 0.0).astype(BF)
        for h in range(2):
            kaug[h, i * 128 : (i + 1) * 128, 128:256] = masks

    def x_wait(k, carry):
        x_copy(0, lax.rem(s + k, n)).wait_recv()
        return carry

    lax.fori_loop(1, n, x_wait, 0)
    tail64 = lax.broadcasted_iota(jnp.int32, (64, 128), 0)
    ones_row = jnp.where(tail64 == 0, 1.0, 0.0).astype(BF)
    for i in range(n):
        cols = slice(i * 128, (i + 1) * 128)
        rows = xall[order[i]]
        z2[0:64, cols] = rows
        z2[128:192, cols] = rows
        z2[64:128, cols] = ones_row
        z2[192:256, cols] = ones_row

    def a_wait(k, carry):
        a_copy(0, lax.rem(s + k, n)).wait_recv()
        return carry

    lax.fori_loop(1, n, a_wait, 0)
    rstd = jnp.concatenate([ag[order[i], 0:1, 256:384] for i in range(n)], axis=1)
    both = jnp.concatenate([ag[d, :, 0:256] for d in range(RED)], axis=0)
    z0 = z2[0:128, :]
    z0f = z0[0:ROWS, :].astype(F32)
    scales = []
    for j in range(2):
        g_j = both[:, j * 128 : (j + 1) * 128]
        hi, lo = split(g_j)
        t = dot(hi, z0) + dot(lo, z0)
        quad = jnp.sum(t * z0f, axis=0, keepdims=True)
        total = rstd * rstd * quad + 2.0 * rstd * t[65:66, :] + g_j[65:66, 65:66]
        scales.append(lax.rsqrt(jnp.maximum(total, 0.0) * (1.0 / (n * 256)) + EPS))
    r_q = scales[0] * (LOG2E / HD**0.5)
    r_k = scales[1]

    piece = 512
    for i in range(tokens // piece):
        cols = slice(i * piece, (i + 1) * piece)
        rhs = z2[:, cols]
        r_i = rstd[:, cols]
        q_w = r_q[:, cols]
        k_w = r_k[:, cols]
        q_t = (dot(mt2[0], rhs) * (q_w * r_i) + mtf[0, :, 65:66] * q_w).astype(BF)
        k_t = dot(mt2[1], rhs) * (k_w * r_i) + mtf[1, :, 65:66] * k_w
        v_t = (dot(mt2[2], rhs) * r_i + mtf[2, :, 65:66]).astype(BF)
        for h in range(2):
            rows = slice(h * 128, (h + 1) * 128)
            qaug[h, 0:128, cols] = q_t[rows, :]
            vaug[h, 0:128, cols] = v_t[rows, :]
            kaug[h, cols, 0:128] = k_t[rows, :].T.astype(BF)

    blocks = tokens // QB

    def o_copy(block, side, h, peer, src):
        return pltpu.make_async_remote_copy(
            src_ref=ostage.at[h, block, pl.ds(side * 128, 128)],
            dst_ref=out_hbm.at[:, pl.ds(pl.multiple_of(src * 256 + h * 128, 128), 128)],
            send_sem=osend.at[h, OWNERS * block + side],
            recv_sem=orecv.at[h, src],
            device_id={"seq": peer},
            device_id_type=MESH,
        )

    def own_copy(h):
        return pltpu.make_async_copy(
            ostage.at[h, blocks - 1, pl.ds((OWNERS - 1) * 128, 128)],
            out_hbm.at[:, pl.ds(pl.multiple_of(s * 256 + h * 128, 128), 128)],
            load_sem.at[h],
        )

    def block_owner(block, side):
        return owner([pick(block, [STEPS[b][side][a] for b in range(blocks)]) for a in range(2)])

    def send(block, h):
        for side in range(OWNERS - 1):
            o_copy(block, side, h, block_owner(block, side), s).start()

        @pl.when(block < blocks - 1)
        def _():
            o_copy(block, OWNERS - 1, h, block_owner(block, OWNERS - 1), s).start()

        @pl.when(block == blocks - 1)
        def _():
            own_copy(h).start()

    def unit(block, h, now, top, next_block, next_h, later):
        query = qaug[next_h, :, pl.ds(pl.multiple_of(next_block * QB, QB), QB)]
        next_top = jnp.full((8, QB), -3e38, F32)
        total = jnp.zeros((144, QB), F32)
        for c in range(tokens // KB):
            rows = slice(c * KB, (c + 1) * KB)
            score = dot(kaug[next_h, rows, :], query)
            later[rows, :] = score
            next_top = jnp.maximum(next_top, jnp.max(score.reshape(KB // 8, 8, QB), axis=0))
            weight = jnp.exp2(now[rows, :] - top).astype(BF)
            total = total + dot(vaug[h, :, rows], weight)
        row = lax.broadcasted_iota(jnp.int32, (1, 128), 1)
        live = [row + block_owner(block, side) * 128 < length for side in range(OWNERS)]
        inverse = 1.0 / total[128:129, :]
        inverse = jnp.concatenate(
            [jnp.where(live[a], inverse[:, a * 128 : (a + 1) * 128], 0.0) for a in range(OWNERS)], axis=1
        )
        ostage[h, block] = (total[0:128, :] * inverse).T.astype(BF)
        return jnp.max(next_top, axis=0, keepdims=True)

    def attend(block, top):
        top = unit(block, 0, s_a, top, block, 1, s_b)
        send(block, 0)
        top = unit(block, 1, s_b, top, lax.rem(block + 1, blocks), 0, s_a)
        send(block, 1)
        return top

    first_top = jnp.full((8, QB), -3e38, F32)
    for c in range(tokens // KB):
        rows = slice(c * KB, (c + 1) * KB)
        score = dot(kaug[0, rows, :], qaug[0, :, 0:QB])
        s_a[rows, :] = score
        first_top = jnp.maximum(first_top, jnp.max(score.reshape(KB // 8, 8, QB), axis=0))
    lax.fori_loop(0, blocks, attend, jnp.max(first_top, axis=0, keepdims=True))

    @pl.when(e == 1)
    def _():
        for src in range(2):
            cache_copy(src, 0).wait_recv()
            forward_copy(src, core).start()
        for src in range(2):
            forward_copy(src, core).wait_send()
            forward_copy(src, 1 - core).wait_recv()

    @pl.when(e == 0)
    def _():
        for dst in range(4):
            z_copy(g, dst).wait_send()
        for dst in range(2):
            cache_copy(half, dst).wait_send()

    def finish(k, carry):
        peer = lax.rem(s + k, n)
        x_copy(peer, s).wait_send()
        a_copy(peer, s).wait_send()

        @pl.when(peer < RED)
        def _():
            r_copy(peer, s).wait_send()

        for h in range(2):
            o_copy(lax.div(k - 1, OWNERS), lax.rem(k - 1, OWNERS), h, peer, s).wait_send()
            o_copy(0, 0, h, peer, peer).wait_recv()
        return carry

    lax.fori_loop(1, n, finish, 0)
    for h in range(2):
        own_copy(h).wait()


def place(crossing, raw, land, cache, out, cache_out, rows_v, cache_v, sem):
    e = lax.axis_index("expert")
    g = lax.axis_index("group")
    hit0 = crossing[0, 1] == g
    hit1 = crossing[1, 1] == g
    arrived = jnp.logical_and(e == 1, jnp.logical_or(hit0, hit1))
    left = jnp.logical_and(e == 0, jnp.logical_or(crossing[0, 0] == g, crossing[1, 0] == g))
    source = jnp.where(hit0, crossing[0, 0], jnp.where(hit1, crossing[1, 0], 0))
    parts = 4
    height = raw.shape[0] // parts
    reads = []
    writes = []
    for i in range(parts):
        rows = pl.ds(i * height, height)
        reads.append(pltpu.make_async_copy(raw.at[rows], rows_v.at[rows], sem.at[0, i]))
        writes.append(pltpu.make_async_copy(rows_v.at[rows], out.at[rows], sem.at[1, i]))
    read_cache = pltpu.make_async_copy(cache, cache_v, sem.at[0, parts])
    write_cache = pltpu.make_async_copy(cache_v, cache_out, sem.at[1, parts])

    @pl.when(arrived)
    def _():
        pltpu.make_async_copy(land.at[source], cache_v, sem.at[0, parts]).start()

    @pl.when(jnp.logical_not(arrived))
    def _():
        read_cache.start()

    for copy in reads:
        copy.start()
    read_cache.wait()

    @pl.when(left)
    def _():
        cache_v[...] = jnp.zeros_like(cache_v)

    write_cache.start()
    for read, write in zip(reads, writes):
        read.wait()
        write.start()
    write_cache.wait()
    for write in writes:
        write.wait()


def shards(
    n,
    latent,
    text_cache,
    patch_weight,
    patch_bias,
    qkv_weight,
    qk_gain,
    modulation,
    step_index,
    lengths,
    crossing,
):
    tokens = n * 128
    width = qkv_weight.shape[1]
    xt = latent[0, 0].T
    w3 = jnp.transpose(qkv_weight[0], (1, 0, 2))
    cache = text_cache[0, 0]
    smem = pl.BlockSpec(memory_space=pltpu.SMEM)
    hbm = pl.BlockSpec(memory_space=pl.ANY)
    dma = pltpu.SemaphoreType.DMA
    raw, land = pl.pallas_call(
        functools.partial(kernel, n),
        out_shape=(
            jax.ShapeDtypeStruct((128, n * 256), BF),
            jax.ShapeDtypeStruct((4,) + cache.shape, BF),
        ),
        in_specs=[smem] * 3 + [hbm] * 7,
        out_specs=(hbm, hbm),
        scratch_shapes=[
            pltpu.VMEM((64, 128), BF),
            pltpu.VMEM((1, width), F32),
            pltpu.VMEM((2, 256), F32),
            pltpu.VMEM((64, width), BF),
            pltpu.VMEM(modulation.shape[1:], F32),
            pltpu.VMEM((3, width, 256), BF),
            pltpu.VMEM((2 * ROWS, width), BF),
            pltpu.VMEM((128, width), BF),
            pltpu.VMEM((4, 64, 128), BF),
            pltpu.VMEM((n, 64, 128), BF),
            pltpu.VMEM((3, 128, 256), F32),
            pltpu.VMEM((ROWS, 256), F32),
            pltpu.VMEM((n, 8, 256), F32),
            pltpu.VMEM((n, 8, 384), F32),
            pltpu.VMEM((256, tokens), BF),
            pltpu.VMEM((3, 256, 256), BF),
            pltpu.VMEM((3, 256, 128), F32),
            pltpu.VMEM((2, 256, tokens), BF),
            pltpu.VMEM((2, tokens, 256), BF),
            pltpu.VMEM((2, 144, tokens), BF),
            pltpu.VMEM((tokens, QB), F32),
            pltpu.VMEM((tokens, QB), F32),
            pltpu.VMEM((2, tokens // QB, QB, 128), BF),
            dma((8,)),
            dma((4,)),
            dma((4,)),
            dma((2,)),
            dma((2,)),
            dma((2,)),
            dma((2,)),
            dma((n,)),
            dma((n,)),
            dma((n,)),
            dma((n,)),
            dma((n,)),
            dma((n,)),
            dma((2, n)),
            dma((2, n)),
        ],
        compiler_params=pltpu.CompilerParams(
            collective_id=0, has_side_effects=True, vmem_limit_bytes=58 * 1024 * 1024
        ),
    )(
        crossing,
        lengths,
        step_index,
        xt,
        patch_bias,
        qk_gain[0],
        patch_weight[0],
        modulation[0],
        w3,
        cache,
    )
    attended, cache_after = pl.pallas_call(
        place,
        out_shape=(
            jax.ShapeDtypeStruct(raw.shape, BF),
            jax.ShapeDtypeStruct(cache.shape, BF),
        ),
        in_specs=[smem, hbm, hbm, hbm],
        out_specs=(hbm, hbm),
        scratch_shapes=[pltpu.VMEM(raw.shape, BF), pltpu.VMEM(cache.shape, BF), dma((2, 5))],
    )(crossing, raw, land, cache)
    return (attended[None, None], cache_after[None, None])


def solution(mesh):
    in_specs = (
        P("expert", "group", "seq", None),
        P("expert", "group", None, "seq", None),
        P("expert", None, None),
        P("expert", None),
        P("expert", None, None, "seq"),
        P("expert", None, "seq"),
        P("expert", None, None, None),
        P(),
        P(),
        P(),
    )
    out_specs = (P("expert", "group", "seq", None), P("expert", "group", None, "seq", None))
    return jax.shard_map(
        functools.partial(shards, mesh.shape["seq"]),
        mesh=mesh,
        in_specs=in_specs,
        out_specs=out_specs,
        check_vma=False,
    )
```

```python
import functools

import jax
import jax.numpy as jnp
from jax import lax
from jax.experimental import pallas as pl
from jax.experimental.pallas import tpu as pltpu
from jax.sharding import PartitionSpec as P

HD = 128
EPS = 1e-06
MASKED = -1e30
LOG2E = 1.4426950408889634
BF = jnp.bfloat16
F32 = jnp.float32
MESH = pl.DeviceIdType.MESH
ROWS = 80
PACKED = 40
SIDE = 4
QB = 512
KB = 256
OWNERS = QB // 128
STEPS = (
    ((1, 0), (3, 0), (1, 2), (3, 2)),
    ((0, 1), (0, 3), (2, 1), (2, 3)),
    ((1, 1), (3, 3), (2, 0), (0, 2)),
    ((1, 3), (3, 1), (2, 2), (0, 0)),
)


def dot(a, b):
    return jnp.dot(a, b, preferred_element_type=F32)


def dot_nt(a, b):
    return lax.dot_general(a, b, (((1,), (1,)), ((), ())), preferred_element_type=F32)


def split(a):
    hi = a.astype(BF)
    lo = (a - hi.astype(F32)).astype(BF)
    return hi, lo


def gram(a):
    hi, lo = split(a)
    return dot_nt(hi, hi) + dot_nt(hi, lo) + dot_nt(lo, hi)


def pick(block, choices):
    value = choices[-1]
    for at in range(len(choices) - 2, -1, -1):
        value = jnp.where(block == at, choices[at], value)
    return value


def kernel(
    n,
    crossing_hbm,
    lengths_hbm,
    steps_hbm,
    xt_hbm,
    b_hbm,
    gain_hbm,
    p_hbm,
    mod_hbm,
    w_hbm,
    cache_hbm,
    out_hbm,
    land_hbm,
    crossing,
    lengths,
    steps,
    x_v,
    b_v,
    gain_v,
    p_v,
    mod_v,
    w_v,
    a2,
    c2,
    zin,
    xall,
    m_v,
    gbuf,
    g_in,
    z2,
    mt2,
    mtf,
    raw_v,
    qaug,
    kaug,
    vaug,
    s_a,
    s_b,
    ostage,
    load_sem,
    zsend,
    zrecv,
    csend,
    crecv,
    fsend,
    frecv,
    xsend,
    xrecv,
    gsend,
    grecv,
    osend,
    orecv,
):
    e = lax.axis_index("expert")
    g = lax.axis_index("group")
    s = lax.axis_index("seq")
    half = lax.div(g, 2)
    core = lax.rem(g, 2)
    my_x = lax.div(s, SIDE)
    my_y = lax.rem(s, SIDE)
    tokens = n * 128
    width = p_v.shape[1]

    def owner(step):
        return lax.rem(my_x + step[0], SIDE) * SIDE + lax.rem(my_y + step[1], SIDE)

    order = [owner(step) for block in STEPS for step in block]

    ld_p = pltpu.make_async_copy(p_hbm, p_v, load_sem.at[0])
    ld_b = pltpu.make_async_copy(b_hbm, b_v, load_sem.at[1])
    ld_x = pltpu.make_async_copy(xt_hbm, x_v, load_sem.at[2])
    ld_mod = pltpu.make_async_copy(mod_hbm, mod_v, load_sem.at[3])
    ld_gain = pltpu.make_async_copy(gain_hbm, gain_v, load_sem.at[4])
    ld_w = [pltpu.make_async_copy(w_hbm.at[j], w_v.at[j], load_sem.at[5 + j]) for j in range(3)]
    ld_scalars = [
        pltpu.make_async_copy(src, dst, load_sem.at[8 + i])
        for i, (src, dst) in enumerate(
            ((crossing_hbm, crossing), (lengths_hbm, lengths), (steps_hbm, steps))
        )
    ]
    for copy in [ld_x] + ld_scalars + [ld_p, ld_b, ld_mod, ld_gain] + ld_w:
        copy.start()

    barrier = pltpu.get_barrier_semaphore()

    def greet(k, carry):
        pl.semaphore_signal(barrier, inc=1, device_id={"seq": lax.rem(s + k, n)}, device_id_type=MESH)
        return carry

    for other in range(4):
        pl.semaphore_signal(
            barrier, inc=1, device_id={"expert": 1 - e, "group": other}, device_id_type=MESH
        )
    lax.fori_loop(1, n, greet, 0)

    @pl.when(e == 1)
    def _():
        pl.semaphore_signal(barrier, inc=1, device_id={"group": 2 * half + 1 - core}, device_id_type=MESH)

    def z_copy(src_group, dst_group):
        return pltpu.make_async_remote_copy(
            src_ref=xt_hbm,
            dst_ref=zin.at[src_group],
            send_sem=zsend.at[dst_group],
            recv_sem=zrecv.at[src_group],
            device_id={"expert": 1, "group": dst_group},
            device_id_type=MESH,
        )

    def cache_copy(src_half, dst_half):
        return pltpu.make_async_remote_copy(
            src_ref=cache_hbm,
            dst_ref=land_hbm.at[2 * src_half + core],
            send_sem=csend.at[dst_half],
            recv_sem=crecv.at[src_half],
            device_id={"expert": 1, "group": 2 * dst_half + core},
            device_id_type=MESH,
        )

    def forward_copy(src_half, src_core):
        return pltpu.make_async_remote_copy(
            src_ref=land_hbm.at[2 * src_half + src_core],
            dst_ref=land_hbm.at[2 * src_half + src_core],
            send_sem=fsend.at[src_half],
            recv_sem=frecv.at[src_half],
            device_id={"expert": 1, "group": 2 * half + 1 - core},
            device_id_type=MESH,
        )

    def x_copy(peer, slot):
        return pltpu.make_async_remote_copy(
            src_ref=xall.at[slot],
            dst_ref=xall.at[slot],
            send_sem=xsend.at[peer],
            recv_sem=xrecv.at[slot],
            device_id={"seq": peer},
            device_id_type=MESH,
        )

    def x_start(k, carry):
        x_copy(lax.rem(s + k, n), s).start()
        return carry

    ld_x.wait()
    pl.semaphore_wait(barrier, n - 1 + 4 + e)

    @pl.when(e == 0)
    def _():
        for dst in range(4):
            z_copy(g, dst).start()
        xall[s] = x_v[...]
        lax.fori_loop(1, n, x_start, 0)
        for dst in range(2):
            cache_copy(half, dst).start()

    for copy in ld_scalars:
        copy.wait()
    hit0 = crossing[0, 1] == g
    hit1 = crossing[1, 1] == g
    arrived = jnp.logical_and(e == 1, jnp.logical_or(hit0, hit1))
    left = jnp.logical_and(e == 0, jnp.logical_or(crossing[0, 0] == g, crossing[1, 0] == g))
    source = jnp.where(hit0, crossing[0, 0], jnp.where(hit1, crossing[1, 0], 0))
    step_now = jnp.where(arrived, steps[0, source], steps[e, g])
    length = jnp.where(left, 0, jnp.where(arrived, lengths[0, source], lengths[e, g]))

    ld_p.wait()
    ld_b.wait()
    p_mean = jnp.mean(p_v[...].astype(F32), axis=1, keepdims=True)
    b_mean = jnp.mean(b_v[...], axis=1, keepdims=True)
    ld_mod.wait()
    part = 1024
    tail_row = lax.broadcasted_iota(jnp.int32, (16, part), 0)
    for i in range(width // part):
        cols = pl.ds(i * part, part)
        modulate = mod_v[step_now, :, cols]
        scale = 1.0 + modulate[1:2, :]
        shift = modulate[0:1, :]
        top = (p_v[:, cols].astype(F32) - p_mean) * scale
        bias = (b_v[:, cols] - b_mean) * scale
        bottom = jnp.where(
            tail_row == 0,
            jnp.broadcast_to(bias, (16, part)),
            jnp.where(tail_row == 1, jnp.broadcast_to(shift, (16, part)), 0.0),
        )
        hi, lo = split(top)
        a2[0:64, cols] = hi
        a2[ROWS : ROWS + 64, cols] = lo
        hi, lo = split(bottom)
        a2[64:ROWS, cols] = hi
        a2[ROWS + 64 : 2 * ROWS, cols] = lo

    def project(j):
        raw = dot(a2[...], w_v[j])
        total = raw[0:ROWS, :] + raw[ROWS : 2 * ROWS, :]
        m_v[j, 0:ROWS, :] = total
        return total

    ld_w[0].wait()
    m_q = project(0)
    ld_w[1].wait()
    m_k = project(1)

    @pl.when(e == 1)
    def _():
        for src in range(4):
            z_copy(src, 0).wait_recv()
        xall[s] = jnp.where(arrived, zin[source], x_v[...])
        lax.fori_loop(1, n, x_start, 0)

    gram_q = gram(m_q)
    gram_k = gram(m_k)
    at_row = lax.broadcasted_iota(jnp.int32, (64, 64), 0)
    at_col = lax.broadcasted_iota(jnp.int32, (64, 64), 1)
    core_q = gram_q[0:64, 0:64]
    core_k = gram_k[0:64, 0:64]
    both = jnp.where(at_col < at_row, 2.0 * core_q, jnp.where(at_col == at_row, core_q, 2.0 * core_k))
    gbuf[...] = jnp.zeros_like(gbuf)
    gbuf[0:32, 0:64] = both[0:32, :]
    gbuf[0:32, 64:128] = both[32:64, :]
    for at, values in enumerate((gram_q, gram_k)):
        gbuf[32:34, at * 64 : at * 64 + 64] = values[64:66, 0:64]
        gbuf[35 + 2 * at : 37 + 2 * at, 0:16] = values[64:66, 64:80]
    gbuf[34:35, 0:64] = jnp.sum(jnp.where(at_col == at_row, core_k, 0.0), axis=0, keepdims=True)

    def g_copy(peer, slot):
        return pltpu.make_async_remote_copy(
            src_ref=gbuf,
            dst_ref=g_in.at[slot],
            send_sem=gsend.at[peer],
            recv_sem=grecv.at[slot],
            device_id={"seq": peer},
            device_id_type=MESH,
        )

    def g_start(k, carry):
        g_copy(lax.rem(s + k, n), s).start()
        return carry

    lax.fori_loop(1, n, g_start, 0)
    g_in[s] = gbuf[...]

    for i in range(width // part):
        cols = pl.ds(i * part, part)
        hi, lo = split(p_v[:, cols].astype(F32) - p_mean)
        c2[0:64, cols] = hi
        c2[ROWS : ROWS + 64, cols] = lo
        bias = jnp.broadcast_to(b_v[:, cols] - b_mean, (16, part))
        hi, lo = split(jnp.where(tail_row == 0, bias, 0.0))
        c2[64:ROWS, cols] = hi
        c2[ROWS + 64 : 2 * ROWS, cols] = lo
    var_gram = (
        dot_nt(c2[0:ROWS, :], c2[0:ROWS, :])
        + dot_nt(c2[0:ROWS, :], c2[ROWS : 2 * ROWS, :])
        + dot_nt(c2[ROWS : 2 * ROWS, :], c2[0:ROWS, :])
    ) * (1.0 / width)

    ld_w[2].wait()
    project(2)

    ld_gain.wait()
    for j in range(3):
        m_v[j, ROWS:128, :] = jnp.zeros((128 - ROWS, 256), F32)
        full = m_v[j]
        if j < 2:
            full = full * gain_v[j : j + 1, :]
        flipped = full.T
        hi, lo = split(flipped)
        mt2[j, :, 0:128] = hi
        mt2[j, :, 128:256] = lo
        mtf[j] = flipped

    first16 = lax.broadcasted_iota(jnp.int32, (16, tokens), 0)
    first128 = lax.broadcasted_iota(jnp.int32, (128, tokens), 0)
    one16 = jnp.where(first16 == 0, 1.0, 0.0).astype(BF)
    one128 = jnp.where(first128 == 0, 1.0, 0.0).astype(BF)
    for h in range(2):
        qaug[h, 128:256, :] = one128
        vaug[h, 128:144, :] = one16
    key_at = lax.broadcasted_iota(jnp.int32, (128, 128), 0)
    for i in range(n):
        masks = jnp.where(key_at + order[i] * 128 >= length, MASKED, 0.0).astype(BF)
        for h in range(2):
            kaug[h, i * 128 : (i + 1) * 128, 128:256] = masks

    def x_wait(k, carry):
        x_copy(0, lax.rem(s + k, n)).wait_recv()
        return carry

    lax.fori_loop(1, n, x_wait, 0)
    tail64 = lax.broadcasted_iota(jnp.int32, (64, 128), 0)
    ones_row = jnp.where(tail64 == 0, 1.0, 0.0).astype(BF)
    for i in range(n):
        cols = slice(i * 128, (i + 1) * 128)
        rows = xall[order[i]]
        z2[0:64, cols] = rows
        z2[128:192, cols] = rows
        z2[64:128, cols] = ones_row
        z2[192:256, cols] = ones_row

    x64 = z2[0:64, :]
    z80 = z2[0:ROWS, :]
    hi, lo = split(var_gram)
    t = dot(hi, z80) + dot(lo, z80)
    var = jnp.maximum(jnp.sum(t * z80.astype(F32), axis=0, keepdims=True), 0.0)
    rstd = lax.rsqrt(var + EPS)

    piece = 512
    for i in range(tokens // piece):
        cols = slice(i * piece, (i + 1) * piece)
        rhs = z2[:, cols]
        r_i = rstd[:, cols]
        for j in range(2):
            raw_v[j, :, cols] = dot(mt2[j], rhs) * r_i + mtf[j, :, 65:66]
        v_t = (dot(mt2[2], rhs) * r_i + mtf[2, :, 65:66]).astype(BF)
        for h in range(2):
            vaug[h, 0:128, cols] = v_t[h * 128 : (h + 1) * 128, :]

    def g_wait(k, carry):
        g_copy(0, lax.rem(s + k, n)).wait_recv()
        return carry

    lax.fori_loop(1, n, g_wait, 0)
    packed = g_in[0]
    for src in range(1, n):
        packed = packed + g_in[src]
    both = jnp.concatenate([packed[0:32, 0:64], packed[0:32, 64:128]], axis=0)
    lower = jnp.where(at_col <= at_row, both, 0.0)
    diagonal = jnp.where(at_col == at_row, jnp.broadcast_to(packed[34:35, 0:64], (64, 64)), 0.0)
    upper = jnp.where(at_col > at_row, both, diagonal)
    tail16 = lax.broadcasted_iota(jnp.int32, (16, 64), 0)
    linear = jnp.zeros((16, 64), F32)
    for at, row in enumerate(
        (packed[32:33, 0:64], packed[33:34, 0:64], packed[32:33, 64:128], packed[33:34, 64:128])
    ):
        linear = jnp.where(tail16 == at, jnp.broadcast_to(row, (16, 64)), linear)
    hi, lo = split(jnp.concatenate([lower, upper, linear], axis=0))
    t = dot(hi, x64) + dot(lo, x64)
    xf = x64.astype(F32)
    scales = []
    for j in range(2):
        quad = jnp.sum(t[j * 64 : j * 64 + 64, :] * xf, axis=0, keepdims=True)
        by_bias = t[128 + 2 * j : 129 + 2 * j, :]
        by_shift = t[129 + 2 * j : 130 + 2 * j, :]
        at = 35 + 2 * j
        total = (
            rstd * rstd * (quad + 2.0 * by_bias + packed[at : at + 1, 0:1])
            + 2.0 * rstd * (by_shift + packed[at : at + 1, 1:2])
            + packed[at + 1 : at + 2, 1:2]
        )
        scales.append(lax.rsqrt(jnp.maximum(total, 0.0) * (1.0 / (n * 256)) + EPS))
    r_q = scales[0] * (LOG2E / HD**0.5)
    r_k = scales[1]

    for i in range(tokens // piece):
        cols = slice(i * piece, (i + 1) * piece)
        for h in range(2):
            rows = slice(h * 128, (h + 1) * 128)
            qaug[h, 0:128, cols] = (raw_v[0, rows, cols] * r_q[:, cols]).astype(BF)
            kaug[h, cols, 0:128] = (raw_v[1, rows, cols] * r_k[:, cols]).T.astype(BF)

    blocks = tokens // QB

    def o_copy(block, side, h, peer, src):
        return pltpu.make_async_remote_copy(
            src_ref=ostage.at[h, block, pl.ds(side * 128, 128)],
            dst_ref=out_hbm.at[:, pl.ds(pl.multiple_of(src * 256 + h * 128, 128), 128)],
            send_sem=osend.at[h, OWNERS * block + side],
            recv_sem=orecv.at[h, src],
            device_id={"seq": peer},
            device_id_type=MESH,
        )

    def own_copy(h):
        return pltpu.make_async_copy(
            ostage.at[h, blocks - 1, pl.ds((OWNERS - 1) * 128, 128)],
            out_hbm.at[:, pl.ds(pl.multiple_of(s * 256 + h * 128, 128), 128)],
            load_sem.at[h],
        )

    def block_owner(block, side):
        return owner([pick(block, [STEPS[b][side][a] for b in range(blocks)]) for a in range(2)])

    def send(block, h):
        for side in range(OWNERS - 1):
            o_copy(block, side, h, block_owner(block, side), s).start()

        @pl.when(block < blocks - 1)
        def _():
            o_copy(block, OWNERS - 1, h, block_owner(block, OWNERS - 1), s).start()

        @pl.when(block == blocks - 1)
        def _():
            own_copy(h).start()

    def unit(block, h, now, top, next_block, next_h, later):
        query = qaug[next_h, :, pl.ds(pl.multiple_of(next_block * QB, QB), QB)]
        next_top = jnp.full((8, QB), -3e38, F32)
        total = jnp.zeros((144, QB), F32)
        for c in range(tokens // KB):
            rows = slice(c * KB, (c + 1) * KB)
            score = dot(kaug[next_h, rows, :], query)
            later[rows, :] = score
            next_top = jnp.maximum(next_top, jnp.max(score.reshape(KB // 8, 8, QB), axis=0))
            weight = jnp.exp2(now[rows, :] - top).astype(BF)
            total = total + dot(vaug[h, :, rows], weight)
        row = lax.broadcasted_iota(jnp.int32, (1, 128), 1)
        live = [row + block_owner(block, side) * 128 < length for side in range(OWNERS)]
        inverse = 1.0 / total[128:129, :]
        inverse = jnp.concatenate(
            [jnp.where(live[a], inverse[:, a * 128 : (a + 1) * 128], 0.0) for a in range(OWNERS)], axis=1
        )
        ostage[h, block] = (total[0:128, :] * inverse).T.astype(BF)
        return jnp.max(next_top, axis=0, keepdims=True)

    def attend(block, top):
        top = unit(block, 0, s_a, top, block, 1, s_b)
        send(block, 0)
        top = unit(block, 1, s_b, top, lax.rem(block + 1, blocks), 0, s_a)
        send(block, 1)

        @pl.when(jnp.logical_and(e == 1, block == blocks // 2))
        def _():
            for src in range(2):
                cache_copy(src, 0).wait_recv()
                forward_copy(src, core).start()

        return top

    first_top = jnp.full((8, QB), -3e38, F32)
    for c in range(tokens // KB):
        rows = slice(c * KB, (c + 1) * KB)
        score = dot(kaug[0, rows, :], qaug[0, :, 0:QB])
        s_a[rows, :] = score
        first_top = jnp.maximum(first_top, jnp.max(score.reshape(KB // 8, 8, QB), axis=0))
    lax.fori_loop(0, blocks, attend, jnp.max(first_top, axis=0, keepdims=True))

    @pl.when(e == 1)
    def _():
        for src in range(2):
            forward_copy(src, core).wait_send()
            forward_copy(src, 1 - core).wait_recv()

    @pl.when(e == 0)
    def _():
        for dst in range(4):
            z_copy(g, dst).wait_send()
        for dst in range(2):
            cache_copy(half, dst).wait_send()

    def finish(k, carry):
        peer = lax.rem(s + k, n)
        x_copy(peer, s).wait_send()
        g_copy(peer, s).wait_send()
        for h in range(2):
            o_copy(lax.div(k - 1, OWNERS), lax.rem(k - 1, OWNERS), h, peer, s).wait_send()
            o_copy(0, 0, h, peer, peer).wait_recv()
        return carry

    lax.fori_loop(1, n, finish, 0)
    for h in range(2):
        own_copy(h).wait()


def place(crossing_hbm, raw, land, cache, out, cache_out, crossing, rows_v, cache_v, sem):
    e = lax.axis_index("expert")
    g = lax.axis_index("group")
    scalars = pltpu.make_async_copy(crossing_hbm, crossing, sem.at[0, 5])
    scalars.start()
    parts = 4
    height = raw.shape[0] // parts
    reads = []
    writes = []
    for i in range(parts):
        rows = pl.ds(i * height, height)
        reads.append(pltpu.make_async_copy(raw.at[rows], rows_v.at[rows], sem.at[0, i]))
        writes.append(pltpu.make_async_copy(rows_v.at[rows], out.at[rows], sem.at[1, i]))
    for copy in reads:
        copy.start()
    read_cache = pltpu.make_async_copy(cache, cache_v, sem.at[0, parts])
    write_cache = pltpu.make_async_copy(cache_v, cache_out, sem.at[1, parts])

    scalars.wait()
    hit0 = crossing[0, 1] == g
    hit1 = crossing[1, 1] == g
    arrived = jnp.logical_and(e == 1, jnp.logical_or(hit0, hit1))
    left = jnp.logical_and(e == 0, jnp.logical_or(crossing[0, 0] == g, crossing[1, 0] == g))
    source = jnp.where(hit0, crossing[0, 0], jnp.where(hit1, crossing[1, 0], 0))

    @pl.when(arrived)
    def _():
        pltpu.make_async_copy(land.at[source], cache_v, sem.at[0, parts]).start()

    @pl.when(jnp.logical_not(arrived))
    def _():
        read_cache.start()

    read_cache.wait()

    @pl.when(left)
    def _():
        cache_v[...] = jnp.zeros_like(cache_v)

    write_cache.start()
    for read, write in zip(reads, writes):
        read.wait()
        write.start()
    write_cache.wait()
    for write in writes:
        write.wait()


def shards(
    n,
    latent,
    text_cache,
    patch_weight,
    patch_bias,
    qkv_weight,
    qk_gain,
    modulation,
    step_index,
    lengths,
    crossing,
):
    tokens = n * 128
    width = qkv_weight.shape[1]
    xt = latent[0, 0].T
    w3 = jnp.transpose(qkv_weight[0], (1, 0, 2))
    cache = text_cache[0, 0]
    hbm = pl.BlockSpec(memory_space=pl.ANY)
    dma = pltpu.SemaphoreType.DMA
    raw, land = pl.pallas_call(
        functools.partial(kernel, n),
        out_shape=(
            jax.ShapeDtypeStruct((128, n * 256), BF),
            jax.ShapeDtypeStruct((4,) + cache.shape, BF),
        ),
        in_specs=[hbm] * 10,
        out_specs=(hbm, hbm),
        scratch_shapes=[
            pltpu.SMEM((2, 2), jnp.int32),
            pltpu.SMEM((2, 4), jnp.int32),
            pltpu.SMEM((2, 4), jnp.int32),
            pltpu.VMEM((64, 128), BF),
            pltpu.VMEM((1, width), F32),
            pltpu.VMEM((2, 256), F32),
            pltpu.VMEM((64, width), BF),
            pltpu.VMEM(modulation.shape[1:], F32),
            pltpu.VMEM((3, width, 256), BF),
            pltpu.VMEM((2 * ROWS, width), BF),
            pltpu.VMEM((2 * ROWS, width), BF),
            pltpu.VMEM((4, 64, 128), BF),
            pltpu.VMEM((n, 64, 128), BF),
            pltpu.VMEM((3, 128, 256), F32),
            pltpu.VMEM((PACKED, 128), F32),
            pltpu.VMEM((n, PACKED, 128), F32),
            pltpu.VMEM((256, tokens), BF),
            pltpu.VMEM((3, 256, 256), BF),
            pltpu.VMEM((3, 256, 128), F32),
            pltpu.VMEM((2, 256, tokens), F32),
            pltpu.VMEM((2, 256, tokens), BF),
            pltpu.VMEM((2, tokens, 256), BF),
            pltpu.VMEM((2, 144, tokens), BF),
            pltpu.VMEM((tokens, QB), F32),
            pltpu.VMEM((tokens, QB), F32),
            pltpu.VMEM((2, tokens // QB, QB, 128), BF),
            dma((11,)),
            dma((4,)),
            dma((4,)),
            dma((2,)),
            dma((2,)),
            dma((2,)),
            dma((2,)),
            dma((n,)),
            dma((n,)),
            dma((n,)),
            dma((n,)),
            dma((2, n)),
            dma((2, n)),
        ],
        compiler_params=pltpu.CompilerParams(
            collective_id=0, has_side_effects=True, vmem_limit_bytes=58 * 1024 * 1024
        ),
    )(
        crossing,
        lengths,
        step_index,
        xt,
        patch_bias,
        qk_gain[0],
        patch_weight[0],
        modulation[0],
        w3,
        cache,
    )
    attended, cache_after = pl.pallas_call(
        place,
        out_shape=(
            jax.ShapeDtypeStruct(raw.shape, BF),
            jax.ShapeDtypeStruct(cache.shape, BF),
        ),
        in_specs=[hbm] * 4,
        out_specs=(hbm, hbm),
        scratch_shapes=[
            pltpu.SMEM((2, 2), jnp.int32),
            pltpu.VMEM(raw.shape, BF),
            pltpu.VMEM(cache.shape, BF),
            dma((2, 6)),
        ],
    )(crossing, raw, land, cache)
    return (attended[None, None], cache_after[None, None])


def solution(mesh):
    in_specs = (
        P("expert", "group", "seq", None),
        P("expert", "group", None, "seq", None),
        P("expert", None, None),
        P("expert", None),
        P("expert", None, None, "seq"),
        P("expert", None, "seq"),
        P("expert", None, None, None),
        P(),
        P(),
        P(),
    )
    out_specs = (P("expert", "group", "seq", None), P("expert", "group", None, "seq", None))
    return jax.shard_map(
        functools.partial(shards, mesh.shape["seq"]),
        mesh=mesh,
        in_specs=in_specs,
        out_specs=out_specs,
        check_vma=False,
    )
```

```python
import functools

import jax
import jax.numpy as jnp
from jax import lax
from jax.experimental import pallas as pl
from jax.experimental.pallas import tpu as pltpu
from jax.sharding import PartitionSpec as P

HD = 128
EPS = 1e-06
MASKED = -1e30
LOG2E = 1.4426950408889634
BF = jnp.bfloat16
F32 = jnp.float32
MESH = pl.DeviceIdType.MESH
ROWS = 80
PACKED = 40
SIDE = 4
QB = 512
KB = 256
OWNERS = QB // 128
STEPS = (
    ((1, 0), (3, 0), (1, 2), (3, 2))
    + ((0, 1), (0, 3), (2, 1), (2, 3))
    + ((1, 1), (3, 3), (2, 0), (0, 2))
    + ((1, 3), (3, 1), (2, 2), (0, 0))
)


def dot(a, b):
    return jnp.dot(a, b, preferred_element_type=F32)


def dot_nt(a, b):
    return lax.dot_general(a, b, (((1,), (1,)), ((), ())), preferred_element_type=F32)


def split(a):
    hi = a.astype(BF)
    lo = (a - hi.astype(F32)).astype(BF)
    return hi, lo


def gram(a):
    hi, lo = split(a)
    return dot_nt(hi, hi) + dot_nt(hi, lo) + dot_nt(lo, hi)


def pick(block, choices):
    value = choices[-1]
    for at in range(len(choices) - 2, -1, -1):
        value = jnp.where(block == at, choices[at], value)
    return value


def kernel(
    n,
    crossing_hbm,
    lengths_hbm,
    steps_hbm,
    xt_hbm,
    b_hbm,
    gain_hbm,
    p_hbm,
    mod_hbm,
    w_hbm,
    cache_hbm,
    out_hbm,
    cache_out,
    crossing,
    lengths,
    steps,
    x_v,
    b_v,
    gain_v,
    p_v,
    mod_v,
    w_v,
    a2,
    c2,
    zin,
    xall,
    m_v,
    gbuf,
    g_in,
    z2,
    mt2,
    mtf,
    qaug,
    kaug,
    vaug,
    s_a,
    s_b,
    ostage,
    own_cache,
    land,
    load_sem,
    zsend,
    zrecv,
    csend,
    crecv,
    fsend,
    frecv,
    xsend,
    xrecv,
    gsend,
    grecv,
    osend,
    orecv,
):
    e = lax.axis_index("expert")
    g = lax.axis_index("group")
    s = lax.axis_index("seq")
    half = lax.div(g, 2)
    core = lax.rem(g, 2)
    my_x = lax.div(s, SIDE)
    my_y = lax.rem(s, SIDE)
    tokens = n * 128
    width = p_v.shape[1]

    def owner(step):
        return lax.rem(my_x + step[0], SIDE) * SIDE + lax.rem(my_y + step[1], SIDE)

    order = [owner(step) for step in STEPS]

    ld_p = pltpu.make_async_copy(p_hbm, p_v, load_sem.at[0])
    ld_b = pltpu.make_async_copy(b_hbm, b_v, load_sem.at[1])
    ld_x = pltpu.make_async_copy(xt_hbm, x_v, load_sem.at[2])
    ld_mod = pltpu.make_async_copy(mod_hbm, mod_v, load_sem.at[3])
    ld_gain = pltpu.make_async_copy(gain_hbm, gain_v, load_sem.at[4])
    ld_w = [pltpu.make_async_copy(w_hbm.at[j], w_v.at[j], load_sem.at[5 + j]) for j in range(3)]
    ld_scalars = [
        pltpu.make_async_copy(src, dst, load_sem.at[8 + i])
        for i, (src, dst) in enumerate(
            ((crossing_hbm, crossing), (lengths_hbm, lengths), (steps_hbm, steps))
        )
    ]
    ld_cache = pltpu.make_async_copy(cache_hbm, own_cache, load_sem.at[11])
    st_cache = pltpu.make_async_copy(own_cache, cache_out, load_sem.at[11])
    for copy in [ld_x] + ld_scalars + [ld_p, ld_b, ld_mod, ld_gain] + ld_w + [ld_cache]:
        copy.start()

    barrier = pltpu.get_barrier_semaphore()

    def greet(k, carry):
        pl.semaphore_signal(barrier, inc=1, device_id={"seq": lax.rem(s + k, n)}, device_id_type=MESH)
        return carry

    for other in range(4):
        pl.semaphore_signal(
            barrier, inc=1, device_id={"expert": 1 - e, "group": other}, device_id_type=MESH
        )
    lax.fori_loop(1, n, greet, 0)

    @pl.when(e == 1)
    def _():
        pl.semaphore_signal(barrier, inc=1, device_id={"group": 2 * half + 1 - core}, device_id_type=MESH)

    def z_copy(src_group, dst_group):
        return pltpu.make_async_remote_copy(
            src_ref=xt_hbm,
            dst_ref=zin.at[src_group],
            send_sem=zsend.at[dst_group],
            recv_sem=zrecv.at[src_group],
            device_id={"expert": 1, "group": dst_group},
            device_id_type=MESH,
        )

    def cache_copy(src_half, dst_half):
        return pltpu.make_async_remote_copy(
            src_ref=cache_hbm,
            dst_ref=land.at[2 * src_half + core],
            send_sem=csend.at[dst_half],
            recv_sem=crecv.at[src_half],
            device_id={"expert": 1, "group": 2 * dst_half + core},
            device_id_type=MESH,
        )

    def forward_copy(src_half, src_core):
        return pltpu.make_async_remote_copy(
            src_ref=land.at[2 * src_half + src_core],
            dst_ref=land.at[2 * src_half + src_core],
            send_sem=fsend.at[src_half],
            recv_sem=frecv.at[src_half],
            device_id={"expert": 1, "group": 2 * half + 1 - core},
            device_id_type=MESH,
        )

    def x_copy(peer, slot):
        return pltpu.make_async_remote_copy(
            src_ref=xall.at[slot],
            dst_ref=xall.at[slot],
            send_sem=xsend,
            recv_sem=xrecv,
            device_id={"seq": peer},
            device_id_type=MESH,
        )

    def x_all():
        return pltpu.make_async_remote_copy(
            src_ref=xall.at[pl.ds(0, n - 1)],
            dst_ref=xall.at[pl.ds(0, n - 1)],
            send_sem=xsend,
            recv_sem=xrecv,
            device_id={"seq": lax.rem(s + 1, n)},
            device_id_type=MESH,
        )

    def x_start(k, carry):
        x_copy(lax.rem(s + k, n), s).start()
        return carry

    ld_x.wait()
    pl.semaphore_wait(barrier, n - 1 + 4 + e)

    @pl.when(e == 0)
    def _():
        for dst in range(4):
            z_copy(g, dst).start()
        xall[s] = x_v[...]
        lax.fori_loop(1, n, x_start, 0)
        for dst in range(2):
            cache_copy(half, dst).start()

    for copy in ld_scalars:
        copy.wait()
    hit0 = crossing[0, 1] == g
    hit1 = crossing[1, 1] == g
    arrived = jnp.logical_and(e == 1, jnp.logical_or(hit0, hit1))
    left = jnp.logical_and(e == 0, jnp.logical_or(crossing[0, 0] == g, crossing[1, 0] == g))
    source = jnp.where(hit0, crossing[0, 0], jnp.where(hit1, crossing[1, 0], 0))
    step_now = jnp.where(arrived, steps[0, source], steps[e, g])
    length = jnp.where(left, 0, jnp.where(arrived, lengths[0, source], lengths[e, g]))

    ld_p.wait()
    ld_b.wait()
    p_mean = jnp.mean(p_v[...].astype(F32), axis=1, keepdims=True)
    b_mean = jnp.mean(b_v[...], axis=1, keepdims=True)
    ld_mod.wait()
    part = 1024
    tail_row = lax.broadcasted_iota(jnp.int32, (16, part), 0)
    for i in range(width // part):
        cols = pl.ds(i * part, part)
        modulate = mod_v[step_now, :, cols]
        scale = 1.0 + modulate[1:2, :]
        shift = modulate[0:1, :]
        top = (p_v[:, cols].astype(F32) - p_mean) * scale
        bias = (b_v[:, cols] - b_mean) * scale
        bottom = jnp.where(
            tail_row == 0,
            jnp.broadcast_to(bias, (16, part)),
            jnp.where(tail_row == 1, jnp.broadcast_to(shift, (16, part)), 0.0),
        )
        hi, lo = split(top)
        a2[0:64, cols] = hi
        a2[ROWS : ROWS + 64, cols] = lo
        hi, lo = split(bottom)
        a2[64:ROWS, cols] = hi
        a2[ROWS + 64 : 2 * ROWS, cols] = lo

    def project(j):
        raw = dot(a2[...], w_v[j])
        total = raw[0:ROWS, :] + raw[ROWS : 2 * ROWS, :]
        m_v[j, 0:ROWS, :] = total
        return total

    ld_w[0].wait()
    m_q = project(0)
    ld_w[1].wait()
    m_k = project(1)

    gram_q = gram(m_q)
    gram_k = gram(m_k)
    at_row = lax.broadcasted_iota(jnp.int32, (64, 64), 0)
    at_col = lax.broadcasted_iota(jnp.int32, (64, 64), 1)
    core_q = gram_q[0:64, 0:64]
    core_k = gram_k[0:64, 0:64]
    both = jnp.where(at_col < at_row, 2.0 * core_q, jnp.where(at_col == at_row, core_q, 2.0 * core_k))
    gbuf[...] = jnp.zeros_like(gbuf)
    gbuf[0:32, 0:64] = both[0:32, :]
    gbuf[0:32, 64:128] = both[32:64, :]
    for at, values in enumerate((gram_q, gram_k)):
        gbuf[32:34, at * 64 : at * 64 + 64] = values[64:66, 0:64]
        gbuf[35 + 2 * at : 37 + 2 * at, 0:16] = values[64:66, 64:80]
    gbuf[34:35, 0:64] = jnp.sum(jnp.where(at_col == at_row, core_k, 0.0), axis=0, keepdims=True)

    def g_copy(peer, slot):
        return pltpu.make_async_remote_copy(
            src_ref=gbuf,
            dst_ref=g_in.at[slot],
            send_sem=gsend,
            recv_sem=grecv,
            device_id={"seq": peer},
            device_id_type=MESH,
        )

    def g_all():
        return pltpu.make_async_remote_copy(
            src_ref=g_in.at[pl.ds(0, n - 1)],
            dst_ref=g_in.at[pl.ds(0, n - 1)],
            send_sem=gsend,
            recv_sem=grecv,
            device_id={"seq": lax.rem(s + 1, n)},
            device_id_type=MESH,
        )

    def g_start(k, carry):
        g_copy(lax.rem(s + k, n), s).start()
        return carry

    lax.fori_loop(1, n, g_start, 0)

    @pl.when(e == 1)
    def _():
        for src in range(4):
            z_copy(src, 0).wait_recv()
        xall[s] = jnp.where(arrived, zin[source], x_v[...])
        lax.fori_loop(1, n, x_start, 0)

    g_in[s] = gbuf[...]

    for i in range(width // part):
        cols = pl.ds(i * part, part)
        hi, lo = split(p_v[:, cols].astype(F32) - p_mean)
        c2[0:64, cols] = hi
        c2[ROWS : ROWS + 64, cols] = lo
        bias = jnp.broadcast_to(b_v[:, cols] - b_mean, (16, part))
        hi, lo = split(jnp.where(tail_row == 0, bias, 0.0))
        c2[64:ROWS, cols] = hi
        c2[ROWS + 64 : 2 * ROWS, cols] = lo
    var_gram = (
        dot_nt(c2[0:ROWS, :], c2[0:ROWS, :])
        + dot_nt(c2[0:ROWS, :], c2[ROWS : 2 * ROWS, :])
        + dot_nt(c2[ROWS : 2 * ROWS, :], c2[0:ROWS, :])
    ) * (1.0 / width)

    ld_w[2].wait()
    project(2)

    ld_gain.wait()
    for j in range(3):
        m_v[j, ROWS:128, :] = jnp.zeros((128 - ROWS, 256), F32)
        full = m_v[j]
        if j < 2:
            full = full * gain_v[j : j + 1, :]
        flipped = full.T
        hi, lo = split(flipped)
        mt2[j * 256 : (j + 1) * 256, 0:128] = hi
        mt2[j * 256 : (j + 1) * 256, 128:256] = lo
        mtf[j] = flipped

    first16 = lax.broadcasted_iota(jnp.int32, (16, tokens), 0)
    first128 = lax.broadcasted_iota(jnp.int32, (128, tokens), 0)
    one16 = jnp.where(first16 == 0, 1.0, 0.0).astype(BF)
    one128 = jnp.where(first128 == 0, 1.0, 0.0).astype(BF)
    for h in range(2):
        qaug[h, 128:256, :] = one128
        vaug[h, 128:144, :] = one16
    key_at = lax.broadcasted_iota(jnp.int32, (128, 128), 0)
    for i in range(n):
        masks = jnp.where(key_at + order[i] * 128 >= length, MASKED, 0.0).astype(BF)
        for h in range(2):
            kaug[h, i * 128 : (i + 1) * 128, 128:256] = masks

    x_all().wait_recv()
    tail64 = lax.broadcasted_iota(jnp.int32, (64, 128), 0)
    ones_row = jnp.where(tail64 == 0, 1.0, 0.0).astype(BF)
    for i in range(n):
        cols = slice(i * 128, (i + 1) * 128)
        rows = xall[order[i]]
        z2[0:64, cols] = rows
        z2[128:192, cols] = rows
        z2[64:128, cols] = ones_row
        z2[192:256, cols] = ones_row

    x64 = z2[0:64, :]
    z80 = z2[0:ROWS, :]
    hi, lo = split(var_gram)
    t = dot(hi, z80) + dot(lo, z80)
    var = jnp.maximum(jnp.sum(t * z80.astype(F32), axis=0, keepdims=True), 0.0)
    rstd = lax.rsqrt(var + EPS)

    piece = 512
    for i in range(tokens // piece):
        cols = slice(i * piece, (i + 1) * piece)
        v_t = (dot(mt2[512:768, :], z2[:, cols]) * rstd[:, cols] + mtf[2, :, 65:66]).astype(BF)
        for h in range(2):
            vaug[h, 0:128, cols] = v_t[h * 128 : (h + 1) * 128, :]

    g_all().wait_recv()
    packed = g_in[0]
    for src in range(1, n):
        packed = packed + g_in[src]
    both = jnp.concatenate([packed[0:32, 0:64], packed[0:32, 64:128]], axis=0)
    lower = jnp.where(at_col <= at_row, both, 0.0)
    diagonal = jnp.where(at_col == at_row, jnp.broadcast_to(packed[34:35, 0:64], (64, 64)), 0.0)
    upper = jnp.where(at_col > at_row, both, diagonal)
    tail16 = lax.broadcasted_iota(jnp.int32, (16, 64), 0)
    linear = jnp.zeros((16, 64), F32)
    for at, row in enumerate(
        (packed[32:33, 0:64], packed[33:34, 0:64], packed[32:33, 64:128], packed[33:34, 64:128])
    ):
        linear = jnp.where(tail16 == at, jnp.broadcast_to(row, (16, 64)), linear)
    hi, lo = split(jnp.concatenate([lower, upper, linear], axis=0))
    t = dot(hi, x64) + dot(lo, x64)
    xf = x64.astype(F32)
    scales = []
    for j in range(2):
        quad = jnp.sum(t[j * 64 : j * 64 + 64, :] * xf, axis=0, keepdims=True)
        by_bias = t[128 + 2 * j : 129 + 2 * j, :]
        by_shift = t[129 + 2 * j : 130 + 2 * j, :]
        at = 35 + 2 * j
        total = (
            rstd * rstd * (quad + 2.0 * by_bias + packed[at : at + 1, 0:1])
            + 2.0 * rstd * (by_shift + packed[at : at + 1, 1:2])
            + packed[at + 1 : at + 2, 1:2]
        )
        scales.append(lax.rsqrt(jnp.maximum(total, 0.0) * (1.0 / (n * 256)) + EPS))
    r_q = scales[0] * (LOG2E / HD**0.5)
    r_k = scales[1]

    q_u = r_q * rstd
    k_u = r_k * rstd
    for i in range(tokens // piece):
        cols = slice(i * piece, (i + 1) * piece)
        raw = dot(mt2[0:512, :], z2[:, cols])
        q_t = (raw[0:256, :] * q_u[:, cols] + mtf[0, :, 65:66] * r_q[:, cols]).astype(BF)
        k_t = raw[256:512, :] * k_u[:, cols] + mtf[1, :, 65:66] * r_k[:, cols]
        for h in range(2):
            rows = slice(h * 128, (h + 1) * 128)
            qaug[h, 0:128, cols] = q_t[rows, :]
            kaug[h, cols, 0:128] = k_t[rows, :].T.astype(BF)

    blocks = tokens // QB

    def o_copy(block, side, h, peer, src):
        return pltpu.make_async_remote_copy(
            src_ref=ostage.at[h, block, pl.ds(side * 128, 128)],
            dst_ref=out_hbm.at[:, pl.ds(pl.multiple_of(src * 256 + h * 128, 128), 128)],
            send_sem=osend,
            recv_sem=orecv,
            device_id={"seq": peer},
            device_id_type=MESH,
        )

    def o_all():
        return pltpu.make_async_remote_copy(
            src_ref=out_hbm.at[:, pl.ds(0, (n - 1) * 256)],
            dst_ref=out_hbm.at[:, pl.ds(0, (n - 1) * 256)],
            send_sem=osend,
            recv_sem=orecv,
            device_id={"seq": lax.rem(s + 1, n)},
            device_id_type=MESH,
        )

    def own_copy(h):
        return pltpu.make_async_copy(
            ostage.at[h, blocks - 1, pl.ds((OWNERS - 1) * 128, 128)],
            out_hbm.at[:, pl.ds(pl.multiple_of(s * 256 + h * 128, 128), 128)],
            load_sem.at[h],
        )

    def block_owner(block, side):
        return owner([pick(block, [STEPS[b * OWNERS + side][a] for b in range(blocks)]) for a in range(2)])

    def send(block, h):
        for side in range(OWNERS - 1):
            o_copy(block, side, h, block_owner(block, side), s).start()

        @pl.when(block < blocks - 1)
        def _():
            o_copy(block, OWNERS - 1, h, block_owner(block, OWNERS - 1), s).start()

        @pl.when(block == blocks - 1)
        def _():
            own_copy(h).start()

    def unit(block, h, now, top, next_block, next_h, later):
        query = qaug[next_h, :, pl.ds(pl.multiple_of(next_block * QB, QB), QB)]
        next_top = jnp.full((8, QB), -3e38, F32)
        total = jnp.zeros((144, QB), F32)
        for c in range(tokens // KB):
            rows = slice(c * KB, (c + 1) * KB)
            score = dot(kaug[next_h, rows, :], query)
            later[rows, :] = score
            next_top = jnp.maximum(next_top, jnp.max(score.reshape(KB // 8, 8, QB), axis=0))
            weight = jnp.exp2(now[rows, :] - top).astype(BF)
            total = total + dot(vaug[h, :, rows], weight)
        row = lax.broadcasted_iota(jnp.int32, (1, 128), 1)
        live = [row + block_owner(block, side) * 128 < length for side in range(OWNERS)]
        inverse = 1.0 / total[128:129, :]
        inverse = jnp.concatenate(
            [jnp.where(live[a], inverse[:, a * 128 : (a + 1) * 128], 0.0) for a in range(OWNERS)], axis=1
        )
        ostage[h, block] = (total[0:128, :] * inverse).T.astype(BF)
        return jnp.max(next_top, axis=0, keepdims=True)

    def attend(block, top):
        top = unit(block, 0, s_a, top, block, 1, s_b)
        send(block, 0)
        top = unit(block, 1, s_b, top, lax.rem(block + 1, blocks), 0, s_a)
        send(block, 1)

        @pl.when(jnp.logical_and(e == 1, block == blocks // 2))
        def _():
            for src in range(2):
                cache_copy(src, 0).wait_recv()
                forward_copy(src, core).start()

        return top

    first_top = jnp.full((8, QB), -3e38, F32)
    for c in range(tokens // KB):
        rows = slice(c * KB, (c + 1) * KB)
        score = dot(kaug[0, rows, :], qaug[0, :, 0:QB])
        s_a[rows, :] = score
        first_top = jnp.maximum(first_top, jnp.max(score.reshape(KB // 8, 8, QB), axis=0))
    lax.fori_loop(0, blocks, attend, jnp.max(first_top, axis=0, keepdims=True))

    ld_cache.wait()
    height = own_cache.shape[0] // 8

    @pl.when(e == 1)
    def _():
        for src in range(2):
            forward_copy(src, core).wait_send()
            forward_copy(src, 1 - core).wait_recv()

        def choose(i, carry):
            rows = pl.ds(i * height, height)
            own_cache[rows] = jnp.where(arrived, land[source, rows], own_cache[rows])
            return carry

        lax.fori_loop(0, 8, choose, 0)

    @pl.when(e == 0)
    def _():
        for dst in range(4):
            z_copy(g, dst).wait_send()
        for dst in range(2):
            cache_copy(half, dst).wait_send()

        def choose(i, carry):
            rows = pl.ds(i * height, height)
            kept = own_cache[rows]
            own_cache[rows] = jnp.where(left, jnp.zeros_like(kept), kept)
            return carry

        lax.fori_loop(0, 8, choose, 0)

    st_cache.start()
    x_all().wait_send()
    g_all().wait_send()
    o_all().wait_send()
    for h in range(2):
        own_copy(h).wait()
    st_cache.wait()
    o_all().wait_recv()


def place(raw, cache, out, cache_out, rows_v, cache_v, sem):
    parts = 4
    reads = []
    writes = []
    for at, (src, mid, dst) in enumerate(((raw, rows_v, out), (cache, cache_v, cache_out))):
        height = src.shape[0] // parts
        for i in range(parts):
            rows = pl.ds(i * height, height)
            reads.append(pltpu.make_async_copy(src.at[rows], mid.at[rows], sem.at[0, at, i]))
            writes.append(pltpu.make_async_copy(mid.at[rows], dst.at[rows], sem.at[1, at, i]))
    for copy in reads:
        copy.start()
    for read, write in zip(reads, writes):
        read.wait()
        write.start()
    for copy in writes:
        copy.wait()


def shards(
    n,
    latent,
    text_cache,
    patch_weight,
    patch_bias,
    qkv_weight,
    qk_gain,
    modulation,
    step_index,
    lengths,
    crossing,
):
    tokens = n * 128
    width = qkv_weight.shape[1]
    xt = latent[0, 0].T
    w3 = jnp.transpose(qkv_weight[0], (1, 0, 2))
    cache = text_cache[0, 0]
    hbm = pl.BlockSpec(memory_space=pl.ANY)
    dma = pltpu.SemaphoreType.DMA
    raw, chosen = pl.pallas_call(
        functools.partial(kernel, n),
        out_shape=(
            jax.ShapeDtypeStruct((128, n * 256), BF),
            jax.ShapeDtypeStruct(cache.shape, BF),
        ),
        in_specs=[hbm] * 10,
        out_specs=(hbm, hbm),
        scratch_shapes=[
            pltpu.SMEM((2, 2), jnp.int32),
            pltpu.SMEM((2, 4), jnp.int32),
            pltpu.SMEM((2, 4), jnp.int32),
            pltpu.VMEM((64, 128), BF),
            pltpu.VMEM((1, width), F32),
            pltpu.VMEM((2, 256), F32),
            pltpu.VMEM((64, width), BF),
            pltpu.VMEM(modulation.shape[1:], F32),
            pltpu.VMEM((3, width, 256), BF),
            pltpu.VMEM((2 * ROWS, width), BF),
            pltpu.VMEM((2 * ROWS, width), BF),
            pltpu.VMEM((4, 64, 128), BF),
            pltpu.VMEM((n, 64, 128), BF),
            pltpu.VMEM((3, 128, 256), F32),
            pltpu.VMEM((PACKED, 128), F32),
            pltpu.VMEM((n, PACKED, 128), F32),
            pltpu.VMEM((256, tokens), BF),
            pltpu.VMEM((768, 256), BF),
            pltpu.VMEM((3, 256, 128), F32),
            pltpu.VMEM((2, 256, tokens), BF),
            pltpu.VMEM((2, tokens, 256), BF),
            pltpu.VMEM((2, 144, tokens), BF),
            pltpu.VMEM((tokens, QB), F32),
            pltpu.VMEM((tokens, QB), F32),
            pltpu.VMEM((2, tokens // QB, QB, 128), BF),
            pltpu.VMEM(cache.shape, BF),
            pltpu.VMEM((4,) + cache.shape, BF),
            dma((12,)),
            dma((4,)),
            dma((4,)),
            dma((2,)),
            dma((2,)),
            dma((2,)),
            dma((2,)),
            dma,
            dma,
            dma,
            dma,
            dma,
            dma,
        ],
        compiler_params=pltpu.CompilerParams(
            collective_id=0, has_side_effects=True, vmem_limit_bytes=58 * 1024 * 1024
        ),
    )(
        crossing,
        lengths,
        step_index,
        xt,
        patch_bias,
        qk_gain[0],
        patch_weight[0],
        modulation[0],
        w3,
        cache,
    )
    attended, cache_after = pl.pallas_call(
        place,
        out_shape=(
            jax.ShapeDtypeStruct(raw.shape, BF),
            jax.ShapeDtypeStruct(cache.shape, BF),
        ),
        in_specs=[hbm] * 2,
        out_specs=(hbm, hbm),
        scratch_shapes=[
            pltpu.VMEM(raw.shape, BF),
            pltpu.VMEM(cache.shape, BF),
            dma((2, 2, 4)),
        ],
    )(raw, chosen)
    return (attended[None, None], cache_after[None, None])


def solution(mesh):
    in_specs = (
        P("expert", "group", "seq", None),
        P("expert", "group", None, "seq", None),
        P("expert", None, None),
        P("expert", None),
        P("expert", None, None, "seq"),
        P("expert", None, "seq"),
        P("expert", None, None, None),
        P(),
        P(),
        P(),
    )
    out_specs = (P("expert", "group", "seq", None), P("expert", "group", None, "seq", None))
    return jax.shard_map(
        functools.partial(shards, mesh.shape["seq"]),
        mesh=mesh,
        in_specs=in_specs,
        out_specs=out_specs,
        check_vma=False,
    )
```

```python
import functools

import jax
import jax.numpy as jnp
from jax import lax
from jax.experimental import pallas as pl
from jax.experimental.pallas import tpu as pltpu
from jax.sharding import PartitionSpec as P

HD = 128
EPS = 1e-06
MASKED = -1e30
LOG2E = 1.4426950408889634
BF = jnp.bfloat16
F32 = jnp.float32
MESH = pl.DeviceIdType.MESH
ROWS = 80
PACKED = 40
SIDE = 4
QB = 512
KB = 256
OWNERS = QB // 128
STEPS = (
    ((2, 2), (1, 1), (3, 3), (2, 0))
    + ((0, 2), (1, 2), (3, 1), (2, 3))
    + ((1, 3), (3, 2), (2, 1), (0, 3))
    + ((1, 0), (3, 0), (0, 1), (0, 0))
)


def dot(a, b):
    return jnp.dot(a, b, preferred_element_type=F32)


def dot_nt(a, b):
    return lax.dot_general(a, b, (((1,), (1,)), ((), ())), preferred_element_type=F32)


def split(a):
    hi = a.astype(BF)
    lo = (a - hi.astype(F32)).astype(BF)
    return hi, lo


def gram(a):
    hi, lo = split(a)
    return dot_nt(hi, hi) + dot_nt(hi, lo) + dot_nt(lo, hi)


def kernel(
    n,
    crossing_hbm,
    lengths_hbm,
    steps_hbm,
    xt_hbm,
    b_hbm,
    gain_hbm,
    p_hbm,
    mod_hbm,
    w_hbm,
    cache_hbm,
    out_hbm,
    cache_out,
    crossing,
    lengths,
    steps,
    x_v,
    b_v,
    gain_v,
    p_v,
    mod_v,
    w_v,
    a2,
    c2,
    zin,
    xall,
    m_v,
    gbuf,
    g_in,
    stat,
    z2,
    mt2,
    mtf,
    qaug,
    kaug,
    vaug,
    s_a,
    s_b,
    ostage,
    own_cache,
    land,
    load_sem,
    zsend,
    zrecv,
    csend,
    crecv,
    fsend,
    frecv,
    xsend,
    xrecv,
    gsend,
    grecv,
    osend,
    orecv,
):
    e = lax.axis_index("expert")
    g = lax.axis_index("group")
    s = lax.axis_index("seq")
    half = lax.div(g, 2)
    core = lax.rem(g, 2)
    my_x = lax.div(s, SIDE)
    my_y = lax.rem(s, SIDE)
    tokens = n * 128
    width = p_v.shape[1]

    def owner(step):
        return lax.rem(my_x + step[0], SIDE) * SIDE + lax.rem(my_y + step[1], SIDE)

    order = [owner(step) for step in STEPS]

    ld_p = pltpu.make_async_copy(p_hbm, p_v, load_sem.at[0])
    ld_b = pltpu.make_async_copy(b_hbm, b_v, load_sem.at[1])
    ld_x = pltpu.make_async_copy(xt_hbm, x_v, load_sem.at[2])
    ld_mod = pltpu.make_async_copy(mod_hbm, mod_v, load_sem.at[3])
    ld_gain = pltpu.make_async_copy(gain_hbm, gain_v, load_sem.at[4])
    ld_w = [pltpu.make_async_copy(w_hbm.at[j], w_v.at[j], load_sem.at[5 + j]) for j in range(3)]
    ld_scalars = [
        pltpu.make_async_copy(src, dst, load_sem.at[8 + i])
        for i, (src, dst) in enumerate(
            ((crossing_hbm, crossing), (lengths_hbm, lengths), (steps_hbm, steps))
        )
    ]
    ld_cache = pltpu.make_async_copy(cache_hbm, own_cache, load_sem.at[11])
    st_cache = pltpu.make_async_copy(own_cache, cache_out, load_sem.at[11])
    for copy in [ld_x] + ld_scalars + [ld_p, ld_b, ld_mod, ld_gain, ld_w[0], ld_w[1]]:
        copy.start()

    barrier = pltpu.get_barrier_semaphore()

    def greet(k, carry):
        pl.semaphore_signal(barrier, inc=1, device_id={"seq": lax.rem(s + k, n)}, device_id_type=MESH)
        return carry

    for other in range(4):
        pl.semaphore_signal(
            barrier, inc=1, device_id={"expert": 1 - e, "group": other}, device_id_type=MESH
        )
    lax.fori_loop(1, n, greet, 0)

    @pl.when(e == 1)
    def _():
        pl.semaphore_signal(barrier, inc=1, device_id={"group": 2 * half + 1 - core}, device_id_type=MESH)

    def z_copy(src_group, dst_group):
        return pltpu.make_async_remote_copy(
            src_ref=x_v,
            dst_ref=zin.at[src_group],
            send_sem=zsend.at[dst_group],
            recv_sem=zrecv.at[src_group],
            device_id={"expert": 1, "group": dst_group},
            device_id_type=MESH,
        )

    def cache_copy(src_half, dst_half):
        return pltpu.make_async_remote_copy(
            src_ref=cache_hbm,
            dst_ref=land.at[2 * src_half + core],
            send_sem=csend.at[dst_half],
            recv_sem=crecv.at[src_half],
            device_id={"expert": 1, "group": 2 * dst_half + core},
            device_id_type=MESH,
        )

    def forward_copy(src_half, src_core):
        return pltpu.make_async_remote_copy(
            src_ref=land.at[2 * src_half + src_core],
            dst_ref=land.at[2 * src_half + src_core],
            send_sem=fsend.at[src_half],
            recv_sem=frecv.at[src_half],
            device_id={"expert": 1, "group": 2 * half + 1 - core},
            device_id_type=MESH,
        )

    def x_copy(peer, slot):
        return pltpu.make_async_remote_copy(
            src_ref=xall.at[slot],
            dst_ref=xall.at[slot],
            send_sem=xsend,
            recv_sem=xrecv,
            device_id={"seq": peer},
            device_id_type=MESH,
        )

    def x_all():
        return pltpu.make_async_remote_copy(
            src_ref=xall.at[pl.ds(0, n - 1)],
            dst_ref=xall.at[pl.ds(0, n - 1)],
            send_sem=xsend,
            recv_sem=xrecv,
            device_id={"seq": lax.rem(s + 1, n)},
            device_id_type=MESH,
        )

    def x_start(k, carry):
        x_copy(lax.rem(s + k, n), s).start()
        return carry

    ld_x.wait()
    pl.semaphore_wait(barrier, n - 1 + 4 + e)

    @pl.when(e == 0)
    def _():
        for dst in range(4):
            z_copy(g, dst).start()
        xall[s] = x_v[...]
        lax.fori_loop(1, n, x_start, 0)
        for dst in range(2):
            cache_copy(half, dst).start()

    for copy in ld_scalars:
        copy.wait()
    hit0 = crossing[0, 1] == g
    hit1 = crossing[1, 1] == g
    arrived = jnp.logical_and(e == 1, jnp.logical_or(hit0, hit1))
    left = jnp.logical_and(e == 0, jnp.logical_or(crossing[0, 0] == g, crossing[1, 0] == g))
    source = jnp.where(hit0, crossing[0, 0], jnp.where(hit1, crossing[1, 0], 0))
    step_now = jnp.where(arrived, steps[0, source], steps[e, g])
    length = jnp.where(left, 0, jnp.where(arrived, lengths[0, source], lengths[e, g]))

    ld_p.wait()
    ld_b.wait()
    p_mean = jnp.mean(p_v[...].astype(F32), axis=1, keepdims=True)
    b_mean = jnp.mean(b_v[...], axis=1, keepdims=True)
    ld_mod.wait()
    part = 1024
    tail_row = lax.broadcasted_iota(jnp.int32, (16, part), 0)
    for i in range(width // part):
        cols = pl.ds(i * part, part)
        modulate = mod_v[step_now, :, cols]
        scale = 1.0 + modulate[1:2, :]
        shift = modulate[0:1, :]
        top = (p_v[:, cols].astype(F32) - p_mean) * scale
        bias = (b_v[:, cols] - b_mean) * scale
        bottom = jnp.where(
            tail_row == 0,
            jnp.broadcast_to(bias, (16, part)),
            jnp.where(tail_row == 1, jnp.broadcast_to(shift, (16, part)), 0.0),
        )
        hi, lo = split(top)
        a2[0:64, cols] = hi
        a2[ROWS : ROWS + 64, cols] = lo
        hi, lo = split(bottom)
        a2[64:ROWS, cols] = hi
        a2[ROWS + 64 : 2 * ROWS, cols] = lo

    def project(j):
        raw = dot(a2[...], w_v[j])
        total = raw[0:ROWS, :] + raw[ROWS : 2 * ROWS, :]
        m_v[j, 0:ROWS, :] = total
        return total

    ld_w[0].wait()
    ld_w[2].start()
    ld_cache.start()
    m_q = project(0)
    ld_w[1].wait()
    m_k = project(1)

    gram_q = gram(m_q)
    gram_k = gram(m_k)
    at_row = lax.broadcasted_iota(jnp.int32, (64, 64), 0)
    at_col = lax.broadcasted_iota(jnp.int32, (64, 64), 1)
    core_q = gram_q[0:64, 0:64]
    core_k = gram_k[0:64, 0:64]
    both = jnp.where(at_col < at_row, 2.0 * core_q, jnp.where(at_col == at_row, core_q, 2.0 * core_k))
    gbuf[...] = jnp.zeros_like(gbuf)
    gbuf[0:32, 0:64] = both[0:32, :]
    gbuf[0:32, 64:128] = both[32:64, :]
    for at, values in enumerate((gram_q, gram_k)):
        gbuf[32:34, at * 64 : at * 64 + 64] = values[64:66, 0:64]
        gbuf[35 + 2 * at : 37 + 2 * at, 0:16] = values[64:66, 64:80]
    gbuf[34:35, 0:64] = jnp.sum(jnp.where(at_col == at_row, core_k, 0.0), axis=0, keepdims=True)

    def g_copy(peer, slot):
        return pltpu.make_async_remote_copy(
            src_ref=gbuf,
            dst_ref=g_in.at[slot],
            send_sem=gsend,
            recv_sem=grecv,
            device_id={"seq": peer},
            device_id_type=MESH,
        )

    def g_all():
        return pltpu.make_async_remote_copy(
            src_ref=g_in.at[pl.ds(0, n - 1)],
            dst_ref=g_in.at[pl.ds(0, n - 1)],
            send_sem=gsend,
            recv_sem=grecv,
            device_id={"seq": lax.rem(s + 1, n)},
            device_id_type=MESH,
        )

    def g_start(k, carry):
        g_copy(lax.rem(s + k, n), s).start()
        return carry

    lax.fori_loop(1, n, g_start, 0)

    @pl.when(e == 1)
    def _():
        for src in range(4):
            z_copy(src, 0).wait_recv()
        xall[s] = jnp.where(arrived, zin[source], x_v[...])
        lax.fori_loop(1, n, x_start, 0)

    g_in[s] = gbuf[...]

    for i in range(width // part):
        cols = pl.ds(i * part, part)
        hi, lo = split(p_v[:, cols].astype(F32) - p_mean)
        c2[0:64, cols] = hi
        c2[ROWS : ROWS + 64, cols] = lo
        bias = jnp.broadcast_to(b_v[:, cols] - b_mean, (16, part))
        hi, lo = split(jnp.where(tail_row == 0, bias, 0.0))
        c2[64:ROWS, cols] = hi
        c2[ROWS + 64 : 2 * ROWS, cols] = lo
    var_gram = (
        dot_nt(c2[0:ROWS, :], c2[0:ROWS, :])
        + dot_nt(c2[0:ROWS, :], c2[ROWS : 2 * ROWS, :])
        + dot_nt(c2[ROWS : 2 * ROWS, :], c2[0:ROWS, :])
    ) * (1.0 / width)

    ld_w[2].wait()
    project(2)

    ld_gain.wait()
    for j in range(3):
        m_v[j, ROWS:128, :] = jnp.zeros((128 - ROWS, 256), F32)
        full = m_v[j]
        if j < 2:
            full = full * gain_v[j : j + 1, :]
        flipped = full.T
        hi, lo = split(flipped)
        for h in range(2):
            at = 512 + h * 128 if j == 2 else h * 256 + j * 128
            rows = slice(h * 128, (h + 1) * 128)
            mt2[at : at + 128, 0:128] = hi[rows, :]
            mt2[at : at + 128, 128:256] = lo[rows, :]
        mtf[j] = flipped

    first16 = lax.broadcasted_iota(jnp.int32, (16, tokens), 0)
    first128 = lax.broadcasted_iota(jnp.int32, (128, tokens), 0)
    one16 = jnp.where(first16 == 0, 1.0, 0.0).astype(BF)
    one128 = jnp.where(first128 == 0, 1.0, 0.0).astype(BF)
    for h in range(2):
        qaug[h, 128:256, :] = one128
        vaug[h, 128:144, :] = one16
    key_at = lax.broadcasted_iota(jnp.int32, (128, 128), 0)
    for i in range(n):
        masks = jnp.where(key_at + order[i] * 128 >= length, MASKED, 0.0).astype(BF)
        for h in range(2):
            kaug[h, i * 128 : (i + 1) * 128, 128:256] = masks

    tail64 = lax.broadcasted_iota(jnp.int32, (64, tokens), 0)
    ones_row = jnp.where(tail64 == 0, 1.0, 0.0).astype(BF)
    z2[64:128, :] = ones_row
    z2[192:256, :] = ones_row
    hi, lo = split(var_gram)
    stat[...] = jnp.zeros_like(stat)
    stat[0:ROWS, 0:ROWS] = hi
    stat[0:ROWS, 128 : 128 + ROWS] = lo
    g_all().wait_recv()
    packed = g_in[0]
    for src in range(1, n):
        packed = packed + g_in[src]
    both = jnp.concatenate([packed[0:32, 0:64], packed[0:32, 64:128]], axis=0)
    lower = jnp.where(at_col <= at_row, both, 0.0)
    diagonal = jnp.where(at_col == at_row, jnp.broadcast_to(packed[34:35, 0:64], (64, 64)), 0.0)
    upper = jnp.where(at_col > at_row, both, diagonal)
    tail16 = lax.broadcasted_iota(jnp.int32, (16, 64), 0)
    linear = jnp.zeros((16, 64), F32)
    for at, row in enumerate(
        (packed[32:33, 0:64], packed[33:34, 0:64], packed[32:33, 64:128], packed[33:34, 64:128])
    ):
        linear = jnp.where(tail16 == at, jnp.broadcast_to(row, (16, 64)), linear)
    hi, lo = split(jnp.concatenate([lower, upper, linear], axis=0))
    stat[ROWS : ROWS + 144, 0:64] = hi
    stat[ROWS : ROWS + 144, 128:192] = lo

    x_all().wait_recv()
    for i in range(n):
        cols = slice(i * 128, (i + 1) * 128)
        rows = xall[order[i]]
        z2[0:64, cols] = rows
        z2[128:192, cols] = rows
    t = dot(stat[...], z2[...])
    z80 = z2[0:ROWS, :].astype(F32)
    var = jnp.maximum(jnp.sum(t[0:ROWS, :] * z80, axis=0, keepdims=True), 0.0)
    rstd = lax.rsqrt(var + EPS)
    scales = []
    for j in range(2):
        base = ROWS + j * 64
        quad = jnp.sum(t[base : base + 64, :] * z80[0:64, :], axis=0, keepdims=True)
        base = ROWS + 128 + 2 * j
        by_bias = t[base : base + 1, :]
        by_shift = t[base + 1 : base + 2, :]
        at = 35 + 2 * j
        total = (
            rstd * rstd * (quad + 2.0 * by_bias + packed[at : at + 1, 0:1])
            + 2.0 * rstd * (by_shift + packed[at : at + 1, 1:2])
            + packed[at + 1 : at + 2, 1:2]
        )
        scales.append(lax.rsqrt(jnp.maximum(total, 0.0) * (1.0 / (n * 256)) + EPS))
    r_q = scales[0] * (LOG2E / HD**0.5)
    r_k = scales[1]

    q_u = r_q * rstd
    k_u = r_k * rstd
    piece = 512

    def heads(h):
        for i in range(tokens // piece):
            cols = slice(i * piece, (i + 1) * piece)
            raw = dot(mt2[h * 256 : (h + 1) * 256, :], z2[:, cols])
            rows = slice(h * 128, (h + 1) * 128)
            qaug[h, 0:128, cols] = (
                raw[0:128, :] * q_u[:, cols] + mtf[0, rows, 65:66] * r_q[:, cols]
            ).astype(BF)
            k_t = raw[128:256, :] * k_u[:, cols] + mtf[1, rows, 65:66] * r_k[:, cols]
            kaug[h, cols, 0:128] = k_t.T.astype(BF)

    heads(0)
    first_top = jnp.full((8, QB), -3e38, F32)
    for c in range(tokens // KB):
        rows = slice(c * KB, (c + 1) * KB)
        score = dot(kaug[0, rows, :], qaug[0, :, 0:QB])
        s_a[rows, :] = score
        first_top = jnp.maximum(first_top, jnp.max(score.reshape(KB // 8, 8, QB), axis=0))
    def values(h):
        for i in range(tokens // piece):
            cols = slice(i * piece, (i + 1) * piece)
            rows = slice(h * 128, (h + 1) * 128)
            raw = dot(mt2[512 + h * 128 : 640 + h * 128, :], z2[:, cols])
            vaug[h, 0:128, cols] = (raw * rstd[:, cols] + mtf[2, rows, 65:66]).astype(BF)

    blocks = tokens // QB

    def o_copy(block, side, h, peer, src):
        return pltpu.make_async_remote_copy(
            src_ref=ostage.at[h, block, pl.ds(side * 128, 128)],
            dst_ref=out_hbm.at[:, pl.ds(pl.multiple_of(src * 256 + h * 128, 128), 128)],
            send_sem=osend,
            recv_sem=orecv,
            device_id={"seq": peer},
            device_id_type=MESH,
        )

    def o_all():
        return pltpu.make_async_remote_copy(
            src_ref=out_hbm.at[:, pl.ds(0, (n - 1) * 256)],
            dst_ref=out_hbm.at[:, pl.ds(0, (n - 1) * 256)],
            send_sem=osend,
            recv_sem=orecv,
            device_id={"seq": lax.rem(s + 1, n)},
            device_id_type=MESH,
        )

    def own_copy(h):
        return pltpu.make_async_copy(
            ostage.at[h, blocks - 1, pl.ds((OWNERS - 1) * 128, 128)],
            out_hbm.at[:, pl.ds(pl.multiple_of(s * 256 + h * 128, 128), 128)],
            load_sem.at[h],
        )

    def send(block, h):
        for side in range(OWNERS - 1):
            o_copy(block, side, h, order[block * OWNERS + side], s).start()

        if block == blocks - 1:
            own_copy(h).start()
        else:
            o_copy(block, OWNERS - 1, h, order[block * OWNERS + OWNERS - 1], s).start()

    def unit(block, h, now, top, next_block, next_h, later):
        ahead = later is not None
        if ahead:
            query = qaug[next_h, :, next_block * QB : (next_block + 1) * QB]
        next_top = jnp.full((8, QB), -3e38, F32)
        total = jnp.zeros((144, QB), F32)
        for c in range(tokens // KB):
            rows = slice(c * KB, (c + 1) * KB)
            if ahead:
                score = dot(kaug[next_h, rows, :], query)
                later[rows, :] = score
                next_top = jnp.maximum(next_top, jnp.max(score.reshape(KB // 8, 8, QB), axis=0))
            weight = jnp.exp2(now[rows, :] - top).astype(BF)
            total = total + dot(vaug[h, :, rows], weight)
        row = lax.broadcasted_iota(jnp.int32, (1, 128), 1)
        live = [row + order[block * OWNERS + side] * 128 < length for side in range(OWNERS)]
        inverse = 1.0 / total[128:129, :]
        inverse = jnp.concatenate(
            [jnp.where(live[a], inverse[:, a * 128 : (a + 1) * 128], 0.0) for a in range(OWNERS)], axis=1
        )
        ostage[h, block] = (total[0:128, :] * inverse).T.astype(BF)
        return jnp.max(next_top, axis=0, keepdims=True)

    def forward():
        @pl.when(e == 1)
        def _():
            for src in range(2):
                cache_copy(src, 0).wait_recv()
                forward_copy(src, core).start()

    units = [(block, h) for h in range(2) for block in range(blocks)]
    halves = (s_a, s_b)
    values(0)
    top = jnp.max(first_top, axis=0, keepdims=True)
    for at, (block, h) in enumerate(units):
        if at == 2:
            heads(1)
        if at == blocks:
            values(1)
        if at == len(units) - 2:
            forward()
        if at + 1 < len(units):
            top = unit(block, h, halves[at % 2], top, *units[at + 1], halves[(at + 1) % 2])
        else:
            unit(block, h, halves[at % 2], top, None, None, None)
        send(block, h)

    ld_cache.wait()
    height = own_cache.shape[0] // 8

    @pl.when(e == 1)
    def _():
        for src in range(2):
            forward_copy(src, core).wait_send()
            forward_copy(src, 1 - core).wait_recv()

        def choose(i, carry):
            rows = pl.ds(i * height, height)
            own_cache[rows] = jnp.where(arrived, land[source, rows], own_cache[rows])
            return carry

        lax.fori_loop(0, 8, choose, 0)

    @pl.when(e == 0)
    def _():
        for dst in range(4):
            z_copy(g, dst).wait_send()
        for dst in range(2):
            cache_copy(half, dst).wait_send()

        def choose(i, carry):
            rows = pl.ds(i * height, height)
            kept = own_cache[rows]
            own_cache[rows] = jnp.where(left, jnp.zeros_like(kept), kept)
            return carry

        lax.fori_loop(0, 8, choose, 0)

    st_cache.start()
    x_all().wait_send()
    g_all().wait_send()
    o_all().wait_send()
    for h in range(2):
        own_copy(h).wait()
    st_cache.wait()
    o_all().wait_recv()


def place(raw, cache, out, cache_out, sem):
    parts = 4
    writes = []
    for at, (src, dst) in enumerate(((raw, out), (cache, cache_out))):
        height = src.shape[0] // parts
        for i in range(parts):
            rows = pl.ds(i * height, height)
            writes.append(pltpu.make_async_copy(src.at[rows], dst.at[rows], sem.at[at, i]))
    for copy in writes:
        copy.start()
    for copy in writes:
        copy.wait()


def shards(
    n,
    latent,
    text_cache,
    patch_weight,
    patch_bias,
    qkv_weight,
    qk_gain,
    modulation,
    step_index,
    lengths,
    crossing,
):
    tokens = n * 128
    width = qkv_weight.shape[1]
    xt = latent[0, 0].T
    w3 = jnp.transpose(qkv_weight[0], (1, 0, 2))
    cache = text_cache[0, 0]
    hbm = pl.BlockSpec(memory_space=pl.ANY)
    dma = pltpu.SemaphoreType.DMA
    raw, chosen = pl.pallas_call(
        functools.partial(kernel, n),
        out_shape=(
            pltpu.VMEM((128, n * 256), BF),
            pltpu.VMEM(cache.shape, BF),
        ),
        in_specs=[hbm] * 10,
        out_specs=(hbm, hbm),
        scratch_shapes=[
            pltpu.SMEM((2, 2), jnp.int32),
            pltpu.SMEM((2, 4), jnp.int32),
            pltpu.SMEM((2, 4), jnp.int32),
            pltpu.VMEM((64, 128), BF),
            pltpu.VMEM((1, width), F32),
            pltpu.VMEM((2, 256), F32),
            pltpu.VMEM((64, width), BF),
            pltpu.VMEM(modulation.shape[1:], F32),
            pltpu.VMEM((3, width, 256), BF),
            pltpu.VMEM((2 * ROWS, width), BF),
            pltpu.VMEM((2 * ROWS, width), BF),
            pltpu.VMEM((4, 64, 128), BF),
            pltpu.VMEM((n, 64, 128), BF),
            pltpu.VMEM((3, 128, 256), F32),
            pltpu.VMEM((PACKED, 128), F32),
            pltpu.VMEM((n, PACKED, 128), F32),
            pltpu.VMEM((ROWS + 144, 256), BF),
            pltpu.VMEM((256, tokens), BF),
            pltpu.VMEM((768, 256), BF),
            pltpu.VMEM((3, 256, 128), F32),
            pltpu.VMEM((2, 256, tokens), BF),
            pltpu.VMEM((2, tokens, 256), BF),
            pltpu.VMEM((2, 144, tokens), BF),
            pltpu.VMEM((tokens, QB), F32),
            pltpu.VMEM((tokens, QB), F32),
            pltpu.VMEM((2, tokens // QB, QB, 128), BF),
            pltpu.VMEM(cache.shape, BF),
            pltpu.VMEM((4,) + cache.shape, BF),
            dma((12,)),
            dma((4,)),
            dma((4,)),
            dma((2,)),
            dma((2,)),
            dma((2,)),
            dma((2,)),
            dma,
            dma,
            dma,
            dma,
            dma,
            dma,
        ],
        compiler_params=pltpu.CompilerParams(
            collective_id=0, has_side_effects=True, vmem_limit_bytes=58 * 1024 * 1024
        ),
    )(
        crossing,
        lengths,
        step_index,
        xt,
        patch_bias,
        qk_gain[0],
        patch_weight[0],
        modulation[0],
        w3,
        cache,
    )
    attended, cache_after = pl.pallas_call(
        place,
        out_shape=(
            jax.ShapeDtypeStruct(raw.shape, BF),
            jax.ShapeDtypeStruct(cache.shape, BF),
        ),
        in_specs=[hbm] * 2,
        out_specs=(hbm, hbm),
        scratch_shapes=[dma((2, 4))],
    )(
        pltpu.with_memory_space_constraint(raw, pltpu.VMEM),
        pltpu.with_memory_space_constraint(chosen, pltpu.VMEM),
    )
    return (attended[None, None], cache_after[None, None])


def solution(mesh):
    in_specs = (
        P("expert", "group", "seq", None),
        P("expert", "group", None, "seq", None),
        P("expert", None, None),
        P("expert", None),
        P("expert", None, None, "seq"),
        P("expert", None, "seq"),
        P("expert", None, None, None),
        P(),
        P(),
        P(),
    )
    out_specs = (P("expert", "group", "seq", None), P("expert", "group", None, "seq", None))
    return jax.shard_map(
        functools.partial(shards, mesh.shape["seq"]),
        mesh=mesh,
        in_specs=in_specs,
        out_specs=out_specs,
        check_vma=False,
    )
```

```python
import functools

import jax
import jax.numpy as jnp
from jax import lax
from jax.experimental import pallas as pl
from jax.experimental.pallas import tpu as pltpu
from jax.sharding import PartitionSpec as P

HD = 128
EPS = 1e-06
MASKED = -1e30
LOG2E = 1.4426950408889634
BF = jnp.bfloat16
F32 = jnp.float32
MESH = pl.DeviceIdType.MESH
ROWS = 80
PACKED = 48
SIDE = 4
QB = 512
KB = 256
OWNERS = QB // 128
STEPS = (
    ((2, 2), (1, 1), (3, 3), (2, 0))
    + ((0, 2), (1, 2), (3, 1), (2, 3))
    + ((1, 3), (3, 2), (2, 1), (0, 3))
    + ((1, 0), (3, 0), (0, 1), (0, 0))
)


def dot(a, b):
    return jnp.dot(a, b, preferred_element_type=F32)


def dot_nt(a, b):
    return lax.dot_general(a, b, (((1,), (1,)), ((), ())), preferred_element_type=F32)


def split(a):
    hi = a.astype(BF)
    lo = (a - hi.astype(F32)).astype(BF)
    return hi, lo


def gram(a):
    hi, lo = split(a)
    return dot_nt(hi, hi) + dot_nt(hi, lo) + dot_nt(lo, hi)


def kernel(
    n,
    crossing_hbm,
    lengths_hbm,
    steps_hbm,
    xt_hbm,
    b_hbm,
    gain_hbm,
    p_hbm,
    mod_hbm,
    w_hbm,
    cache_hbm,
    out_hbm,
    cache_out,
    crossing,
    lengths,
    steps,
    x_v,
    b_v,
    gain_v,
    p_v,
    mod_v,
    w_v,
    a2,
    c2,
    zin,
    xall,
    m_v,
    gbuf,
    rest,
    g_in,
    stat,
    z2,
    mt2,
    mtf,
    qaug,
    kaug,
    vaug,
    s_a,
    s_b,
    ostage,
    own_cache,
    land,
    load_sem,
    zsend,
    zrecv,
    csend,
    crecv,
    fsend,
    frecv,
    xsend,
    xrecv,
    gsend,
    grecv,
    osend,
    orecv,
):
    e = lax.axis_index("expert")
    g = lax.axis_index("group")
    s = lax.axis_index("seq")
    half = lax.div(g, 2)
    core = lax.rem(g, 2)
    my_x = lax.div(s, SIDE)
    my_y = lax.rem(s, SIDE)
    tokens = n * 128
    width = p_v.shape[1]

    def owner(step):
        return lax.rem(my_x + step[0], SIDE) * SIDE + lax.rem(my_y + step[1], SIDE)

    order = [owner(step) for step in STEPS]

    ld_p = pltpu.make_async_copy(p_hbm, p_v, load_sem.at[0])
    ld_b = pltpu.make_async_copy(b_hbm, b_v, load_sem.at[1])
    ld_x = pltpu.make_async_copy(xt_hbm, x_v, load_sem.at[2])
    ld_mod = pltpu.make_async_copy(mod_hbm, mod_v, load_sem.at[3])
    ld_gain = pltpu.make_async_copy(gain_hbm, gain_v, load_sem.at[4])
    ld_w = [pltpu.make_async_copy(w_hbm.at[j], w_v.at[j], load_sem.at[5 + j]) for j in range(3)]
    ld_scalars = [
        pltpu.make_async_copy(src, dst, load_sem.at[8 + i])
        for i, (src, dst) in enumerate(
            ((crossing_hbm, crossing), (lengths_hbm, lengths), (steps_hbm, steps))
        )
    ]
    ld_cache = pltpu.make_async_copy(cache_hbm, own_cache, load_sem.at[11])
    st_cache = pltpu.make_async_copy(own_cache, cache_out, load_sem.at[11])
    for copy in [ld_x] + ld_scalars + [ld_p, ld_b, ld_mod, ld_gain, ld_w[0], ld_w[1]]:
        copy.start()

    barrier = pltpu.get_barrier_semaphore()

    def greet(k, carry):
        pl.semaphore_signal(barrier, inc=1, device_id={"seq": lax.rem(s + k, n)}, device_id_type=MESH)
        return carry

    for other in range(4):
        pl.semaphore_signal(
            barrier, inc=1, device_id={"expert": 1 - e, "group": other}, device_id_type=MESH
        )
    lax.fori_loop(1, n, greet, 0)

    @pl.when(e == 1)
    def _():
        pl.semaphore_signal(barrier, inc=1, device_id={"group": 2 * half + 1 - core}, device_id_type=MESH)

    def z_copy(src_group, dst_group):
        return pltpu.make_async_remote_copy(
            src_ref=x_v,
            dst_ref=zin.at[src_group],
            send_sem=zsend.at[dst_group],
            recv_sem=zrecv.at[src_group],
            device_id={"expert": 1, "group": dst_group},
            device_id_type=MESH,
        )

    def cache_copy(src_half, dst_half):
        return pltpu.make_async_remote_copy(
            src_ref=cache_hbm,
            dst_ref=land.at[2 * src_half + core],
            send_sem=csend.at[dst_half],
            recv_sem=crecv.at[src_half],
            device_id={"expert": 1, "group": 2 * dst_half + core},
            device_id_type=MESH,
        )

    def forward_copy(src_half, src_core):
        return pltpu.make_async_remote_copy(
            src_ref=land.at[2 * src_half + src_core],
            dst_ref=land.at[2 * src_half + src_core],
            send_sem=fsend.at[src_half],
            recv_sem=frecv.at[src_half],
            device_id={"expert": 1, "group": 2 * half + 1 - core},
            device_id_type=MESH,
        )

    def x_copy(peer, slot):
        return pltpu.make_async_remote_copy(
            src_ref=xall.at[slot],
            dst_ref=xall.at[slot],
            send_sem=xsend,
            recv_sem=xrecv,
            device_id={"seq": peer},
            device_id_type=MESH,
        )

    def x_all():
        return pltpu.make_async_remote_copy(
            src_ref=xall.at[pl.ds(0, n - 1)],
            dst_ref=xall.at[pl.ds(0, n - 1)],
            send_sem=xsend,
            recv_sem=xrecv,
            device_id={"seq": lax.rem(s + 1, n)},
            device_id_type=MESH,
        )

    def x_start(k, carry):
        x_copy(lax.rem(s + k, n), s).start()
        return carry

    ld_x.wait()

    @pl.when(e == 0)
    def _():
        pl.semaphore_wait(barrier, n - 1 + 4)
        for dst in range(4):
            z_copy(g, dst).start()
        xall[s] = x_v[...]
        lax.fori_loop(1, n, x_start, 0)

    for copy in ld_scalars:
        copy.wait()
    hit0 = crossing[0, 1] == g
    hit1 = crossing[1, 1] == g
    arrived = jnp.logical_and(e == 1, jnp.logical_or(hit0, hit1))
    left = jnp.logical_and(e == 0, jnp.logical_or(crossing[0, 0] == g, crossing[1, 0] == g))
    source = jnp.where(hit0, crossing[0, 0], jnp.where(hit1, crossing[1, 0], 0))
    step_now = jnp.where(arrived, steps[0, source], steps[e, g])
    length = jnp.where(left, 0, jnp.where(arrived, lengths[0, source], lengths[e, g]))

    ld_p.wait()
    ld_b.wait()
    p_mean = jnp.mean(p_v[...].astype(F32), axis=1, keepdims=True)
    b_mean = jnp.mean(b_v[...], axis=1, keepdims=True)
    ld_mod.wait()
    part = 1024
    tail_row = lax.broadcasted_iota(jnp.int32, (16, part), 0)
    for i in range(width // part):
        cols = pl.ds(i * part, part)
        modulate = mod_v[step_now, :, cols]
        scale = 1.0 + modulate[1:2, :]
        shift = modulate[0:1, :]
        top = (p_v[:, cols].astype(F32) - p_mean) * scale
        bias = (b_v[:, cols] - b_mean) * scale
        bottom = jnp.where(
            tail_row == 0,
            jnp.broadcast_to(bias, (16, part)),
            jnp.where(tail_row == 1, jnp.broadcast_to(shift, (16, part)), 0.0),
        )
        hi, lo = split(top)
        a2[0:64, cols] = hi
        a2[ROWS : ROWS + 64, cols] = lo
        hi, lo = split(bottom)
        a2[64:ROWS, cols] = hi
        a2[ROWS + 64 : 2 * ROWS, cols] = lo

    def project(j):
        raw = dot(a2[...], w_v[j])
        total = raw[0:ROWS, :] + raw[ROWS : 2 * ROWS, :]
        m_v[j, 0:ROWS, :] = total
        return total

    ld_w[0].wait()
    ld_w[2].start()
    ld_cache.start()
    m_q = project(0)
    ld_w[1].wait()
    m_k = project(1)

    gram_q = gram(m_q)
    gram_k = gram(m_k)
    at_row = lax.broadcasted_iota(jnp.int32, (64, 64), 0)
    at_col = lax.broadcasted_iota(jnp.int32, (64, 64), 1)
    core_q = gram_q[0:64, 0:64]
    core_k = gram_k[0:64, 0:64]
    both = jnp.where(at_col < at_row, 2.0 * core_q, jnp.where(at_col > at_row, 2.0 * core_k, 0.0)).astype(BF)
    gbuf[0:32, 0:64] = both[0:32, :]
    gbuf[0:32, 64:128] = both[32:64, :]
    rest[...] = jnp.zeros_like(rest)
    for at, (values, centre) in enumerate(((gram_q, core_q), (gram_k, core_k))):
        cols = slice(at * 64, at * 64 + 64)
        rest[0:2, cols] = values[64:66, 0:64]
        rest[2:3, cols] = jnp.sum(jnp.where(at_col == at_row, centre, 0.0), axis=0, keepdims=True)
        rest[3 + 2 * at : 5 + 2 * at, 0:16] = values[64:66, 64:80]
    hi, lo = split(rest[...])
    gbuf[32:48, :] = jnp.concatenate([hi.astype(F32), lo.astype(F32)], axis=0).astype(BF)

    def g_copy(peer, slot):
        return pltpu.make_async_remote_copy(
            src_ref=gbuf,
            dst_ref=g_in.at[slot],
            send_sem=gsend,
            recv_sem=grecv,
            device_id={"seq": peer},
            device_id_type=MESH,
        )

    def g_all():
        return pltpu.make_async_remote_copy(
            src_ref=g_in.at[pl.ds(0, n - 1)],
            dst_ref=g_in.at[pl.ds(0, n - 1)],
            send_sem=gsend,
            recv_sem=grecv,
            device_id={"seq": lax.rem(s + 1, n)},
            device_id_type=MESH,
        )

    def g_start(k, carry):
        g_copy(lax.rem(s + k, n), s).start()
        return carry

    @pl.when(e == 1)
    def _():
        pl.semaphore_wait(barrier, n - 1 + 4 + 1)

    lax.fori_loop(1, n, g_start, 0)

    @pl.when(e == 0)
    def _():
        for dst in range(2):
            cache_copy(half, dst).start()


    @pl.when(e == 1)
    def _():
        for src in range(4):
            z_copy(src, 0).wait_recv()
        xall[s] = jnp.where(arrived, zin[source], x_v[...])
        lax.fori_loop(1, n, x_start, 0)

    g_in[s] = gbuf[...]

    for i in range(width // part):
        cols = pl.ds(i * part, part)
        hi, lo = split(p_v[:, cols].astype(F32) - p_mean)
        c2[0:64, cols] = hi
        c2[ROWS : ROWS + 64, cols] = lo
        bias = jnp.broadcast_to(b_v[:, cols] - b_mean, (16, part))
        hi, lo = split(jnp.where(tail_row == 0, bias, 0.0))
        c2[64:ROWS, cols] = hi
        c2[ROWS + 64 : 2 * ROWS, cols] = lo
    var_gram = (
        dot_nt(c2[0:ROWS, :], c2[0:ROWS, :])
        + dot_nt(c2[0:ROWS, :], c2[ROWS : 2 * ROWS, :])
        + dot_nt(c2[ROWS : 2 * ROWS, :], c2[0:ROWS, :])
    ) * (1.0 / width)

    ld_w[2].wait()
    project(2)

    ld_gain.wait()
    for j in range(3):
        m_v[j, ROWS:128, :] = jnp.zeros((128 - ROWS, 256), F32)
        full = m_v[j]
        if j < 2:
            full = full * gain_v[j : j + 1, :]
        flipped = full.T
        hi, lo = split(flipped)
        for h in range(2):
            at = 512 + h * 128 if j == 2 else h * 256 + j * 128
            rows = slice(h * 128, (h + 1) * 128)
            mt2[at : at + 128, 0:128] = hi[rows, :]
            mt2[at : at + 128, 128:256] = lo[rows, :]
        mtf[j] = flipped

    first16 = lax.broadcasted_iota(jnp.int32, (16, tokens), 0)
    first128 = lax.broadcasted_iota(jnp.int32, (128, tokens), 0)
    one16 = jnp.where(first16 == 0, 1.0, 0.0).astype(BF)
    one128 = jnp.where(first128 == 0, 1.0, 0.0).astype(BF)
    for h in range(2):
        qaug[h, 128:256, :] = one128
        vaug[h, 128:144, :] = one16
    key_at = lax.broadcasted_iota(jnp.int32, (128, 128), 0)
    for i in range(n):
        masks = jnp.where(key_at + order[i] * 128 >= length, MASKED, 0.0).astype(BF)
        for h in range(2):
            kaug[h, i * 128 : (i + 1) * 128, 128:256] = masks

    tail64 = lax.broadcasted_iota(jnp.int32, (64, tokens), 0)
    ones_row = jnp.where(tail64 == 0, 1.0, 0.0).astype(BF)
    z2[64:128, :] = ones_row
    z2[192:256, :] = ones_row
    hi, lo = split(var_gram)
    stat[...] = jnp.zeros_like(stat)
    stat[0:ROWS, 0:ROWS] = hi
    stat[0:ROWS, 128 : 128 + ROWS] = lo
    g_all().wait_recv()
    packed = g_in[0].astype(F32)
    for src in range(1, n):
        packed = packed + g_in[src].astype(F32)
    both = jnp.concatenate([packed[0:32, 0:64], packed[0:32, 64:128]], axis=0)
    packed = packed[32:40, :] + packed[40:48, :]
    diagonals = [
        jnp.where(at_col == at_row, jnp.broadcast_to(packed[2:3, j * 64 : j * 64 + 64], (64, 64)), 0.0)
        for j in range(2)
    ]
    lower = jnp.where(at_col < at_row, both, diagonals[0])
    upper = jnp.where(at_col > at_row, both, diagonals[1])
    tail16 = lax.broadcasted_iota(jnp.int32, (16, 64), 0)
    linear = jnp.zeros((16, 64), F32)
    for at, row in enumerate(
        (packed[0:1, 0:64], packed[1:2, 0:64], packed[0:1, 64:128], packed[1:2, 64:128])
    ):
        linear = jnp.where(tail16 == at, jnp.broadcast_to(row, (16, 64)), linear)
    hi, lo = split(jnp.concatenate([lower, upper, linear], axis=0))
    stat[ROWS : ROWS + 144, 0:64] = hi
    stat[ROWS : ROWS + 144, 128:192] = lo

    x_all().wait_recv()
    for i in range(n):
        cols = slice(i * 128, (i + 1) * 128)
        rows = xall[order[i]]
        z2[0:64, cols] = rows
        z2[128:192, cols] = rows
    t = dot(stat[...], z2[...])
    z80 = z2[0:ROWS, :].astype(F32)
    var = jnp.maximum(jnp.sum(t[0:ROWS, :] * z80, axis=0, keepdims=True), 0.0)
    rstd = lax.rsqrt(var + EPS)
    scales = []
    for j in range(2):
        base = ROWS + j * 64
        quad = jnp.sum(t[base : base + 64, :] * z80[0:64, :], axis=0, keepdims=True)
        base = ROWS + 128 + 2 * j
        by_bias = t[base : base + 1, :]
        by_shift = t[base + 1 : base + 2, :]
        at = 3 + 2 * j
        total = (
            rstd * rstd * (quad + 2.0 * by_bias + packed[at : at + 1, 0:1])
            + 2.0 * rstd * (by_shift + packed[at : at + 1, 1:2])
            + packed[at + 1 : at + 2, 1:2]
        )
        scales.append(lax.rsqrt(jnp.maximum(total, 0.0) * (1.0 / (n * 256)) + EPS))
    r_q = scales[0] * (LOG2E / HD**0.5)
    r_k = scales[1]

    q_u = r_q * rstd
    k_u = r_k * rstd
    piece = 512

    def heads(h):
        for i in range(tokens // piece):
            cols = slice(i * piece, (i + 1) * piece)
            raw = dot(mt2[h * 256 : (h + 1) * 256, :], z2[:, cols])
            rows = slice(h * 128, (h + 1) * 128)
            qaug[h, 0:128, cols] = (
                raw[0:128, :] * q_u[:, cols] + mtf[0, rows, 65:66] * r_q[:, cols]
            ).astype(BF)
            k_t = raw[128:256, :] * k_u[:, cols] + mtf[1, rows, 65:66] * r_k[:, cols]
            kaug[h, cols, 0:128] = k_t.T.astype(BF)

    heads(0)
    first_top = jnp.full((8, QB), -3e38, F32)
    for c in range(tokens // KB):
        rows = slice(c * KB, (c + 1) * KB)
        score = dot(kaug[0, rows, :], qaug[0, :, 0:QB])
        s_a[rows, :] = score
        first_top = jnp.maximum(first_top, jnp.max(score.reshape(KB // 8, 8, QB), axis=0))
    def values(h):
        for i in range(tokens // piece):
            cols = slice(i * piece, (i + 1) * piece)
            rows = slice(h * 128, (h + 1) * 128)
            raw = dot(mt2[512 + h * 128 : 640 + h * 128, :], z2[:, cols])
            vaug[h, 0:128, cols] = (raw * rstd[:, cols] + mtf[2, rows, 65:66]).astype(BF)

    blocks = tokens // QB

    def o_copy(block, side, h, peer, src):
        return pltpu.make_async_remote_copy(
            src_ref=ostage.at[h, block, pl.ds(side * 128, 128)],
            dst_ref=out_hbm.at[:, pl.ds(pl.multiple_of(src * 256 + h * 128, 128), 128)],
            send_sem=osend,
            recv_sem=orecv,
            device_id={"seq": peer},
            device_id_type=MESH,
        )

    def o_all():
        return pltpu.make_async_remote_copy(
            src_ref=out_hbm.at[:, pl.ds(0, (n - 1) * 256)],
            dst_ref=out_hbm.at[:, pl.ds(0, (n - 1) * 256)],
            send_sem=osend,
            recv_sem=orecv,
            device_id={"seq": lax.rem(s + 1, n)},
            device_id_type=MESH,
        )

    def own_copy(h):
        return pltpu.make_async_copy(
            ostage.at[h, blocks - 1, pl.ds((OWNERS - 1) * 128, 128)],
            out_hbm.at[:, pl.ds(pl.multiple_of(s * 256 + h * 128, 128), 128)],
            load_sem.at[h],
        )

    def send(block, h):
        for side in range(OWNERS - 1):
            o_copy(block, side, h, order[block * OWNERS + side], s).start()

        if block == blocks - 1:
            own_copy(h).start()
        else:
            o_copy(block, OWNERS - 1, h, order[block * OWNERS + OWNERS - 1], s).start()

    def unit(block, h, now, top, next_block, next_h, later):
        ahead = later is not None
        if ahead:
            query = qaug[next_h, :, next_block * QB : (next_block + 1) * QB]
        next_top = jnp.full((8, QB), -3e38, F32)
        total = jnp.zeros((144, QB), F32)
        for c in range(tokens // KB):
            rows = slice(c * KB, (c + 1) * KB)
            if ahead:
                score = dot(kaug[next_h, rows, :], query)
                later[rows, :] = score
                next_top = jnp.maximum(next_top, jnp.max(score.reshape(KB // 8, 8, QB), axis=0))
            weight = jnp.exp2(now[rows, :] - top).astype(BF)
            total = total + dot(vaug[h, :, rows], weight)
        row = lax.broadcasted_iota(jnp.int32, (1, 128), 1)
        live = [row + order[block * OWNERS + side] * 128 < length for side in range(OWNERS)]
        inverse = 1.0 / total[128:129, :]
        inverse = jnp.concatenate(
            [jnp.where(live[a], inverse[:, a * 128 : (a + 1) * 128], 0.0) for a in range(OWNERS)], axis=1
        )
        ostage[h, block] = (total[0:128, :] * inverse).T.astype(BF)
        return jnp.max(next_top, axis=0, keepdims=True)

    def forward():
        @pl.when(e == 1)
        def _():
            for src in range(2):
                cache_copy(src, 0).wait_recv()
                forward_copy(src, core).start()

    units = [(block, h) for h in range(2) for block in range(blocks)]
    halves = (s_a, s_b)
    values(0)
    top = jnp.max(first_top, axis=0, keepdims=True)
    for at, (block, h) in enumerate(units):
        if at == 2:
            heads(1)
        if at == blocks:
            values(1)
        if at == len(units) - 2:
            forward()
        if at + 1 < len(units):
            top = unit(block, h, halves[at % 2], top, *units[at + 1], halves[(at + 1) % 2])
        else:
            unit(block, h, halves[at % 2], top, None, None, None)
        send(block, h)

    ld_cache.wait()
    height = own_cache.shape[0] // 8

    @pl.when(e == 1)
    def _():
        for src in range(2):
            forward_copy(src, core).wait_send()
            forward_copy(src, 1 - core).wait_recv()

        def choose(i, carry):
            rows = pl.ds(i * height, height)
            own_cache[rows] = jnp.where(arrived, land[source, rows], own_cache[rows])
            return carry

        lax.fori_loop(0, 8, choose, 0)

    @pl.when(e == 0)
    def _():
        for dst in range(4):
            z_copy(g, dst).wait_send()
        for dst in range(2):
            cache_copy(half, dst).wait_send()

        def choose(i, carry):
            rows = pl.ds(i * height, height)
            kept = own_cache[rows]
            own_cache[rows] = jnp.where(left, jnp.zeros_like(kept), kept)
            return carry

        lax.fori_loop(0, 8, choose, 0)

    st_cache.start()
    x_all().wait_send()
    g_all().wait_send()
    o_all().wait_send()
    for h in range(2):
        own_copy(h).wait()
    st_cache.wait()
    o_all().wait_recv()


def place(raw, cache, out, cache_out, sem):
    parts = 4
    writes = []
    for at, (src, dst) in enumerate(((raw, out), (cache, cache_out))):
        height = src.shape[0] // parts
        for i in range(parts):
            rows = pl.ds(i * height, height)
            writes.append(pltpu.make_async_copy(src.at[rows], dst.at[rows], sem.at[at, i]))
    for copy in writes:
        copy.start()
    for copy in writes:
        copy.wait()


def shards(
    n,
    latent,
    text_cache,
    patch_weight,
    patch_bias,
    qkv_weight,
    qk_gain,
    modulation,
    step_index,
    lengths,
    crossing,
):
    tokens = n * 128
    width = qkv_weight.shape[1]
    xt = latent[0, 0].T
    w3 = jnp.transpose(qkv_weight[0], (1, 0, 2))
    cache = text_cache[0, 0]
    hbm = pl.BlockSpec(memory_space=pl.ANY)
    dma = pltpu.SemaphoreType.DMA
    raw, chosen = pl.pallas_call(
        functools.partial(kernel, n),
        out_shape=(
            pltpu.VMEM((128, n * 256), BF),
            pltpu.VMEM(cache.shape, BF),
        ),
        in_specs=[hbm] * 10,
        out_specs=(hbm, hbm),
        scratch_shapes=[
            pltpu.SMEM((2, 2), jnp.int32),
            pltpu.SMEM((2, 4), jnp.int32),
            pltpu.SMEM((2, 4), jnp.int32),
            pltpu.VMEM((64, 128), BF),
            pltpu.VMEM((1, width), F32),
            pltpu.VMEM((2, 256), F32),
            pltpu.VMEM((64, width), BF),
            pltpu.VMEM(modulation.shape[1:], F32),
            pltpu.VMEM((3, width, 256), BF),
            pltpu.VMEM((2 * ROWS, width), BF),
            pltpu.VMEM((2 * ROWS, width), BF),
            pltpu.VMEM((4, 64, 128), BF),
            pltpu.VMEM((n, 64, 128), BF),
            pltpu.VMEM((3, 128, 256), F32),
            pltpu.VMEM((PACKED, 128), BF),
            pltpu.VMEM((8, 128), F32),
            pltpu.VMEM((n, PACKED, 128), BF),
            pltpu.VMEM((ROWS + 144, 256), BF),
            pltpu.VMEM((256, tokens), BF),
            pltpu.VMEM((768, 256), BF),
            pltpu.VMEM((3, 256, 128), F32),
            pltpu.VMEM((2, 256, tokens), BF),
            pltpu.VMEM((2, tokens, 256), BF),
            pltpu.VMEM((2, 144, tokens), BF),
            pltpu.VMEM((tokens, QB), F32),
            pltpu.VMEM((tokens, QB), F32),
            pltpu.VMEM((2, tokens // QB, QB, 128), BF),
            pltpu.VMEM(cache.shape, BF),
            pltpu.VMEM((4,) + cache.shape, BF),
            dma((12,)),
            dma((4,)),
            dma((4,)),
            dma((2,)),
            dma((2,)),
            dma((2,)),
            dma((2,)),
            dma,
            dma,
            dma,
            dma,
            dma,
            dma,
        ],
        compiler_params=pltpu.CompilerParams(
            collective_id=0, has_side_effects=True, vmem_limit_bytes=58 * 1024 * 1024
        ),
    )(
        crossing,
        lengths,
        step_index,
        xt,
        patch_bias,
        qk_gain[0],
        patch_weight[0],
        modulation[0],
        w3,
        cache,
    )
    attended, cache_after = pl.pallas_call(
        place,
        out_shape=(
            jax.ShapeDtypeStruct(raw.shape, BF),
            jax.ShapeDtypeStruct(cache.shape, BF),
        ),
        in_specs=[hbm] * 2,
        out_specs=(hbm, hbm),
        scratch_shapes=[dma((2, 4))],
    )(
        pltpu.with_memory_space_constraint(raw, pltpu.VMEM),
        pltpu.with_memory_space_constraint(chosen, pltpu.VMEM),
    )
    return (attended[None, None], cache_after[None, None])


def solution(mesh):
    in_specs = (
        P("expert", "group", "seq", None),
        P("expert", "group", None, "seq", None),
        P("expert", None, None),
        P("expert", None),
        P("expert", None, None, "seq"),
        P("expert", None, "seq"),
        P("expert", None, None, None),
        P(),
        P(),
        P(),
    )
    out_specs = (P("expert", "group", "seq", None), P("expert", "group", None, "seq", None))
    return jax.shard_map(
        functools.partial(shards, mesh.shape["seq"]),
        mesh=mesh,
        in_specs=in_specs,
        out_specs=out_specs,
        check_vma=False,
    )
```

```python
import functools

import jax
import jax.numpy as jnp
from jax import lax
from jax.experimental import pallas as pl
from jax.experimental.pallas import tpu as pltpu
from jax.sharding import PartitionSpec as P

HD = 128
EPS = 1e-06
MASKED = -1e30
LOG2E = 1.4426950408889634
BF = jnp.bfloat16
F32 = jnp.float32
MESH = pl.DeviceIdType.MESH
ROWS = 80
PACKED = 48
SIDE = 4
QB = 512
KB = 256
OWNERS = QB // 128
STEPS = (
    ((2, 2), (1, 1), (3, 3), (2, 0))
    + ((0, 2), (1, 2), (3, 1), (2, 3))
    + ((1, 3), (3, 2), (2, 1), (0, 3))
    + ((1, 0), (3, 0), (0, 1), (0, 0))
)


def dot(a, b):
    return jnp.dot(a, b, preferred_element_type=F32)


def dot_nt(a, b):
    return lax.dot_general(a, b, (((1,), (1,)), ((), ())), preferred_element_type=F32)


def split(a):
    hi = a.astype(BF)
    lo = (a - hi.astype(F32)).astype(BF)
    return hi, lo


def gram(a):
    hi, lo = split(a)
    return dot_nt(hi, hi) + dot_nt(hi, lo) + dot_nt(lo, hi)


def kernel(
    n,
    crossing_hbm,
    lengths_hbm,
    steps_hbm,
    xt_hbm,
    b_hbm,
    gain_hbm,
    p_hbm,
    mod_hbm,
    w_hbm,
    cache_hbm,
    out_hbm,
    cache_out,
    crossing,
    lengths,
    steps,
    x_v,
    b_v,
    gain_v,
    p_v,
    mod_v,
    w_v,
    a2,
    c2,
    zin,
    xall,
    m_v,
    gbuf,
    rest,
    g_in,
    stat,
    z2,
    mt2,
    mtf,
    qaug,
    kaug,
    vaug,
    s_a,
    s_b,
    ostage,
    own_cache,
    land,
    load_sem,
    zsend,
    zrecv,
    csend,
    crecv,
    fsend,
    frecv,
    xsend,
    xrecv,
    gsend,
    grecv,
    osend,
    orecv,
):
    e = lax.axis_index("expert")
    g = lax.axis_index("group")
    s = lax.axis_index("seq")
    half = lax.div(g, 2)
    core = lax.rem(g, 2)
    my_x = lax.div(s, SIDE)
    my_y = lax.rem(s, SIDE)
    tokens = n * 128
    width = p_v.shape[1]

    def owner(step):
        return lax.rem(my_x + step[0], SIDE) * SIDE + lax.rem(my_y + step[1], SIDE)

    order = [owner(step) for step in STEPS]

    ld_p = pltpu.make_async_copy(p_hbm, p_v, load_sem.at[0])
    ld_b = pltpu.make_async_copy(b_hbm, b_v, load_sem.at[1])
    ld_x = pltpu.make_async_copy(xt_hbm, x_v, load_sem.at[2])
    ld_mod = pltpu.make_async_copy(mod_hbm, mod_v, load_sem.at[3])
    ld_gain = pltpu.make_async_copy(gain_hbm, gain_v, load_sem.at[4])
    ld_w = [pltpu.make_async_copy(w_hbm.at[j], w_v.at[j], load_sem.at[5 + j]) for j in range(3)]
    ld_scalars = [
        pltpu.make_async_copy(src, dst, load_sem.at[8 + i])
        for i, (src, dst) in enumerate(
            ((crossing_hbm, crossing), (lengths_hbm, lengths), (steps_hbm, steps))
        )
    ]
    ld_cache = pltpu.make_async_copy(cache_hbm, own_cache, load_sem.at[11])
    st_cache = pltpu.make_async_copy(own_cache, cache_out, load_sem.at[11])
    for copy in [ld_x] + ld_scalars + [ld_p, ld_b, ld_mod, ld_gain, ld_w[0], ld_w[1]]:
        copy.start()

    barrier = pltpu.get_barrier_semaphore()

    def greet(k, carry):
        pl.semaphore_signal(barrier, inc=1, device_id={"seq": lax.rem(s + k, n)}, device_id_type=MESH)
        return carry

    for other in range(4):
        pl.semaphore_signal(
            barrier, inc=1, device_id={"expert": 1 - e, "group": other}, device_id_type=MESH
        )
    lax.fori_loop(1, n, greet, 0)

    @pl.when(e == 1)
    def _():
        pl.semaphore_signal(barrier, inc=1, device_id={"group": 2 * half + 1 - core}, device_id_type=MESH)

    def z_copy(src_group, dst_group):
        return pltpu.make_async_remote_copy(
            src_ref=x_v,
            dst_ref=zin.at[src_group],
            send_sem=zsend.at[dst_group],
            recv_sem=zrecv.at[src_group],
            device_id={"expert": 1, "group": dst_group},
            device_id_type=MESH,
        )

    def cache_copy(src_half, dst_half):
        return pltpu.make_async_remote_copy(
            src_ref=cache_hbm,
            dst_ref=land.at[2 * src_half + core],
            send_sem=csend.at[dst_half],
            recv_sem=crecv.at[src_half],
            device_id={"expert": 1, "group": 2 * dst_half + core},
            device_id_type=MESH,
        )

    def forward_copy(src_half, src_core):
        return pltpu.make_async_remote_copy(
            src_ref=land.at[2 * src_half + src_core],
            dst_ref=land.at[2 * src_half + src_core],
            send_sem=fsend.at[src_half],
            recv_sem=frecv.at[src_half],
            device_id={"expert": 1, "group": 2 * half + 1 - core},
            device_id_type=MESH,
        )

    def x_copy(peer, slot):
        return pltpu.make_async_remote_copy(
            src_ref=xall.at[slot],
            dst_ref=xall.at[slot],
            send_sem=xsend,
            recv_sem=xrecv,
            device_id={"seq": peer},
            device_id_type=MESH,
        )

    def x_all():
        return pltpu.make_async_remote_copy(
            src_ref=xall.at[pl.ds(0, n - 1)],
            dst_ref=xall.at[pl.ds(0, n - 1)],
            send_sem=xsend,
            recv_sem=xrecv,
            device_id={"seq": lax.rem(s + 1, n)},
            device_id_type=MESH,
        )

    def x_start():
        for peer in order[: n - 1]:
            x_copy(peer, s).start()

    ld_x.wait()

    @pl.when(e == 0)
    def _():
        pl.semaphore_wait(barrier, n - 1 + 4)
        for dst in range(4):
            z_copy(g, dst).start()
        xall[s] = x_v[...]
        x_start()

    for copy in ld_scalars:
        copy.wait()
    hit0 = crossing[0, 1] == g
    hit1 = crossing[1, 1] == g
    arrived = jnp.logical_and(e == 1, jnp.logical_or(hit0, hit1))
    left = jnp.logical_and(e == 0, jnp.logical_or(crossing[0, 0] == g, crossing[1, 0] == g))
    source = jnp.where(hit0, crossing[0, 0], jnp.where(hit1, crossing[1, 0], 0))
    step_now = jnp.where(arrived, steps[0, source], steps[e, g])
    length = jnp.where(left, 0, jnp.where(arrived, lengths[0, source], lengths[e, g]))

    ld_p.wait()
    ld_b.wait()
    p_mean = jnp.mean(p_v[...].astype(F32), axis=1, keepdims=True)
    b_mean = jnp.mean(b_v[...], axis=1, keepdims=True)
    ld_mod.wait()
    part = 1024
    tail_row = lax.broadcasted_iota(jnp.int32, (16, part), 0)
    for i in range(width // part):
        cols = pl.ds(i * part, part)
        modulate = mod_v[step_now, :, cols]
        scale = 1.0 + modulate[1:2, :]
        shift = modulate[0:1, :]
        top = (p_v[:, cols].astype(F32) - p_mean) * scale
        bias = (b_v[:, cols] - b_mean) * scale
        bottom = jnp.where(
            tail_row == 0,
            jnp.broadcast_to(bias, (16, part)),
            jnp.where(tail_row == 1, jnp.broadcast_to(shift, (16, part)), 0.0),
        )
        hi, lo = split(top)
        a2[0:64, cols] = hi
        a2[ROWS : ROWS + 64, cols] = lo
        hi, lo = split(bottom)
        a2[64:ROWS, cols] = hi
        a2[ROWS + 64 : 2 * ROWS, cols] = lo

    def project(j):
        raw = dot(a2[...], w_v[j])
        total = raw[0:ROWS, :] + raw[ROWS : 2 * ROWS, :]
        m_v[j, 0:ROWS, :] = total
        return total

    ld_w[0].wait()
    ld_w[2].start()
    ld_cache.start()
    m_q = project(0)
    ld_w[1].wait()
    m_k = project(1)

    gram_q = gram(m_q)
    gram_k = gram(m_k)
    at_row = lax.broadcasted_iota(jnp.int32, (64, 64), 0)
    at_col = lax.broadcasted_iota(jnp.int32, (64, 64), 1)
    core_q = gram_q[0:64, 0:64]
    core_k = gram_k[0:64, 0:64]
    both = jnp.where(at_col < at_row, 2.0 * core_q, jnp.where(at_col > at_row, 2.0 * core_k, 0.0)).astype(BF)
    gbuf[0:32, 0:64] = both[0:32, :]
    gbuf[0:32, 64:128] = both[32:64, :]
    rest[...] = jnp.zeros_like(rest)
    for at, (values, centre) in enumerate(((gram_q, core_q), (gram_k, core_k))):
        cols = slice(at * 64, at * 64 + 64)
        rest[0:2, cols] = values[64:66, 0:64]
        rest[2:3, cols] = jnp.sum(jnp.where(at_col == at_row, centre, 0.0), axis=0, keepdims=True)
        rest[3 + 2 * at : 5 + 2 * at, 0:16] = values[64:66, 64:80]
    hi, lo = split(rest[...])
    gbuf[32:48, :] = jnp.concatenate([hi.astype(F32), lo.astype(F32)], axis=0).astype(BF)

    def g_copy(peer, slot):
        return pltpu.make_async_remote_copy(
            src_ref=gbuf,
            dst_ref=g_in.at[slot],
            send_sem=gsend,
            recv_sem=grecv,
            device_id={"seq": peer},
            device_id_type=MESH,
        )

    def g_all():
        return pltpu.make_async_remote_copy(
            src_ref=g_in.at[pl.ds(0, n - 1)],
            dst_ref=g_in.at[pl.ds(0, n - 1)],
            send_sem=gsend,
            recv_sem=grecv,
            device_id={"seq": lax.rem(s + 1, n)},
            device_id_type=MESH,
        )

    def g_start():
        for peer in order[: n - 1]:
            g_copy(peer, s).start()

    @pl.when(e == 1)
    def _():
        pl.semaphore_wait(barrier, n - 1 + 4 + 1)

    g_start()

    @pl.when(e == 0)
    def _():
        for dst in range(2):
            cache_copy(half, dst).start()


    @pl.when(e == 1)
    def _():
        for src in range(4):
            z_copy(src, 0).wait_recv()
        xall[s] = jnp.where(arrived, zin[source], x_v[...])
        x_start()

    g_in[s] = gbuf[...]

    for i in range(width // part):
        cols = pl.ds(i * part, part)
        hi, lo = split(p_v[:, cols].astype(F32) - p_mean)
        c2[0:64, cols] = hi
        c2[ROWS : ROWS + 64, cols] = lo
        bias = jnp.broadcast_to(b_v[:, cols] - b_mean, (16, part))
        hi, lo = split(jnp.where(tail_row == 0, bias, 0.0))
        c2[64:ROWS, cols] = hi
        c2[ROWS + 64 : 2 * ROWS, cols] = lo
    var_gram = (
        dot_nt(c2[0:ROWS, :], c2[0:ROWS, :])
        + dot_nt(c2[0:ROWS, :], c2[ROWS : 2 * ROWS, :])
        + dot_nt(c2[ROWS : 2 * ROWS, :], c2[0:ROWS, :])
    ) * (1.0 / width)

    ld_w[2].wait()
    project(2)

    ld_gain.wait()
    for j in range(3):
        m_v[j, ROWS:128, :] = jnp.zeros((128 - ROWS, 256), F32)
        full = m_v[j]
        if j < 2:
            full = full * gain_v[j : j + 1, :]
        flipped = full.T
        hi, lo = split(flipped)
        for h in range(2):
            at = 512 + h * 128 if j == 2 else h * 256 + j * 128
            rows = slice(h * 128, (h + 1) * 128)
            mt2[at : at + 128, 0:128] = hi[rows, :]
            mt2[at : at + 128, 128:256] = lo[rows, :]
        mtf[j] = flipped

    first16 = lax.broadcasted_iota(jnp.int32, (16, tokens), 0)
    first128 = lax.broadcasted_iota(jnp.int32, (128, tokens), 0)
    one16 = jnp.where(first16 == 0, 1.0, 0.0).astype(BF)
    one128 = jnp.where(first128 == 0, 1.0, 0.0).astype(BF)
    for h in range(2):
        qaug[h, 128:256, :] = one128
        vaug[h, 128:144, :] = one16
    key_at = lax.broadcasted_iota(jnp.int32, (128, 128), 0)
    for i in range(n):
        masks = jnp.where(key_at + order[i] * 128 >= length, MASKED, 0.0).astype(BF)
        for h in range(2):
            kaug[h, i * 128 : (i + 1) * 128, 128:256] = masks

    tail64 = lax.broadcasted_iota(jnp.int32, (64, tokens), 0)
    ones_row = jnp.where(tail64 == 0, 1.0, 0.0).astype(BF)
    z2[64:128, :] = ones_row
    z2[192:256, :] = ones_row
    hi, lo = split(var_gram)
    stat[...] = jnp.zeros_like(stat)
    stat[0:ROWS, 0:ROWS] = hi
    stat[0:ROWS, 128 : 128 + ROWS] = lo
    g_all().wait_recv()
    packed = g_in[0].astype(F32)
    for src in range(1, n):
        packed = packed + g_in[src].astype(F32)
    both = jnp.concatenate([packed[0:32, 0:64], packed[0:32, 64:128]], axis=0)
    packed = packed[32:40, :] + packed[40:48, :]
    diagonals = [
        jnp.where(at_col == at_row, jnp.broadcast_to(packed[2:3, j * 64 : j * 64 + 64], (64, 64)), 0.0)
        for j in range(2)
    ]
    lower = jnp.where(at_col < at_row, both, diagonals[0])
    upper = jnp.where(at_col > at_row, both, diagonals[1])
    tail16 = lax.broadcasted_iota(jnp.int32, (16, 64), 0)
    linear = jnp.zeros((16, 64), F32)
    for at, row in enumerate(
        (packed[0:1, 0:64], packed[1:2, 0:64], packed[0:1, 64:128], packed[1:2, 64:128])
    ):
        linear = jnp.where(tail16 == at, jnp.broadcast_to(row, (16, 64)), linear)
    hi, lo = split(jnp.concatenate([lower, upper, linear], axis=0))
    stat[ROWS : ROWS + 144, 0:64] = hi
    stat[ROWS : ROWS + 144, 128:192] = lo

    x_all().wait_recv()
    for i in range(n):
        cols = slice(i * 128, (i + 1) * 128)
        rows = xall[order[i]]
        z2[0:64, cols] = rows
        z2[128:192, cols] = rows
    t = dot(stat[...], z2[...])
    z80 = z2[0:ROWS, :].astype(F32)
    var = jnp.maximum(jnp.sum(t[0:ROWS, :] * z80, axis=0, keepdims=True), 0.0)
    rstd = lax.rsqrt(var + EPS)
    scales = []
    for j in range(2):
        base = ROWS + j * 64
        quad = jnp.sum(t[base : base + 64, :] * z80[0:64, :], axis=0, keepdims=True)
        base = ROWS + 128 + 2 * j
        by_bias = t[base : base + 1, :]
        by_shift = t[base + 1 : base + 2, :]
        at = 3 + 2 * j
        total = (
            rstd * rstd * (quad + 2.0 * by_bias + packed[at : at + 1, 0:1])
            + 2.0 * rstd * (by_shift + packed[at : at + 1, 1:2])
            + packed[at + 1 : at + 2, 1:2]
        )
        scales.append(lax.rsqrt(jnp.maximum(total, 0.0) * (1.0 / (n * 256)) + EPS))
    r_q = scales[0] * (LOG2E / HD**0.5)
    r_k = scales[1]

    q_u = r_q * rstd
    k_u = r_k * rstd
    piece = 512

    def heads(h):
        for i in range(tokens // piece):
            cols = slice(i * piece, (i + 1) * piece)
            raw = dot(mt2[h * 256 : (h + 1) * 256, :], z2[:, cols])
            rows = slice(h * 128, (h + 1) * 128)
            qaug[h, 0:128, cols] = (
                raw[0:128, :] * q_u[:, cols] + mtf[0, rows, 65:66] * r_q[:, cols]
            ).astype(BF)
            k_t = raw[128:256, :] * k_u[:, cols] + mtf[1, rows, 65:66] * r_k[:, cols]
            kaug[h, cols, 0:128] = k_t.T.astype(BF)

    heads(0)
    first_top = jnp.full((8, QB), -3e38, F32)
    for c in range(tokens // KB):
        rows = slice(c * KB, (c + 1) * KB)
        score = dot(kaug[0, rows, :], qaug[0, :, 0:QB])
        s_a[rows, :] = score
        first_top = jnp.maximum(first_top, jnp.max(score.reshape(KB // 8, 8, QB), axis=0))
    def values(h):
        for i in range(tokens // piece):
            cols = slice(i * piece, (i + 1) * piece)
            rows = slice(h * 128, (h + 1) * 128)
            raw = dot(mt2[512 + h * 128 : 640 + h * 128, :], z2[:, cols])
            vaug[h, 0:128, cols] = (raw * rstd[:, cols] + mtf[2, rows, 65:66]).astype(BF)

    blocks = tokens // QB

    def o_copy(block, side, h, peer, src):
        return pltpu.make_async_remote_copy(
            src_ref=ostage.at[h, block, pl.ds(side * 128, 128)],
            dst_ref=out_hbm.at[:, pl.ds(pl.multiple_of(src * 256 + h * 128, 128), 128)],
            send_sem=osend,
            recv_sem=orecv,
            device_id={"seq": peer},
            device_id_type=MESH,
        )

    def o_all():
        return pltpu.make_async_remote_copy(
            src_ref=out_hbm.at[:, pl.ds(0, (n - 1) * 256)],
            dst_ref=out_hbm.at[:, pl.ds(0, (n - 1) * 256)],
            send_sem=osend,
            recv_sem=orecv,
            device_id={"seq": lax.rem(s + 1, n)},
            device_id_type=MESH,
        )

    def own_copy(h):
        return pltpu.make_async_copy(
            ostage.at[h, blocks - 1, pl.ds((OWNERS - 1) * 128, 128)],
            out_hbm.at[:, pl.ds(pl.multiple_of(s * 256 + h * 128, 128), 128)],
            load_sem.at[h],
        )

    def send(block, h):
        for side in range(OWNERS - 1):
            o_copy(block, side, h, order[block * OWNERS + side], s).start()

        if block == blocks - 1:
            own_copy(h).start()
        else:
            o_copy(block, OWNERS - 1, h, order[block * OWNERS + OWNERS - 1], s).start()

    def unit(block, h, now, top, next_block, next_h, later):
        ahead = later is not None
        if ahead:
            query = qaug[next_h, :, next_block * QB : (next_block + 1) * QB]
        next_top = jnp.full((8, QB), -3e38, F32)
        total = jnp.zeros((144, QB), F32)
        for c in range(tokens // KB):
            rows = slice(c * KB, (c + 1) * KB)
            if ahead:
                score = dot(kaug[next_h, rows, :], query)
                later[rows, :] = score
                next_top = jnp.maximum(next_top, jnp.max(score.reshape(KB // 8, 8, QB), axis=0))
            weight = jnp.exp2(now[rows, :] - top).astype(BF)
            total = total + dot(vaug[h, :, rows], weight)
        row = lax.broadcasted_iota(jnp.int32, (1, 128), 1)
        live = [row + order[block * OWNERS + side] * 128 < length for side in range(OWNERS)]
        inverse = 1.0 / total[128:129, :]
        inverse = jnp.concatenate(
            [jnp.where(live[a], inverse[:, a * 128 : (a + 1) * 128], 0.0) for a in range(OWNERS)], axis=1
        )
        ostage[h, block] = (total[0:128, :] * inverse).T.astype(BF)
        return jnp.max(next_top, axis=0, keepdims=True)

    def forward():
        @pl.when(e == 1)
        def _():
            for src in range(2):
                cache_copy(src, 0).wait_recv()
                forward_copy(src, core).start()

    units = [(block, h) for h in range(2) for block in range(blocks)]
    halves = (s_a, s_b)
    values(0)
    top = jnp.max(first_top, axis=0, keepdims=True)
    for at, (block, h) in enumerate(units):
        if at == 2:
            heads(1)
        if at == blocks:
            values(1)
        if at == len(units) - 2:
            forward()
        if at + 1 < len(units):
            top = unit(block, h, halves[at % 2], top, *units[at + 1], halves[(at + 1) % 2])
        else:
            unit(block, h, halves[at % 2], top, None, None, None)
        send(block, h)

    ld_cache.wait()
    height = own_cache.shape[0] // 8

    @pl.when(e == 1)
    def _():
        for src in range(2):
            forward_copy(src, core).wait_send()
            forward_copy(src, 1 - core).wait_recv()

        def choose(i, carry):
            rows = pl.ds(i * height, height)
            own_cache[rows] = jnp.where(arrived, land[source, rows], own_cache[rows])
            return carry

        lax.fori_loop(0, 8, choose, 0)

    @pl.when(e == 0)
    def _():
        for dst in range(4):
            z_copy(g, dst).wait_send()
        for dst in range(2):
            cache_copy(half, dst).wait_send()

        def choose(i, carry):
            rows = pl.ds(i * height, height)
            kept = own_cache[rows]
            own_cache[rows] = jnp.where(left, jnp.zeros_like(kept), kept)
            return carry

        lax.fori_loop(0, 8, choose, 0)

    st_cache.start()
    x_all().wait_send()
    g_all().wait_send()
    o_all().wait_send()
    for h in range(2):
        own_copy(h).wait()
    st_cache.wait()
    o_all().wait_recv()


def place(raw, cache, out, cache_out, sem):
    parts = 4
    writes = []
    for at, (src, dst) in enumerate(((raw, out), (cache, cache_out))):
        height = src.shape[0] // parts
        for i in range(parts):
            rows = pl.ds(i * height, height)
            writes.append(pltpu.make_async_copy(src.at[rows], dst.at[rows], sem.at[at, i]))
    for copy in writes:
        copy.start()
    for copy in writes:
        copy.wait()


def shards(
    n,
    latent,
    text_cache,
    patch_weight,
    patch_bias,
    qkv_weight,
    qk_gain,
    modulation,
    step_index,
    lengths,
    crossing,
):
    tokens = n * 128
    width = qkv_weight.shape[1]
    xt = latent[0, 0].T
    w3 = jnp.transpose(qkv_weight[0], (1, 0, 2))
    cache = text_cache[0, 0]
    hbm = pl.BlockSpec(memory_space=pl.ANY)
    dma = pltpu.SemaphoreType.DMA
    raw, chosen = pl.pallas_call(
        functools.partial(kernel, n),
        out_shape=(
            pltpu.VMEM((128, n * 256), BF),
            pltpu.VMEM(cache.shape, BF),
        ),
        in_specs=[hbm] * 10,
        out_specs=(hbm, hbm),
        scratch_shapes=[
            pltpu.SMEM((2, 2), jnp.int32),
            pltpu.SMEM((2, 4), jnp.int32),
            pltpu.SMEM((2, 4), jnp.int32),
            pltpu.VMEM((64, 128), BF),
            pltpu.VMEM((1, width), F32),
            pltpu.VMEM((2, 256), F32),
            pltpu.VMEM((64, width), BF),
            pltpu.VMEM(modulation.shape[1:], F32),
            pltpu.VMEM((3, width, 256), BF),
            pltpu.VMEM((2 * ROWS, width), BF),
            pltpu.VMEM((2 * ROWS, width), BF),
            pltpu.VMEM((4, 64, 128), BF),
            pltpu.VMEM((n, 64, 128), BF),
            pltpu.VMEM((3, 128, 256), F32),
            pltpu.VMEM((PACKED, 128), BF),
            pltpu.VMEM((8, 128), F32),
            pltpu.VMEM((n, PACKED, 128), BF),
            pltpu.VMEM((ROWS + 144, 256), BF),
            pltpu.VMEM((256, tokens), BF),
            pltpu.VMEM((768, 256), BF),
            pltpu.VMEM((3, 256, 128), F32),
            pltpu.VMEM((2, 256, tokens), BF),
            pltpu.VMEM((2, tokens, 256), BF),
            pltpu.VMEM((2, 144, tokens), BF),
            pltpu.VMEM((tokens, QB), F32),
            pltpu.VMEM((tokens, QB), F32),
            pltpu.VMEM((2, tokens // QB, QB, 128), BF),
            pltpu.VMEM(cache.shape, BF),
            pltpu.VMEM((4,) + cache.shape, BF),
            dma((12,)),
            dma((4,)),
            dma((4,)),
            dma((2,)),
            dma((2,)),
            dma((2,)),
            dma((2,)),
            dma,
            dma,
            dma,
            dma,
            dma,
            dma,
        ],
        compiler_params=pltpu.CompilerParams(
            collective_id=0, has_side_effects=True, vmem_limit_bytes=58 * 1024 * 1024
        ),
    )(
        crossing,
        lengths,
        step_index,
        xt,
        patch_bias,
        qk_gain[0],
        patch_weight[0],
        modulation[0],
        w3,
        cache,
    )
    attended, cache_after = pl.pallas_call(
        place,
        out_shape=(
            jax.ShapeDtypeStruct(raw.shape, BF),
            jax.ShapeDtypeStruct(cache.shape, BF),
        ),
        in_specs=[hbm] * 2,
        out_specs=(hbm, hbm),
        scratch_shapes=[dma((2, 4))],
    )(
        pltpu.with_memory_space_constraint(raw, pltpu.VMEM),
        pltpu.with_memory_space_constraint(chosen, pltpu.VMEM),
    )
    return (attended[None, None], cache_after[None, None])


def solution(mesh):
    in_specs = (
        P("expert", "group", "seq", None),
        P("expert", "group", None, "seq", None),
        P("expert", None, None),
        P("expert", None),
        P("expert", None, None, "seq"),
        P("expert", None, "seq"),
        P("expert", None, None, None),
        P(),
        P(),
        P(),
    )
    out_specs = (P("expert", "group", "seq", None), P("expert", "group", None, "seq", None))
    return jax.shard_map(
        functools.partial(shards, mesh.shape["seq"]),
        mesh=mesh,
        in_specs=in_specs,
        out_specs=out_specs,
        check_vma=False,
    )
```

```python
import functools

import jax
import jax.numpy as jnp
from jax import lax
from jax.experimental import pallas as pl
from jax.experimental.pallas import tpu as pltpu
from jax.sharding import PartitionSpec as P

HD = 128
EPS = 1e-06
MASKED = -1e30
LOG2E = 1.4426950408889634
BF = jnp.bfloat16
F32 = jnp.float32
MESH = pl.DeviceIdType.MESH
ROWS = 80
PACKED = 48
SIDE = 4
QB = 512
KB = 512
OWNERS = QB // 128
STEPS = (
    ((2, 2), (1, 1), (3, 3), (2, 0))
    + ((0, 2), (1, 2), (3, 1), (2, 3))
    + ((1, 3), (3, 2), (2, 1), (0, 3))
    + ((1, 0), (3, 0), (0, 1), (0, 0))
)


def dot(a, b):
    return jnp.dot(a, b, preferred_element_type=F32)


def dot_nt(a, b):
    return lax.dot_general(a, b, (((1,), (1,)), ((), ())), preferred_element_type=F32)


def split(a):
    hi = a.astype(BF)
    lo = (a - hi.astype(F32)).astype(BF)
    return hi, lo


def gram(a):
    hi, lo = split(a)
    return dot_nt(hi, hi) + dot_nt(hi, lo) + dot_nt(lo, hi)


def kernel(
    n,
    crossing_hbm,
    lengths_hbm,
    steps_hbm,
    xt_hbm,
    b_hbm,
    gain_hbm,
    p_hbm,
    mod_hbm,
    w_hbm,
    cache_hbm,
    out_hbm,
    cache_out,
    crossing,
    lengths,
    steps,
    x_v,
    b_v,
    gain_v,
    p_v,
    mod_v,
    w_v,
    a2,
    c2,
    zin,
    xall,
    m_v,
    gbuf,
    rest,
    g_in,
    stat,
    z2,
    mt2,
    mtf,
    qaug,
    kaug,
    vaug,
    s_a,
    s_b,
    ostage,
    own_cache,
    land,
    load_sem,
    zsend,
    zrecv,
    csend,
    crecv,
    fsend,
    frecv,
    xsend,
    xrecv,
    gsend,
    grecv,
    osend,
    orecv,
):
    e = lax.axis_index("expert")
    g = lax.axis_index("group")
    s = lax.axis_index("seq")
    half = lax.div(g, 2)
    core = lax.rem(g, 2)
    my_x = lax.div(s, SIDE)
    my_y = lax.rem(s, SIDE)
    tokens = n * 128
    width = p_v.shape[1]

    def owner(step):
        return lax.rem(my_x + step[0], SIDE) * SIDE + lax.rem(my_y + step[1], SIDE)

    order = [owner(step) for step in STEPS]

    ld_p = pltpu.make_async_copy(p_hbm, p_v, load_sem.at[0])
    ld_b = pltpu.make_async_copy(b_hbm, b_v, load_sem.at[1])
    ld_x = pltpu.make_async_copy(xt_hbm, x_v, load_sem.at[2])
    ld_mod = pltpu.make_async_copy(mod_hbm, mod_v, load_sem.at[3])
    ld_gain = pltpu.make_async_copy(gain_hbm, gain_v, load_sem.at[4])
    ld_w = [pltpu.make_async_copy(w_hbm.at[j], w_v.at[j], load_sem.at[5 + j]) for j in range(3)]
    ld_scalars = [
        pltpu.make_async_copy(src, dst, load_sem.at[8 + i])
        for i, (src, dst) in enumerate(
            ((crossing_hbm, crossing), (lengths_hbm, lengths), (steps_hbm, steps))
        )
    ]
    ld_cache = pltpu.make_async_copy(cache_hbm, own_cache, load_sem.at[11])
    st_cache = pltpu.make_async_copy(own_cache, cache_out, load_sem.at[11])
    for copy in [ld_x] + ld_scalars + [ld_p, ld_b, ld_mod, ld_gain, ld_w[0], ld_w[1]]:
        copy.start()

    barrier = pltpu.get_barrier_semaphore()

    for other in range(4):
        pl.semaphore_signal(
            barrier, inc=1, device_id={"expert": 1 - e, "group": other}, device_id_type=MESH
        )
    for peer in order[: n - 1]:
        pl.semaphore_signal(barrier, inc=1, device_id={"seq": peer}, device_id_type=MESH)

    @pl.when(e == 1)
    def _():
        pl.semaphore_signal(barrier, inc=1, device_id={"group": 2 * half + 1 - core}, device_id_type=MESH)

    def z_copy(src_group, dst_group):
        return pltpu.make_async_remote_copy(
            src_ref=x_v,
            dst_ref=zin.at[src_group],
            send_sem=zsend.at[dst_group],
            recv_sem=zrecv.at[src_group],
            device_id={"expert": 1, "group": dst_group},
            device_id_type=MESH,
        )

    def cache_copy(src_half, dst_half):
        return pltpu.make_async_remote_copy(
            src_ref=cache_hbm,
            dst_ref=land.at[2 * src_half + core],
            send_sem=csend.at[dst_half],
            recv_sem=crecv.at[src_half],
            device_id={"expert": 1, "group": 2 * dst_half + core},
            device_id_type=MESH,
        )

    def forward_copy(src_half, src_core):
        return pltpu.make_async_remote_copy(
            src_ref=land.at[2 * src_half + src_core],
            dst_ref=land.at[2 * src_half + src_core],
            send_sem=fsend.at[src_half],
            recv_sem=frecv.at[src_half],
            device_id={"expert": 1, "group": 2 * half + 1 - core},
            device_id_type=MESH,
        )

    def x_copy(peer, slot):
        return pltpu.make_async_remote_copy(
            src_ref=xall.at[slot],
            dst_ref=xall.at[slot],
            send_sem=xsend,
            recv_sem=xrecv,
            device_id={"seq": peer},
            device_id_type=MESH,
        )

    def x_all():
        return pltpu.make_async_remote_copy(
            src_ref=xall.at[pl.ds(0, n - 1)],
            dst_ref=xall.at[pl.ds(0, n - 1)],
            send_sem=xsend,
            recv_sem=xrecv,
            device_id={"seq": lax.rem(s + 1, n)},
            device_id_type=MESH,
        )

    def x_start():
        for peer in order[: n - 1]:
            x_copy(peer, s).start()

    ld_x.wait()

    @pl.when(e == 0)
    def _():
        pl.semaphore_wait(barrier, n - 1 + 4)
        for dst in range(4):
            z_copy(g, dst).start()
        xall[s] = x_v[...]
        x_start()

    for copy in ld_scalars:
        copy.wait()
    hit0 = crossing[0, 1] == g
    hit1 = crossing[1, 1] == g
    arrived = jnp.logical_and(e == 1, jnp.logical_or(hit0, hit1))
    left = jnp.logical_and(e == 0, jnp.logical_or(crossing[0, 0] == g, crossing[1, 0] == g))
    source = jnp.where(hit0, crossing[0, 0], jnp.where(hit1, crossing[1, 0], 0))
    step_now = jnp.where(arrived, steps[0, source], steps[e, g])
    length = jnp.where(left, 0, jnp.where(arrived, lengths[0, source], lengths[e, g]))

    ld_p.wait()
    ld_b.wait()
    p_mean = jnp.mean(p_v[...].astype(F32), axis=1, keepdims=True)
    b_mean = jnp.mean(b_v[...], axis=1, keepdims=True)
    ld_mod.wait()
    part = 1024
    tail_row = lax.broadcasted_iota(jnp.int32, (16, part), 0)
    for i in range(width // part):
        cols = pl.ds(i * part, part)
        modulate = mod_v[step_now, :, cols]
        scale = 1.0 + modulate[1:2, :]
        shift = modulate[0:1, :]
        top = (p_v[:, cols].astype(F32) - p_mean) * scale
        bias = (b_v[:, cols] - b_mean) * scale
        bottom = jnp.where(
            tail_row == 0,
            jnp.broadcast_to(bias, (16, part)),
            jnp.where(tail_row == 1, jnp.broadcast_to(shift, (16, part)), 0.0),
        )
        hi, lo = split(top)
        a2[0:64, cols] = hi
        a2[ROWS : ROWS + 64, cols] = lo
        hi, lo = split(bottom)
        a2[64:ROWS, cols] = hi
        a2[ROWS + 64 : 2 * ROWS, cols] = lo

    def project(j):
        raw = dot(a2[...], w_v[j])
        total = raw[0:ROWS, :] + raw[ROWS : 2 * ROWS, :]
        m_v[j, 0:ROWS, :] = total
        return total

    ld_w[0].wait()
    ld_w[2].start()
    ld_cache.start()
    m_q = project(0)
    ld_w[1].wait()
    m_k = project(1)

    gram_q = gram(m_q)
    gram_k = gram(m_k)
    at_row = lax.broadcasted_iota(jnp.int32, (64, 64), 0)
    at_col = lax.broadcasted_iota(jnp.int32, (64, 64), 1)
    core_q = gram_q[0:64, 0:64]
    core_k = gram_k[0:64, 0:64]
    both = jnp.where(at_col < at_row, 2.0 * core_q, jnp.where(at_col > at_row, 2.0 * core_k, 0.0)).astype(BF)
    gbuf[0:32, 0:64] = both[0:32, :]
    gbuf[0:32, 64:128] = both[32:64, :]
    rest[...] = jnp.zeros_like(rest)
    for at, (values, centre) in enumerate(((gram_q, core_q), (gram_k, core_k))):
        cols = slice(at * 64, at * 64 + 64)
        rest[0:2, cols] = values[64:66, 0:64]
        rest[2:3, cols] = jnp.sum(jnp.where(at_col == at_row, centre, 0.0), axis=0, keepdims=True)
        rest[3 + 2 * at : 5 + 2 * at, 0:16] = values[64:66, 64:80]
    hi, lo = split(rest[...])
    gbuf[32:48, :] = jnp.concatenate([hi.astype(F32), lo.astype(F32)], axis=0).astype(BF)

    def g_copy(peer, slot):
        return pltpu.make_async_remote_copy(
            src_ref=gbuf,
            dst_ref=g_in.at[slot],
            send_sem=gsend,
            recv_sem=grecv,
            device_id={"seq": peer},
            device_id_type=MESH,
        )

    def g_all():
        return pltpu.make_async_remote_copy(
            src_ref=g_in.at[pl.ds(0, n - 1)],
            dst_ref=g_in.at[pl.ds(0, n - 1)],
            send_sem=gsend,
            recv_sem=grecv,
            device_id={"seq": lax.rem(s + 1, n)},
            device_id_type=MESH,
        )

    def g_start():
        for peer in order[: n - 1]:
            g_copy(peer, s).start()

    @pl.when(e == 1)
    def _():
        pl.semaphore_wait(barrier, n - 1 + 4 + 1)

    g_start()

    @pl.when(e == 0)
    def _():
        for dst in range(2):
            cache_copy(half, dst).start()


    @pl.when(e == 1)
    def _():
        for src in range(4):
            z_copy(src, 0).wait_recv()
        xall[s] = jnp.where(arrived, zin[source], x_v[...])
        x_start()

    g_in[s] = gbuf[...]

    for i in range(width // part):
        cols = pl.ds(i * part, part)
        hi, lo = split(p_v[:, cols].astype(F32) - p_mean)
        c2[0:64, cols] = hi
        c2[ROWS : ROWS + 64, cols] = lo
        bias = jnp.broadcast_to(b_v[:, cols] - b_mean, (16, part))
        hi, lo = split(jnp.where(tail_row == 0, bias, 0.0))
        c2[64:ROWS, cols] = hi
        c2[ROWS + 64 : 2 * ROWS, cols] = lo
    var_gram = (
        dot_nt(c2[0:ROWS, :], c2[0:ROWS, :])
        + dot_nt(c2[0:ROWS, :], c2[ROWS : 2 * ROWS, :])
        + dot_nt(c2[ROWS : 2 * ROWS, :], c2[0:ROWS, :])
    ) * (1.0 / width)

    ld_w[2].wait()
    project(2)

    ld_gain.wait()
    for j in range(3):
        m_v[j, ROWS:128, :] = jnp.zeros((128 - ROWS, 256), F32)
        full = m_v[j]
        if j < 2:
            full = full * gain_v[j : j + 1, :]
        flipped = full.T
        hi, lo = split(flipped)
        for h in range(2):
            at = 512 + h * 128 if j == 2 else h * 256 + j * 128
            rows = slice(h * 128, (h + 1) * 128)
            mt2[at : at + 128, 0:128] = hi[rows, :]
            mt2[at : at + 128, 128:256] = lo[rows, :]
        mtf[j] = flipped

    first16 = lax.broadcasted_iota(jnp.int32, (16, tokens), 0)
    first128 = lax.broadcasted_iota(jnp.int32, (128, tokens), 0)
    one16 = jnp.where(first16 == 0, 1.0, 0.0).astype(BF)
    one128 = jnp.where(first128 == 0, 1.0, 0.0).astype(BF)
    for h in range(2):
        qaug[h, 128:256, :] = one128
        vaug[h, 128:144, :] = one16
    key_at = lax.broadcasted_iota(jnp.int32, (128, 128), 0)
    for i in range(n):
        masks = jnp.where(key_at + order[i] * 128 >= length, MASKED, 0.0).astype(BF)
        for h in range(2):
            kaug[h, i * 128 : (i + 1) * 128, 128:256] = masks

    tail64 = lax.broadcasted_iota(jnp.int32, (64, tokens), 0)
    ones_row = jnp.where(tail64 == 0, 1.0, 0.0).astype(BF)
    z2[64:128, :] = ones_row
    z2[192:256, :] = ones_row
    hi, lo = split(var_gram)
    stat[...] = jnp.zeros_like(stat)
    stat[0:ROWS, 0:ROWS] = hi
    stat[0:ROWS, 128 : 128 + ROWS] = lo
    g_all().wait_recv()
    packed = g_in[0].astype(F32)
    for src in range(1, n):
        packed = packed + g_in[src].astype(F32)
    both = jnp.concatenate([packed[0:32, 0:64], packed[0:32, 64:128]], axis=0)
    packed = packed[32:40, :] + packed[40:48, :]
    diagonals = [
        jnp.where(at_col == at_row, jnp.broadcast_to(packed[2:3, j * 64 : j * 64 + 64], (64, 64)), 0.0)
        for j in range(2)
    ]
    lower = jnp.where(at_col < at_row, both, diagonals[0])
    upper = jnp.where(at_col > at_row, both, diagonals[1])
    tail16 = lax.broadcasted_iota(jnp.int32, (16, 64), 0)
    linear = jnp.zeros((16, 64), F32)
    for at, row in enumerate(
        (packed[0:1, 0:64], packed[1:2, 0:64], packed[0:1, 64:128], packed[1:2, 64:128])
    ):
        linear = jnp.where(tail16 == at, jnp.broadcast_to(row, (16, 64)), linear)
    hi, lo = split(jnp.concatenate([lower, upper, linear], axis=0))
    stat[ROWS : ROWS + 144, 0:64] = hi
    stat[ROWS : ROWS + 144, 128:192] = lo

    x_all().wait_recv()
    for i in range(n):
        cols = slice(i * 128, (i + 1) * 128)
        rows = xall[order[i]]
        z2[0:64, cols] = rows
        z2[128:192, cols] = rows
    t = dot(stat[...], z2[...])
    z80 = z2[0:ROWS, :].astype(F32)
    var = jnp.maximum(jnp.sum(t[0:ROWS, :] * z80, axis=0, keepdims=True), 0.0)
    rstd = lax.rsqrt(var + EPS)
    scales = []
    for j in range(2):
        base = ROWS + j * 64
        quad = jnp.sum(t[base : base + 64, :] * z80[0:64, :], axis=0, keepdims=True)
        base = ROWS + 128 + 2 * j
        by_bias = t[base : base + 1, :]
        by_shift = t[base + 1 : base + 2, :]
        at = 3 + 2 * j
        total = (
            rstd * rstd * (quad + 2.0 * by_bias + packed[at : at + 1, 0:1])
            + 2.0 * rstd * (by_shift + packed[at : at + 1, 1:2])
            + packed[at + 1 : at + 2, 1:2]
        )
        scales.append(lax.rsqrt(jnp.maximum(total, 0.0) * (1.0 / (n * 256)) + EPS))
    r_q = scales[0] * (LOG2E / HD**0.5)
    r_k = scales[1]

    q_u = r_q * rstd
    k_u = r_k * rstd
    piece = 512

    def heads(h):
        for i in range(tokens // piece):
            cols = slice(i * piece, (i + 1) * piece)
            raw = dot(mt2[h * 256 : (h + 1) * 256, :], z2[:, cols])
            rows = slice(h * 128, (h + 1) * 128)
            qaug[h, 0:128, cols] = (
                raw[0:128, :] * q_u[:, cols] + mtf[0, rows, 65:66] * r_q[:, cols]
            ).astype(BF)
            k_t = raw[128:256, :] * k_u[:, cols] + mtf[1, rows, 65:66] * r_k[:, cols]
            kaug[h, cols, 0:128] = k_t.T.astype(BF)

    heads(0)
    first_top = jnp.full((8, QB), -3e38, F32)
    for c in range(tokens // KB):
        rows = slice(c * KB, (c + 1) * KB)
        score = dot(kaug[0, rows, :], qaug[0, :, 0:QB])
        s_a[rows, :] = score
        first_top = jnp.maximum(first_top, jnp.max(score.reshape(KB // 8, 8, QB), axis=0))
    def values(h):
        for i in range(tokens // piece):
            cols = slice(i * piece, (i + 1) * piece)
            rows = slice(h * 128, (h + 1) * 128)
            raw = dot(mt2[512 + h * 128 : 640 + h * 128, :], z2[:, cols])
            vaug[h, 0:128, cols] = (raw * rstd[:, cols] + mtf[2, rows, 65:66]).astype(BF)

    blocks = tokens // QB

    def o_copy(block, side, h, peer, src):
        return pltpu.make_async_remote_copy(
            src_ref=ostage.at[h, block, pl.ds(side * 128, 128)],
            dst_ref=out_hbm.at[:, pl.ds(pl.multiple_of(src * 256 + h * 128, 128), 128)],
            send_sem=osend,
            recv_sem=orecv,
            device_id={"seq": peer},
            device_id_type=MESH,
        )

    def o_all():
        return pltpu.make_async_remote_copy(
            src_ref=out_hbm.at[:, pl.ds(0, (n - 1) * 256)],
            dst_ref=out_hbm.at[:, pl.ds(0, (n - 1) * 256)],
            send_sem=osend,
            recv_sem=orecv,
            device_id={"seq": lax.rem(s + 1, n)},
            device_id_type=MESH,
        )

    def own_copy(h):
        return pltpu.make_async_copy(
            ostage.at[h, blocks - 1, pl.ds((OWNERS - 1) * 128, 128)],
            out_hbm.at[:, pl.ds(pl.multiple_of(s * 256 + h * 128, 128), 128)],
            load_sem.at[h],
        )

    def send(block, h):
        for side in range(OWNERS - 1):
            o_copy(block, side, h, order[block * OWNERS + side], s).start()

        if block == blocks - 1:
            own_copy(h).start()
        else:
            o_copy(block, OWNERS - 1, h, order[block * OWNERS + OWNERS - 1], s).start()

    def unit(block, h, now, top, next_block, next_h, later):
        ahead = later is not None
        if ahead:
            query = qaug[next_h, :, next_block * QB : (next_block + 1) * QB]
        next_top = jnp.full((8, QB), -3e38, F32)
        total = jnp.zeros((144, QB), F32)
        for c in range(tokens // KB):
            rows = slice(c * KB, (c + 1) * KB)
            if ahead:
                score = dot(kaug[next_h, rows, :], query)
                later[rows, :] = score
                next_top = jnp.maximum(next_top, jnp.max(score.reshape(KB // 8, 8, QB), axis=0))
            weight = jnp.exp2(now[rows, :] - top).astype(BF)
            total = total + dot(vaug[h, :, rows], weight)
        row = lax.broadcasted_iota(jnp.int32, (1, 128), 1)
        live = [row + order[block * OWNERS + side] * 128 < length for side in range(OWNERS)]
        inverse = 1.0 / total[128:129, :]
        inverse = jnp.concatenate(
            [jnp.where(live[a], inverse[:, a * 128 : (a + 1) * 128], 0.0) for a in range(OWNERS)], axis=1
        )
        ostage[h, block] = (total[0:128, :] * inverse).T.astype(BF)
        return jnp.max(next_top, axis=0, keepdims=True)

    def forward():
        @pl.when(e == 1)
        def _():
            for src in range(2):
                cache_copy(src, 0).wait_recv()
                forward_copy(src, core).start()

    units = [(block, h) for h in range(2) for block in range(blocks)]
    halves = (s_a, s_b)
    values(0)
    top = jnp.max(first_top, axis=0, keepdims=True)
    for at, (block, h) in enumerate(units):
        if at == 2:
            heads(1)
        if at == blocks:
            values(1)
        if at == len(units) - 2:
            forward()
        if at + 1 < len(units):
            top = unit(block, h, halves[at % 2], top, *units[at + 1], halves[(at + 1) % 2])
        else:
            unit(block, h, halves[at % 2], top, None, None, None)
        send(block, h)

    ld_cache.wait()
    height = own_cache.shape[0] // 8

    @pl.when(e == 1)
    def _():
        for src in range(2):
            forward_copy(src, core).wait_send()
            forward_copy(src, 1 - core).wait_recv()

        def choose(i, carry):
            rows = pl.ds(i * height, height)
            own_cache[rows] = jnp.where(arrived, land[source, rows], own_cache[rows])
            return carry

        lax.fori_loop(0, 8, choose, 0)

    @pl.when(e == 0)
    def _():
        for dst in range(4):
            z_copy(g, dst).wait_send()
        for dst in range(2):
            cache_copy(half, dst).wait_send()

        def choose(i, carry):
            rows = pl.ds(i * height, height)
            kept = own_cache[rows]
            own_cache[rows] = jnp.where(left, jnp.zeros_like(kept), kept)
            return carry

        lax.fori_loop(0, 8, choose, 0)

    st_cache.start()
    x_all().wait_send()
    g_all().wait_send()
    o_all().wait_send()
    for h in range(2):
        own_copy(h).wait()
    st_cache.wait()
    o_all().wait_recv()


def place(raw, cache, out, cache_out, sem):
    parts = 4
    writes = []
    for at, (src, dst) in enumerate(((raw, out), (cache, cache_out))):
        height = src.shape[0] // parts
        for i in range(parts):
            rows = pl.ds(i * height, height)
            writes.append(pltpu.make_async_copy(src.at[rows], dst.at[rows], sem.at[at, i]))
    for copy in writes:
        copy.start()
    for copy in writes:
        copy.wait()


def shards(
    n,
    latent,
    text_cache,
    patch_weight,
    patch_bias,
    qkv_weight,
    qk_gain,
    modulation,
    step_index,
    lengths,
    crossing,
):
    tokens = n * 128
    width = qkv_weight.shape[1]
    xt = latent[0, 0].T
    w3 = jnp.transpose(qkv_weight[0], (1, 0, 2))
    cache = text_cache[0, 0]
    hbm = pl.BlockSpec(memory_space=pl.ANY)
    dma = pltpu.SemaphoreType.DMA
    raw, chosen = pl.pallas_call(
        functools.partial(kernel, n),
        out_shape=(
            pltpu.VMEM((128, n * 256), BF),
            pltpu.VMEM(cache.shape, BF),
        ),
        in_specs=[hbm] * 10,
        out_specs=(hbm, hbm),
        scratch_shapes=[
            pltpu.SMEM((2, 2), jnp.int32),
            pltpu.SMEM((2, 4), jnp.int32),
            pltpu.SMEM((2, 4), jnp.int32),
            pltpu.VMEM((64, 128), BF),
            pltpu.VMEM((1, width), F32),
            pltpu.VMEM((2, 256), F32),
            pltpu.VMEM((64, width), BF),
            pltpu.VMEM(modulation.shape[1:], F32),
            pltpu.VMEM((3, width, 256), BF),
            pltpu.VMEM((2 * ROWS, width), BF),
            pltpu.VMEM((2 * ROWS, width), BF),
            pltpu.VMEM((4, 64, 128), BF),
            pltpu.VMEM((n, 64, 128), BF),
            pltpu.VMEM((3, 128, 256), F32),
            pltpu.VMEM((PACKED, 128), BF),
            pltpu.VMEM((8, 128), F32),
            pltpu.VMEM((n, PACKED, 128), BF),
            pltpu.VMEM((ROWS + 144, 256), BF),
            pltpu.VMEM((256, tokens), BF),
            pltpu.VMEM((768, 256), BF),
            pltpu.VMEM((3, 256, 128), F32),
            pltpu.VMEM((2, 256, tokens), BF),
            pltpu.VMEM((2, tokens, 256), BF),
            pltpu.VMEM((2, 144, tokens), BF),
            pltpu.VMEM((tokens, QB), F32),
            pltpu.VMEM((tokens, QB), F32),
            pltpu.VMEM((2, tokens // QB, QB, 128), BF),
            pltpu.VMEM(cache.shape, BF),
            pltpu.VMEM((4,) + cache.shape, BF),
            dma((12,)),
            dma((4,)),
            dma((4,)),
            dma((2,)),
            dma((2,)),
            dma((2,)),
            dma((2,)),
            dma,
            dma,
            dma,
            dma,
            dma,
            dma,
        ],
        compiler_params=pltpu.CompilerParams(
            collective_id=0, has_side_effects=True, vmem_limit_bytes=58 * 1024 * 1024
        ),
    )(
        crossing,
        lengths,
        step_index,
        xt,
        patch_bias,
        qk_gain[0],
        patch_weight[0],
        modulation[0],
        w3,
        cache,
    )
    attended, cache_after = pl.pallas_call(
        place,
        out_shape=(
            jax.ShapeDtypeStruct(raw.shape, BF),
            jax.ShapeDtypeStruct(cache.shape, BF),
        ),
        in_specs=[hbm] * 2,
        out_specs=(hbm, hbm),
        scratch_shapes=[dma((2, 4))],
    )(
        pltpu.with_memory_space_constraint(raw, pltpu.VMEM),
        pltpu.with_memory_space_constraint(chosen, pltpu.VMEM),
    )
    return (attended[None, None], cache_after[None, None])


def solution(mesh):
    in_specs = (
        P("expert", "group", "seq", None),
        P("expert", "group", None, "seq", None),
        P("expert", None, None),
        P("expert", None),
        P("expert", None, None, "seq"),
        P("expert", None, "seq"),
        P("expert", None, None, None),
        P(),
        P(),
        P(),
    )
    out_specs = (P("expert", "group", "seq", None), P("expert", "group", None, "seq", None))
    return jax.shard_map(
        functools.partial(shards, mesh.shape["seq"]),
        mesh=mesh,
        in_specs=in_specs,
        out_specs=out_specs,
        check_vma=False,
    )
```
